32 devices in a mesh: row: 4 (over y, x), col: 8 (over z, core).
Axes of the slice: x: 2, y: 2, z: 4, core: 2. Of those that a mesh axis runs over, the one named last changes fastest.
Arguments:
- trunk: bfloat16 [1024, 256], P(('row', 'col')), may hold values from -6 to 6
- row_weight: bfloat16 [256, 512], replicated, may hold values from -0.375 to 0.375
- column_weight: bfloat16 [256, 512], replicated, may hold values from -0.375 to 0.375
- pair_map_weight: bfloat16 [512, 48], replicated, may hold values from -0.25 to 0.25
- dilated_weight: bfloat16 [3, 3, 48, 48], replicated, may hold values from -0.3125 to 0.3125
- mixing_weight: bfloat16 [48, 48], replicated, may hold values from -0.875 to 0.875
Outputs:
- block_out: bfloat16 [48, 1024, 1024], P(None, 'row', 'col')
The draws below stay inside these ranges and needn't reach their ends.
All inputs are finite; a program needn't handle non-finite values.
Results may differ from the reference program's by a relative error of at most 0.0067.
Values may be sent and summed in bfloat16 or wider, within the bound.
No kernel may reach another device: no remote copies, remote signals or barrier semaphores. Data moves between devices by JAX's collectives and lax.ppermute only.
A program may use at most 128 MiB of HBM per device.

```python
import jax
import jax.numpy as jnp
from jax import lax

TRUNK = 256
PAIR = 512
MAP_CHANNELS = 48
DILATION_STEP = 8
REGION_BINS = 1024


def level_of(key, extent, pieces, low, top_value):
    def one(axis_at, shards_of):
        draws = jax.random.uniform(jax.random.fold_in(jax.random.fold_in(key, 6), axis_at), (shards_of,), jnp.float32, low / len(pieces), top_value / len(pieces))
        return jnp.repeat(jnp.exp(draws), extent[axis_at] // shards_of).reshape((-1,) + (1,) * (len(extent) - axis_at - 1))

    gain = one(*pieces[0])
    for cut in pieces[1:]:
        gain = gain * one(*cut)
    return gain


def bell_draw(key, dims, scale, limit, cuts=(), kind=jnp.bfloat16):
    drawn = scale * jax.random.normal(key, dims, jnp.float32)
    if cuts:
        drawn = drawn * level_of(key, dims, cuts, -0.22, 0.18)
    return jnp.clip(drawn, -limit, limit).astype(kind)


def setup_inputs(seed: int = 0) -> dict:
    key_of = jax.random.split(jax.random.key(seed), 7)
    return {
        "trunk": bell_draw(key_of[0], (REGION_BINS, TRUNK), 1.0, 6.0, ((0, 32),)),
        "row_weight": bell_draw(key_of[1], (TRUNK, PAIR), TRUNK ** -0.5, 0.375),
        "column_weight": bell_draw(key_of[2], (TRUNK, PAIR), TRUNK ** -0.5, 0.375),
        "pair_map_weight": bell_draw(key_of[3], (PAIR, MAP_CHANNELS), PAIR ** -0.5, 0.25),
        "dilated_weight": bell_draw(key_of[4], (3, 3, MAP_CHANNELS, MAP_CHANNELS), (9 * MAP_CHANNELS) ** -0.5, 0.3125),
        "mixing_weight": bell_draw(key_of[5], (MAP_CHANNELS, MAP_CHANNELS), MAP_CHANNELS ** -0.5, 0.875),
    }


def reference(trunk, row_weight, column_weight, pair_map_weight, dilated_weight, mixing_weight):
    row_proj = jnp.dot(trunk, row_weight, preferred_element_type=jnp.float32).astype(jnp.bfloat16)
    col_proj = jnp.dot(trunk, column_weight, preferred_element_type=jnp.float32).astype(jnp.bfloat16)
    col_wide = col_proj.astype(jnp.float32)
    pair_weight = pair_map_weight.astype(jnp.float32)
    blocksz = min(16, REGION_BINS)
    count = REGION_BINS // blocksz

    def pair_rows(rows):
        summed = rows.astype(jnp.float32)[:, None, :] + col_wide[None, :, :]
        pair_act = jnp.maximum(summed, 0.0).astype(jnp.bfloat16)
        hidden = jnp.einsum('ijk,ko->oij', pair_act.astype(jnp.float32), pair_weight)
        return hidden.astype(jnp.bfloat16)

    stacked = lax.map(pair_rows, row_proj.reshape(count, blocksz, PAIR))
    base = jnp.transpose(stacked, (1, 0, 2, 3)).reshape(MAP_CHANNELS, REGION_BINS, REGION_BINS)
    pair_activation = jnp.maximum(base, jnp.zeros((), jnp.bfloat16))
    padded_pairs = jnp.pad(pair_activation, ((0, 0), (DILATION_STEP, DILATION_STEP), (DILATION_STEP, DILATION_STEP)))
    dilated_kernel_weight = dilated_weight.astype(jnp.float32)
    mix_weight = mixing_weight.astype(jnp.float32)
    row_block_slice = min(256, REGION_BINS)
    nblocks = REGION_BINS // row_block_slice

    def conv_rows(start_index):
        start_index = start_index.astype(jnp.int32)
        total_sum = jnp.zeros((MAP_CHANNELS, row_block_slice, REGION_BINS), jnp.float32)
        for first_tap_offset in range(3):
            for second_tap_offset in range(3):
                neighbour_window = lax.dynamic_slice(padded_pairs, (jnp.int32(0), start_index + first_tap_offset * DILATION_STEP, jnp.int32(second_tap_offset * DILATION_STEP)), (MAP_CHANNELS, row_block_slice, REGION_BINS))
                total_sum = total_sum + jnp.einsum('zy,yea->zea', dilated_kernel_weight[first_tap_offset, second_tap_offset], neighbour_window.astype(jnp.float32))
        mid = jnp.maximum(total_sum, 0.0).astype(jnp.bfloat16)
        here = lax.dynamic_slice(base, (jnp.int32(0), start_index, jnp.int32(0)), (MAP_CHANNELS, row_block_slice, REGION_BINS))
        result = here.astype(jnp.float32) + jnp.einsum('zy,yea->zea', mix_weight, mid.astype(jnp.float32))
        return result.astype(jnp.bfloat16)

    starts = (jnp.arange(nblocks) * row_block_slice).astype(jnp.int32)
    outblk = lax.map(conv_rows, starts)
    return jnp.transpose(outblk, (1, 0, 2, 3)).reshape(MAP_CHANNELS, REGION_BINS, REGION_BINS)
```

```python
import jax
import jax.numpy as jnp
from jax import lax
from jax.sharding import PartitionSpec as P

DILATION_STEP = 8
OUTSIDE = -1e30


def project(source, weight):
    return jnp.dot(source, weight, preferred_element_type=jnp.float32).astype(jnp.bfloat16)


def window(padded, start, size, bins):
    length = size + 2 * DILATION_STEP
    cells = lax.dynamic_slice_in_dim(padded, start, length, 0)
    index = start - DILATION_STEP + jnp.arange(length)
    return cells, ((index >= 0) & (index < bins))[:, None]


def on_device(trunk, row_weight, column_weight, pair_map_weight, dilated_weight, mixing_weight):
    n_row = lax.axis_size("row")
    n_col = lax.axis_size("col")
    bins = trunk.shape[0] * n_row * n_col
    rows = bins // n_row
    cols = bins // n_col
    step = DILATION_STEP
    full = lax.all_gather(trunk, ("row", "col"), axis=0, tiled=True)
    padded = jnp.pad(full, ((step, step), (0, 0)))
    row_src, row_in = window(padded, lax.axis_index("row") * rows, rows, bins)
    col_src, col_in = window(padded, lax.axis_index("col") * cols, cols, bins)
    outside = jnp.asarray(OUTSIDE, jnp.bfloat16)
    row_proj = jnp.where(row_in, project(row_src, row_weight), outside)
    col_proj = jnp.where(col_in, project(col_src, column_weight), outside)
    width = row_weight.shape[1]
    block = 2 * step
    count = (rows + 2 * step) // block

    def pair_rows(part):
        pair_act = jnp.maximum(part[:, None, :] + col_proj[None, :, :], jnp.zeros((), jnp.bfloat16))
        hidden = jnp.einsum(
            "ijk,ko->ijo", pair_act, pair_map_weight, preferred_element_type=jnp.float32
        )
        return hidden.astype(jnp.bfloat16)

    stacked = lax.map(pair_rows, row_proj.reshape(count, block, width))
    channels = pair_map_weight.shape[1]
    base = stacked.reshape(rows + 2 * step, cols + 2 * step, channels)
    act = jnp.maximum(base, jnp.zeros((), jnp.bfloat16))
    total = lax.conv_general_dilated(
        act[None],
        dilated_weight,
        (1, 1),
        "VALID",
        rhs_dilation=(step, step),
        dimension_numbers=("NHWC", "HWOI", "NHWC"),
        preferred_element_type=jnp.float32,
    )[0]
    mid = jnp.maximum(total, 0.0).astype(jnp.bfloat16)
    mixed = jnp.einsum("zy,eay->zea", mixing_weight, mid, preferred_element_type=jnp.float32)
    here = jnp.transpose(base[step : step + rows, step : step + cols], (2, 0, 1))
    return (here.astype(jnp.float32) + mixed).astype(jnp.bfloat16)


def solution(mesh):
    return jax.shard_map(
        on_device,
        mesh=mesh,
        in_specs=(P(("row", "col"), None), P(), P(), P(), P(), P()),
        out_specs=P(None, "row", "col"),
        check_vma=False,
    )
```

```python
import functools

import jax
import jax.numpy as jnp
from jax import lax
from jax.experimental import pallas as pl
from jax.experimental.pallas import tpu as pltpu
from jax.sharding import PartitionSpec as P

STEP = 8
EDGES = 2 * STEP
TAPS = 3
OUTSIDE = -1e30
LANES = 128


def flip(count, bit):
    return [(i, i ^ bit) for i in range(count)]


def doubled(block, axis, bits):
    count = lax.axis_size(axis)
    for at, bit in enumerate(bits):
        other = lax.ppermute(block, axis, flip(count, bit))
        if at == len(bits) - 1:
            return block, other
        block = jnp.concatenate(
            [block[:-EDGES], other[:-EDGES], block[-EDGES:] + other[-EDGES:]], axis=0
        )


def exchange(trunk):
    n_row, n_col = lax.axis_size("row"), lax.axis_size("col")
    total = n_row * n_col
    both = ("row", "col")
    row, col = lax.axis_index("row"), lax.axis_index("col")
    none = jnp.zeros_like(trunk[:STEP])
    after = jnp.concatenate([none, trunk[:STEP]], axis=0)
    before = jnp.concatenate([trunk[-STEP:], none], axis=0)

    def row_edges(at):
        down = [((r - 1) * n_col + n_col - 1, r * n_col + at) for r in range(1, n_row)]
        up = [((r + 1) * n_col, r * n_col + n_col - 1 - at) for r in range(n_row - 1)]
        return down + up

    sent = jnp.where(col == 0, after, before)
    edges = [lax.ppermute(sent, both, row_edges(at)) for at in range(2)]
    pair = lax.ppermute(trunk, "col", flip(n_col, 1))
    row_block = jnp.concatenate([trunk, pair, edges[0] + edges[1]], axis=0)

    sent = jnp.where((row * n_col + col) % n_row == 0, after, before)
    down = [(c * n_row - 1, c) for c in range(1, n_col)]
    up = [((c + 1) * n_row, (n_row - 1) * n_col + c) for c in range(n_col - 1)]
    own = lax.ppermute(
        trunk, both, [(c * n_row + r, r * n_col + c) for r in range(n_row) for c in range(n_col)]
    )
    col_block = jnp.concatenate([own, lax.ppermute(sent, both, down + up)], axis=0)

    def bits(first, count):
        return [1 << b for b in range(first, count.bit_length() - 1)]

    return doubled(row_block, "col", bits(1, n_col)) + doubled(col_block, "row", bits(0, n_row))


def kernel(
    shard,
    n_row,
    n_col,
    row_a,
    row_b,
    col_a,
    col_b,
    row_weight,
    col_weight,
    pair_weight,
    conv_weight,
    mix_weight,
    out,
    row_proj,
    col_proj,
    base,
):
    f32, bf16 = jnp.float32, jnp.bfloat16
    row, col = lax.axis_index("row"), lax.axis_index("col")
    n_rows = shard * n_col
    n_cols = shard * n_row
    width = n_cols + EDGES
    channels = out.shape[1]
    place = lax.broadcasted_iota(jnp.int32, (EDGES, 1), 0)

    def projected(block, weight):
        return jnp.dot(block, weight[...], preferred_element_type=f32).astype(bf16)

    def edges(a, b, weight, first, last):
        cells = projected(a[-EDGES:, :] + b[-EDGES:, :], weight).astype(f32)
        off = ((place < STEP) & first) | ((place >= STEP) & last)
        return jnp.where(off, OUTSIDE, cells)

    half = n_col // 2
    for part, source in enumerate((row_a, row_b)):
        cells = projected(source[: half * shard, :], row_weight).astype(f32)
        for k in range(half):
            at = STEP + (col ^ (part * half + k)) * shard
            row_proj[pl.ds(pl.multiple_of(at, STEP), shard), :] = cells[k * shard : (k + 1) * shard]
    cells = edges(row_a, row_b, row_weight, row == 0, row == n_row - 1)
    row_proj[:STEP, :] = cells[:STEP]
    row_proj[n_rows + STEP :, :] = cells[STEP:]

    half = n_row // 2
    for part, source in enumerate((col_a, col_b)):
        cells = projected(source[: half * shard, :], col_weight)
        for k in range(half):
            at = (row ^ (part * half + k)) * shard
            col_proj[pl.ds(pl.multiple_of(at, EDGES), shard), :] = cells[k * shard : (k + 1) * shard]
    cells = edges(col_a, col_b, col_weight, col == 0, col == n_col - 1)
    col_proj[n_cols:, :] = cells.astype(bf16)

    base[n_rows + EDGES :] = jnp.zeros_like(base[n_rows + EDGES :])

    def pair_rows(at, _):
        rows = row_proj[pl.ds(pl.multiple_of(at * STEP, STEP), STEP), :]
        columns = col_proj[...].reshape(width // EDGES, EDGES, -1)
        acts = []
        for k in range(STEP):
            spread = jnp.broadcast_to(rows[k : k + 1], (EDGES, rows.shape[1])).astype(bf16)
            acts.append(jnp.maximum(columns + spread[None], jnp.zeros((), bf16)))
        act = jnp.concatenate(acts, axis=0).reshape(STEP * width, rows.shape[1])
        hidden = jnp.dot(act, pair_weight[...], preferred_element_type=f32).astype(bf16)
        base[pl.ds(at * STEP, STEP)] = hidden.reshape(STEP, width, -1)
        return _

    lax.fori_loop(0, (n_rows + EDGES) // STEP, pair_rows, 0)

    group = TAPS * STEP
    lane = lax.broadcasted_iota(jnp.int32, (1, base.shape[2]), 1)

    def conv_rows(at, _):
        first = at * group
        for p in range(STEP):
            windows = [base[first + p + STEP * m] for m in range(TAPS + 2)]
            cells = windows[0]
            for m in range(1, TAPS + 2):
                cells = jnp.where(lane >= m * channels, windows[m], cells)
            act = jnp.maximum(cells, jnp.zeros((), bf16))
            left, here, right = (
                jnp.dot(act, conv_weight[b], preferred_element_type=f32) for b in range(TAPS)
            )
            total = (
                here[:n_cols]
                + jnp.concatenate([left[n_cols : n_cols + STEP], left[: n_cols - STEP]], axis=0)
                + jnp.concatenate([right[STEP:n_cols], right[n_cols + STEP :]], axis=0)
            )
            mid = jnp.maximum(total, 0.0).astype(bf16)
            mixed = jnp.dot(mid, mix_weight[...], preferred_element_type=f32)
            result = jnp.transpose(mixed + cells[:n_cols].astype(f32))
            for m in range(TAPS):
                row_at = first + p + STEP * m

                @pl.when(row_at < n_rows)
                def _store():
                    out[row_at] = result[(m + 1) * channels : (m + 2) * channels].astype(bf16)

        return _

    lax.fori_loop(0, -(-n_rows // group), conv_rows, 0)


def on_device(trunk, row_weight, column_weight, pair_map_weight, dilated_weight, mixing_weight):
    n_row = lax.axis_size("row")
    n_col = lax.axis_size("col")
    shard = trunk.shape[0]
    n_rows, n_cols = shard * n_col, shard * n_row
    channels = pair_map_weight.shape[1]
    span = -(-(TAPS + 2) * channels // LANES) * LANES
    windows = TAPS + 2
    pair = jnp.pad(jnp.tile(pair_map_weight, (1, windows)), ((0, 0), (0, span - windows * channels)))
    taps = jnp.transpose(dilated_weight, (1, 0, 3, 2))
    conv = jnp.concatenate(
        [
            jnp.pad(
                taps.reshape(TAPS, TAPS * channels, channels),
                ((0, 0), (m * channels, span - (m + TAPS) * channels), (0, 0)),
            )
            for m in range(TAPS)
        ],
        axis=2,
    )
    conv = jnp.pad(conv, ((0, 0), (0, 0), (0, span - TAPS * channels)))
    mix = jnp.kron(jnp.eye(TAPS, dtype=mixing_weight.dtype), mixing_weight.T)
    mix = jnp.pad(mix, ((0, span - TAPS * channels), (channels, span - (TAPS + 1) * channels)))

    pieces = exchange(trunk)
    group = TAPS * STEP
    base_rows = -(-n_rows // group) * group + EDGES
    out = pl.pallas_call(
        functools.partial(kernel, shard, n_row, n_col),
        out_shape=jax.ShapeDtypeStruct((n_rows, channels, n_cols), jnp.bfloat16),
        scratch_shapes=[
            pltpu.VMEM((n_rows + EDGES, row_weight.shape[1]), jnp.float32),
            pltpu.VMEM((n_cols + EDGES, row_weight.shape[1]), jnp.bfloat16),
            pltpu.VMEM((base_rows, n_cols + EDGES, span), jnp.bfloat16),
        ],
        compiler_params=pltpu.CompilerParams(vmem_limit_bytes=56 * 2**20),
        name="pair_block",
    )(*pieces, row_weight, column_weight, pair, conv, mix)
    return jnp.transpose(out, (1, 0, 2))


def solution(mesh):
    return jax.shard_map(
        on_device,
        mesh=mesh,
        in_specs=(P(("row", "col"), None), P(), P(), P(), P(), P()),
        out_specs=P(None, "row", "col"),
        check_vma=False,
    )
```

```python
import functools

import jax
import jax.numpy as jnp
from jax import lax
from jax.experimental import pallas as pl
from jax.experimental.pallas import tpu as pltpu
from jax.sharding import PartitionSpec as P

STEP = 8
PAIR_TILE = 2 * STEP
TAPS = 3
WINDOWS = TAPS + 2
GROUP = TAPS * STEP
OUTSIDE = -1e30
LANES = 128


def kernel(
    n_row,
    n_col,
    trunk,
    row_weight,
    col_weight,
    pair_weight,
    conv_weight,
    mix_weight,
    out,
    row_proj,
    col_proj,
    base,
    result,
):
    f32, bf16 = jnp.float32, jnp.bfloat16
    row, col = lax.axis_index("row"), lax.axis_index("col")
    channels, n_rows, n_cols = out.shape
    tiles = n_cols // STEP + 2
    bins = trunk.shape[0]
    zero = jnp.zeros((), bf16)

    def projected(start, size, weight):
        cells = trunk[pl.ds(pl.multiple_of(start, PAIR_TILE), size), :]
        return jnp.dot(cells, weight[...], preferred_element_type=f32).astype(bf16).astype(f32)

    def extended(index, count, size, weight):
        start = index * size
        left = projected(jnp.maximum(start - PAIR_TILE, 0), PAIR_TILE, weight)[STEP:]
        right = projected(jnp.minimum(start + size, bins - PAIR_TILE), PAIR_TILE, weight)[:STEP]
        return (
            jnp.where(index == 0, OUTSIDE, left),
            projected(start, size, weight),
            jnp.where(index == count - 1, OUTSIDE, right),
        )

    left, here, right = extended(row, n_row, n_rows, row_weight)
    row_proj[:STEP, :] = left
    row_proj[STEP : STEP + n_rows, :] = here
    row_proj[STEP + n_rows :, :] = right
    columns = jnp.concatenate(extended(col, n_col, n_cols, col_weight), axis=0)
    width = columns.shape[1]
    columns = columns.reshape(tiles, 1, STEP, width)
    columns = jnp.concatenate([columns, columns], axis=1).reshape(tiles * PAIR_TILE, width)
    col_proj[...] = columns.astype(bf16)

    spare = (n_rows + PAIR_TILE) // 2
    base[spare:] = jnp.zeros_like(base[spare:])

    def pair_rows(at, _):
        rows = row_proj[pl.ds(pl.multiple_of(at * STEP, STEP), STEP), :]
        acts = []
        for k in range(0, STEP, 2):
            spread = [jnp.broadcast_to(rows[k + e : k + e + 1], (STEP, width)) for e in range(2)]
            spread = jnp.concatenate(spread, axis=0).astype(bf16)
            cells = col_proj[...].reshape(tiles, PAIR_TILE, width) + spread[None]
            acts.append(jnp.maximum(cells, zero).reshape(tiles * PAIR_TILE, width))
        act = jnp.concatenate(acts, axis=0)
        hidden = jnp.dot(act, pair_weight[...], preferred_element_type=f32).astype(bf16)
        base[pl.ds(at * (STEP // 2), STEP // 2)] = hidden.reshape(STEP // 2, tiles * PAIR_TILE, -1)
        return _

    lax.fori_loop(0, (n_rows + PAIR_TILE) // STEP, pair_rows, 0)

    span = base.shape[2]
    lane = lax.broadcasted_iota(jnp.int32, (1, LANES), 1)
    pairs = STEP // 2
    cells_in = 2 * n_cols

    def conv_rows(at, _):
        first = at * (GROUP // 2)
        cells, windows = [], []
        for p in range(pairs):
            parts = []
            for low in range(0, span, LANES):
                part = None
                for m in range(WINDOWS):
                    begin, end = m * channels - low, (m + 1) * channels - low
                    if end <= 0 or begin >= LANES:
                        continue
                    window = base[first + p + pairs * m, :, low : low + LANES]
                    part = window if part is None else jnp.where(lane >= begin, window, part)
                parts.append(part)
            cells.append(jnp.concatenate(parts, axis=1))
            act = jnp.maximum(cells[-1], zero)
            windows.append(
                jnp.concatenate(
                    [act[b * PAIR_TILE : b * PAIR_TILE + cells_in] for b in range(TAPS)], axis=1
                )
            )
        total = jnp.dot(
            jnp.concatenate(windows, axis=0), conv_weight[...], preferred_element_type=f32
        )
        mid = jnp.maximum(total, 0.0).astype(bf16)
        mixed = jnp.dot(mid, mix_weight[...], preferred_element_type=f32)
        for p in range(pairs):
            full = mixed[p * cells_in : (p + 1) * cells_in] + cells[p][
                PAIR_TILE : PAIR_TILE + cells_in
            ].astype(f32)
            full = full.reshape(n_cols // STEP, 2, STEP, span)
            for e in range(2):
                turned = jnp.transpose(full[:, e].reshape(n_cols, span))
                for m in range(TAPS):
                    row_at = at * GROUP + 2 * p + e + STEP * m
                    result[pl.ds(pl.multiple_of(row_at * channels, STEP), channels), :] = turned[
                        (m + 1) * channels : (m + 2) * channels
                    ]
        return _

    lax.fori_loop(0, -(-n_rows // GROUP), conv_rows, 0)

    def turn(o, _):
        out[o] = result[pl.ds(o, n_rows, stride=channels), :].astype(bf16)
        return _

    lax.fori_loop(0, channels, turn, 0)


def on_device(trunk, row_weight, column_weight, pair_map_weight, dilated_weight, mixing_weight):
    n_row = lax.axis_size("row")
    n_col = lax.axis_size("col")
    shard, depth = trunk.shape
    n_rows, n_cols = shard * n_col, shard * n_row
    channels = pair_map_weight.shape[1]
    width = row_weight.shape[1]
    span = -(-WINDOWS * channels // LANES) * LANES
    pair = jnp.pad(jnp.tile(pair_map_weight, (1, WINDOWS)), ((0, 0), (0, span - WINDOWS * channels)))
    taps = jnp.transpose(dilated_weight, (1, 0, 3, 2))
    conv = jnp.concatenate(
        [
            jnp.pad(
                taps.reshape(TAPS, TAPS * channels, channels),
                ((0, 0), (m * channels, span - (m + TAPS) * channels), (0, 0)),
            )
            for m in range(TAPS)
        ],
        axis=2,
    )
    conv = jnp.pad(conv, ((0, 0), (0, 0), (0, span - TAPS * channels))).reshape(TAPS * span, span)
    mix = jnp.kron(jnp.eye(TAPS, dtype=mixing_weight.dtype), mixing_weight.T)
    mix = jnp.pad(mix, ((0, span - TAPS * channels), (channels, span - (TAPS + 1) * channels)))

    copies = jnp.broadcast_to(trunk[None], (n_row * n_col, shard, depth))
    full = lax.all_to_all(copies, ("row", "col"), 0, 0).reshape(n_row * n_col * shard, depth)
    groups = -(-n_rows // GROUP)
    return pl.pallas_call(
        functools.partial(kernel, n_row, n_col),
        out_shape=jax.ShapeDtypeStruct((channels, n_rows, n_cols), jnp.bfloat16),
        scratch_shapes=[
            pltpu.VMEM((n_rows + PAIR_TILE, width), jnp.float32),
            pltpu.VMEM((2 * (n_cols + PAIR_TILE), width), jnp.bfloat16),
            pltpu.VMEM((groups * GROUP // 2 + STEP, 2 * (n_cols + PAIR_TILE), span), jnp.bfloat16),
            pltpu.VMEM((groups * GROUP * channels, n_cols), jnp.float32),
        ],
        compiler_params=pltpu.CompilerParams(vmem_limit_bytes=56 * 2**20),
        name="pair_block",
    )(full, row_weight, column_weight, pair, conv, mix)


def solution(mesh):
    return jax.shard_map(
        on_device,
        mesh=mesh,
        in_specs=(P(("row", "col"), None), P(), P(), P(), P(), P()),
        out_specs=P(None, "row", "col"),
        check_vma=False,
    )
```

```python
import functools

import jax
import jax.numpy as jnp
from jax import lax
from jax.experimental import pallas as pl
from jax.experimental.pallas import tpu as pltpu
from jax.sharding import PartitionSpec as P

STEP = 8
PAIR_TILE = 2 * STEP
TAPS = 3
WINDOWS = TAPS + 2
GROUP = TAPS * STEP
OUTSIDE = -1e30
LANES = 128


def kernel(
    n_row,
    n_col,
    group_bins,
    pieces,
    row_weight,
    col_weight,
    pair_weight,
    conv_weight,
    mix_weight,
    out,
    row_proj,
    col_proj,
    base,
    result,
):
    f32, bf16 = jnp.float32, jnp.bfloat16
    row, col = lax.axis_index("row"), lax.axis_index("col")
    channels, n_rows, n_cols = out.shape
    tiles = n_cols // STEP + 2
    reach = pieces.shape[1] - 2 * PAIR_TILE
    zero = jnp.zeros((), bf16)

    def projected(cells, weight):
        return jnp.dot(cells, weight[...], preferred_element_type=f32).astype(bf16).astype(f32)

    def first_bins(group, weight):
        group = jnp.minimum(group, n_row - 1)
        return projected(pieces[group, pl.ds(reach, PAIR_TILE)], weight)[:STEP]

    def last_bins(group, weight):
        group = jnp.maximum(group, 0)
        return projected(pieces[group, pl.ds(reach + PAIR_TILE, PAIR_TILE)], weight)[STEP:]

    row_proj[:STEP, :] = jnp.where(row == 0, OUTSIDE, last_bins(row - 1, row_weight))
    row_proj[STEP : STEP + n_rows, :] = projected(group_bins[...], row_weight)
    row_proj[STEP + n_rows :, :] = jnp.where(
        row == n_row - 1, OUTSIDE, first_bins(row + 1, row_weight)
    )

    group, second = col // 2, col % 2 == 1
    cells = projected(pieces[group, pl.ds(0, reach)], col_weight)
    here = jnp.where(second, cells[PAIR_TILE:], cells[:n_cols])
    left = jnp.where(col == 0, OUTSIDE, last_bins(group - 1, col_weight))
    left = jnp.where(second, cells[STEP:PAIR_TILE], left)
    right = jnp.where(col == n_col - 1, OUTSIDE, first_bins(group + 1, col_weight))
    right = jnp.where(second, right, cells[n_cols : n_cols + STEP])
    columns = jnp.concatenate([left, here, right], axis=0)
    width = columns.shape[1]
    columns = columns.reshape(tiles, 1, STEP, width)
    columns = jnp.concatenate([columns, columns], axis=1).reshape(tiles * PAIR_TILE, width)
    col_proj[...] = columns.astype(bf16)

    spare = (n_rows + PAIR_TILE) // 2
    base[spare:] = jnp.zeros_like(base[spare:])

    def pair_rows(at, _):
        rows = row_proj[pl.ds(pl.multiple_of(at * PAIR_TILE, STEP), PAIR_TILE), :]
        acts = []
        for k in range(0, PAIR_TILE, 2):
            spread = [jnp.broadcast_to(rows[k + e : k + e + 1], (STEP, width)) for e in range(2)]
            spread = jnp.concatenate(spread, axis=0).astype(bf16)
            cells = col_proj[...].reshape(tiles, PAIR_TILE, width) + spread[None]
            acts.append(jnp.maximum(cells, zero).reshape(tiles * PAIR_TILE, width))
        act = jnp.concatenate(acts, axis=0)
        hidden = jnp.dot(act, pair_weight[...], preferred_element_type=f32).astype(bf16)
        base[pl.ds(at * STEP, STEP)] = hidden.reshape(STEP, tiles * PAIR_TILE, -1)
        return _

    lax.fori_loop(0, (n_rows + PAIR_TILE) // PAIR_TILE, pair_rows, 0)

    span = base.shape[2]
    lane = lax.broadcasted_iota(jnp.int32, (1, LANES), 1)
    pairs = STEP // 2
    cells_in = 2 * n_cols

    def conv_rows(at, _):
        first = at * (GROUP // 2)
        cells, windows = [], []
        for p in range(pairs):
            parts = []
            for low in range(0, span, LANES):
                part = None
                for m in range(WINDOWS):
                    begin, end = m * channels - low, (m + 1) * channels - low
                    if end <= 0 or begin >= LANES:
                        continue
                    window = base[first + p + pairs * m, :, low : low + LANES]
                    part = window if part is None else jnp.where(lane >= begin, window, part)
                parts.append(part)
            cells.append(jnp.concatenate(parts, axis=1))
            act = jnp.maximum(cells[-1], zero)
            windows.append(
                jnp.concatenate(
                    [act[b * PAIR_TILE : b * PAIR_TILE + cells_in] for b in range(TAPS)], axis=1
                )
            )
        total = jnp.dot(
            jnp.concatenate(windows, axis=0), conv_weight[...], preferred_element_type=f32
        )
        mid = jnp.maximum(total, 0.0).astype(bf16)
        mixed = jnp.dot(mid, mix_weight[...], preferred_element_type=f32)
        for p in range(pairs):
            full = mixed[p * cells_in : (p + 1) * cells_in] + cells[p][
                PAIR_TILE : PAIR_TILE + cells_in
            ].astype(f32)
            full = full.reshape(n_cols // STEP, 2, STEP, span)
            for e in range(2):
                turned = jnp.transpose(full[:, e].reshape(n_cols, span))
                for m in range(TAPS):
                    row_at = at * GROUP + 2 * p + e + STEP * m
                    result[pl.ds(pl.multiple_of(row_at * channels, STEP), channels), :] = turned[
                        (m + 1) * channels : (m + 2) * channels
                    ]
        return _

    lax.fori_loop(0, -(-n_rows // GROUP), conv_rows, 0)

    def turn(o, _):
        out[o] = result[pl.ds(o, n_rows, stride=channels), :].astype(bf16)
        return _

    lax.fori_loop(0, channels, turn, 0)


def on_device(trunk, row_weight, column_weight, pair_map_weight, dilated_weight, mixing_weight):
    n_row = lax.axis_size("row")
    n_col = lax.axis_size("col")
    shard, depth = trunk.shape
    n_rows, n_cols = shard * n_col, shard * n_row
    channels = pair_map_weight.shape[1]
    width = row_weight.shape[1]
    span = -(-WINDOWS * channels // LANES) * LANES
    pair = jnp.pad(jnp.tile(pair_map_weight, (1, WINDOWS)), ((0, 0), (0, span - WINDOWS * channels)))
    taps = jnp.transpose(dilated_weight, (1, 0, 3, 2))
    conv = jnp.concatenate(
        [
            jnp.pad(
                taps.reshape(TAPS, TAPS * channels, channels),
                ((0, 0), (m * channels, span - (m + TAPS) * channels), (0, 0)),
            )
            for m in range(TAPS)
        ],
        axis=2,
    )
    conv = jnp.pad(conv, ((0, 0), (0, 0), (0, span - TAPS * channels))).reshape(TAPS * span, span)
    mix = jnp.kron(jnp.eye(TAPS, dtype=mixing_weight.dtype), mixing_weight.T)
    mix = jnp.pad(mix, ((0, span - TAPS * channels), (channels, span - (TAPS + 1) * channels)))

    copies = jnp.broadcast_to(trunk[None], (n_col, shard, depth))
    group_bins = lax.all_to_all(copies, "col", 0, 0).reshape(n_rows, depth)
    reach = n_cols + PAIR_TILE
    start = jnp.where(lax.axis_index("col") % 2 == 0, 0, n_rows - reach)
    piece = jnp.concatenate(
        [
            lax.dynamic_slice_in_dim(group_bins, start, reach, 0),
            group_bins[:PAIR_TILE],
            group_bins[-PAIR_TILE:],
        ],
        axis=0,
    )
    pieces = lax.all_to_all(jnp.broadcast_to(piece[None], (n_row,) + piece.shape), "row", 0, 0)
    groups = -(-n_rows // GROUP)
    return pl.pallas_call(
        functools.partial(kernel, n_row, n_col),
        out_shape=jax.ShapeDtypeStruct((channels, n_rows, n_cols), jnp.bfloat16),
        scratch_shapes=[
            pltpu.VMEM((n_rows + PAIR_TILE, width), jnp.float32),
            pltpu.VMEM((2 * (n_cols + PAIR_TILE), width), jnp.bfloat16),
            pltpu.VMEM((groups * GROUP // 2 + STEP, 2 * (n_cols + PAIR_TILE), span), jnp.bfloat16),
            pltpu.VMEM((groups * GROUP * channels, n_cols), jnp.float32),
        ],
        compiler_params=pltpu.CompilerParams(vmem_limit_bytes=56 * 2**20),
        name="pair_block",
    )(group_bins, pieces, row_weight, column_weight, pair, conv, mix)


def solution(mesh):
    return jax.shard_map(
        on_device,
        mesh=mesh,
        in_specs=(P(("row", "col"), None), P(), P(), P(), P(), P()),
        out_specs=P(None, "row", "col"),
        check_vma=False,
    )
```

```python
import functools

import jax
import jax.numpy as jnp
from jax import lax
from jax.experimental import pallas as pl
from jax.experimental.pallas import tpu as pltpu
from jax.sharding import Mesh
from jax.sharding import PartitionSpec as P

STEP = 8
TILE = 2 * STEP
TAPS = 3
WINDOWS = TAPS + 2
GROUP = TAPS * STEP
AHEAD = GROUP + TILE
OUTSIDE = -1e30
LANES = 128


def kernel(
    n_row,
    n_chip,
    mine,
    other,
    row_weight,
    col_weight,
    pair_weight,
    conv_weight,
    mix_weight,
    out,
    row_proj,
    col_proj,
    base,
    result,
):
    f32, bf16 = jnp.float32, jnp.bfloat16
    row, chip, core = (lax.axis_index(name) for name in ("row", "chip", "core"))
    channels, n_rows, n_cols = out.shape
    shard = mine.shape[1]
    tiles = n_cols // STEP + 2
    span = base.shape[2]
    groups = -(-n_rows // GROUP)
    zero = jnp.zeros((), bf16)

    def projected(cells, weight):
        return jnp.dot(cells, weight[...], preferred_element_type=f32).astype(bf16).astype(f32)

    def last_bins(at, weight):
        tail = pl.ds(shard - TILE, TILE)
        at = jnp.maximum(at, 0)
        return projected(jnp.where(core == 1, mine[at, tail], other[at, tail]), weight)[STEP:]

    def first_bins(at, weight):
        head = pl.ds(0, TILE)
        at = jnp.minimum(at, n_row * n_chip - 1)
        return projected(jnp.where(core == 0, mine[at, head], other[at, head]), weight)[:STEP]

    first = chip * n_chip + core * (n_chip // 2)
    left = jnp.where((chip == 0) & (core == 0), OUTSIDE, last_bins(first - 1, col_weight))
    right = jnp.where(
        (chip == n_chip - 1) & (core == 1), OUTSIDE, first_bins(first + n_chip // 2, col_weight)
    )

    def put_columns(at, cells):
        size, width = cells.shape
        cells = cells.reshape(size // STEP, 1, STEP, width)
        cells = jnp.concatenate([cells, cells], axis=1).reshape(2 * size, width)
        col_proj[pl.ds(pl.multiple_of(2 * at, TILE), 2 * size), :] = cells.astype(bf16)

    put_columns(0, left)
    put_columns(STEP + n_cols, right)
    for source, turn in ((mine, core), (other, 1 - core)):
        count = n_chip // 2
        cells = source[pl.ds(first, count)].reshape(count * shard, -1)
        cells = projected(cells, col_weight)
        for k in range(count):
            put_columns(STEP + (2 * k + turn) * shard, cells[k * shard : (k + 1) * shard])

    first = row * n_chip
    row_proj[:STEP, :] = jnp.where(row == 0, OUTSIDE, last_bins(first - 1, row_weight))
    row_proj[STEP + n_rows : TILE + n_rows, :] = jnp.where(
        row == n_row - 1, OUTSIDE, first_bins(first + n_chip, row_weight)
    )
    spare = row_proj.shape[0] - TILE - n_rows
    row_proj[TILE + n_rows :, :] = jnp.full((spare, row_proj.shape[1]), OUTSIDE, f32)
    for source, turn in ((mine, core), (other, 1 - core)):
        cells = projected(source[pl.ds(first, n_chip)].reshape(n_chip * shard, -1), row_weight)
        for k in range(n_chip):
            at = STEP + (2 * k + turn) * shard
            row_proj[pl.ds(pl.multiple_of(at, STEP), shard), :] = cells[k * shard : (k + 1) * shard]

    width = row_proj.shape[1]

    def pair_rows(start, count):
        rows = row_proj[pl.ds(pl.multiple_of(start, STEP), count), :]
        acts = []
        for k in range(0, count, 2):
            spread = [jnp.broadcast_to(rows[k + e : k + e + 1], (STEP, width)) for e in range(2)]
            spread = jnp.concatenate(spread, axis=0).astype(bf16)
            cells = col_proj[...].reshape(tiles, TILE, width) + spread[None]
            acts.append(jnp.maximum(cells, zero).reshape(tiles * TILE, width))
        act = jnp.concatenate(acts, axis=0)
        hidden = jnp.dot(act, pair_weight[...], preferred_element_type=f32).astype(bf16)
        base[pl.ds(start // 2, count // 2)] = hidden.reshape(count // 2, tiles * TILE, span)

    lane = lax.broadcasted_iota(jnp.int32, (1, LANES), 1)
    pairs = STEP // 2
    cells_in = 2 * n_cols

    def conv_rows(at):
        first = at * (GROUP // 2)
        cells, windows = [], []
        for p in range(pairs):
            parts = []
            for low in range(0, span, LANES):
                part = None
                for m in range(WINDOWS):
                    begin, end = m * channels - low, (m + 1) * channels - low
                    if end <= 0 or begin >= LANES:
                        continue
                    window = base[first + p + pairs * m, :, low : low + LANES]
                    part = window if part is None else jnp.where(lane >= begin, window, part)
                parts.append(part)
            cells.append(jnp.concatenate(parts, axis=1))
            act = jnp.maximum(cells[-1], zero)
            windows.append(
                jnp.concatenate([act[b * TILE : b * TILE + cells_in] for b in range(TAPS)], axis=1)
            )
        total = jnp.dot(
            jnp.concatenate(windows, axis=0), conv_weight[...], preferred_element_type=f32
        )
        mid = jnp.maximum(total, 0.0).astype(bf16)
        mixed = jnp.dot(mid, mix_weight[...], preferred_element_type=f32)
        for p in range(pairs):
            full = mixed[p * cells_in : (p + 1) * cells_in]
            full = full + cells[p][TILE : TILE + cells_in].astype(f32)
            full = full.reshape(n_cols // STEP, 2, STEP, span)
            for e in range(2):
                turned = jnp.transpose(full[:, e].reshape(n_cols, span))
                for m in range(TAPS):
                    row_at = at * GROUP + 2 * p + e + STEP * m
                    result[pl.ds(pl.multiple_of(row_at * channels, STEP), channels), :] = turned[
                        (m + 1) * channels : (m + 2) * channels
                    ]

    def turn_tiles(at):
        for k in range(2):
            start = jnp.minimum(at * GROUP // TILE + k, n_rows // TILE - 1) * TILE
            start = pl.multiple_of(start, TILE)
            for o in range(channels):
                cells = result[pl.ds(start * channels + o, TILE, stride=channels), :]
                out[o, pl.ds(start, TILE), :] = cells.astype(bf16)

    pair_rows(0, GROUP)
    pair_rows(GROUP, TILE)

    def step(at, _):
        conv_rows(at)
        pair_rows(at * GROUP + AHEAD, GROUP)
        turn_tiles(at)
        return _

    lax.fori_loop(0, groups - 1, step, 0)
    conv_rows(groups - 1)
    turn_tiles(groups - 1)


def on_device(trunk, row_weight, column_weight, pair_map_weight, dilated_weight, mixing_weight):
    n_row, n_chip = lax.axis_size("row"), lax.axis_size("chip")
    shard, depth = trunk.shape
    n_rows, n_cols = shard * n_chip * 2, shard * n_row
    channels = pair_map_weight.shape[1]
    width = row_weight.shape[1]
    span = -(-WINDOWS * channels // LANES) * LANES
    pair = jnp.pad(jnp.tile(pair_map_weight, (1, WINDOWS)), ((0, 0), (0, span - WINDOWS * channels)))
    taps = jnp.transpose(dilated_weight, (1, 0, 3, 2))
    conv = jnp.concatenate(
        [
            jnp.pad(
                taps.reshape(TAPS, TAPS * channels, channels),
                ((0, 0), (m * channels, span - (m + TAPS) * channels), (0, 0)),
            )
            for m in range(TAPS)
        ],
        axis=2,
    )
    conv = jnp.pad(conv, ((0, 0), (0, 0), (0, span - TAPS * channels))).reshape(TAPS * span, span)
    mix = jnp.kron(jnp.eye(TAPS, dtype=mixing_weight.dtype), mixing_weight.T)
    mix = jnp.pad(mix, ((0, span - TAPS * channels), (channels, span - (TAPS + 1) * channels)))

    copies = jnp.broadcast_to(trunk[None], (n_row * n_chip, shard, depth))
    mine = lax.all_to_all(copies, ("row", "chip"), 0, 0)
    other = lax.ppermute(mine, "core", [(0, 1), (1, 0)])
    groups = -(-n_rows // GROUP)
    padded = groups * GROUP + TILE
    return pl.pallas_call(
        functools.partial(kernel, n_row, n_chip),
        out_shape=jax.ShapeDtypeStruct((channels, n_rows, n_cols), jnp.bfloat16),
        scratch_shapes=[
            pltpu.VMEM((padded, width), jnp.float32),
            pltpu.VMEM((2 * (n_cols + TILE), width), jnp.bfloat16),
            pltpu.VMEM((padded // 2, 2 * (n_cols + TILE), span), jnp.bfloat16),
            pltpu.VMEM((groups * GROUP * channels, n_cols), jnp.float32),
        ],
        compiler_params=pltpu.CompilerParams(vmem_limit_bytes=52 * 2**20),
        name="pair_block",
    )(mine, other, row_weight, column_weight, pair, conv, mix)


def solution(mesh):
    n_row, n_col = mesh.devices.shape
    chips = Mesh(mesh.devices.reshape(n_row, n_col // 2, 2), ("row", "chip", "core"))
    return jax.shard_map(
        on_device,
        mesh=chips,
        in_specs=(P(("row", "chip", "core"), None), P(), P(), P(), P(), P()),
        out_specs=P(None, "row", ("chip", "core")),
        check_vma=False,
    )
```

```python
import functools

import jax
import jax.numpy as jnp
from jax import lax
from jax.experimental import pallas as pl
from jax.experimental.pallas import tpu as pltpu
from jax.sharding import Mesh
from jax.sharding import PartitionSpec as P

STEP = 8
TILE = 2 * STEP
TAPS = 3
WINDOWS = TAPS + 2
GROUP = TAPS * STEP
AHEAD = GROUP + TILE
OUTSIDE = -1e30
LANES = 128


def kernel(
    n_row,
    n_chip,
    mine,
    other,
    row_weight,
    col_weight,
    pair_weight,
    conv_weight,
    mix_weight,
    out,
    row_proj,
    col_proj,
    base,
    result,
):
    f32, bf16 = jnp.float32, jnp.bfloat16
    row, chip, core = (lax.axis_index(name) for name in ("row", "chip", "core"))
    channels, n_rows, n_cols = out.shape
    shard = mine.shape[1]
    tiles = n_cols // STEP + 2
    groups = -(-n_rows // GROUP)
    zero = jnp.zeros((), bf16)

    def projected(cells, weight):
        return jnp.dot(cells, weight[...], preferred_element_type=f32).astype(bf16).astype(f32)

    def last_bins(at, weight):
        tail = pl.ds(shard - TILE, TILE)
        at = jnp.maximum(at, 0)
        return projected(jnp.where(core == 1, mine[at, tail], other[at, tail]), weight)[STEP:]

    def first_bins(at, weight):
        head = pl.ds(0, TILE)
        at = jnp.minimum(at, n_row * n_chip - 1)
        return projected(jnp.where(core == 0, mine[at, head], other[at, head]), weight)[:STEP]

    first = chip * n_chip + core * (n_chip // 2)
    left = jnp.where((chip == 0) & (core == 0), OUTSIDE, last_bins(first - 1, col_weight))
    right = jnp.where(
        (chip == n_chip - 1) & (core == 1), OUTSIDE, first_bins(first + n_chip // 2, col_weight)
    )

    def put_columns(at, cells):
        size, width = cells.shape
        cells = cells.reshape(size // STEP, 1, STEP, width)
        cells = jnp.concatenate([cells, cells], axis=1).reshape(2 * size, width)
        col_proj[pl.ds(pl.multiple_of(2 * at, TILE), 2 * size), :] = cells.astype(bf16)

    put_columns(0, left)
    put_columns(STEP + n_cols, right)
    for source, turn in ((mine, core), (other, 1 - core)):
        count = n_chip // 2
        cells = source[pl.ds(first, count)].reshape(count * shard, -1)
        cells = projected(cells, col_weight)
        for k in range(count):
            put_columns(STEP + (2 * k + turn) * shard, cells[k * shard : (k + 1) * shard])

    first = row * n_chip
    row_proj[:STEP, :] = jnp.where(row == 0, OUTSIDE, last_bins(first - 1, row_weight))
    row_proj[STEP + n_rows : TILE + n_rows, :] = jnp.where(
        row == n_row - 1, OUTSIDE, first_bins(first + n_chip, row_weight)
    )
    spare = row_proj.shape[0] - TILE - n_rows
    row_proj[TILE + n_rows :, :] = jnp.full((spare, row_proj.shape[1]), OUTSIDE, f32)
    for source, turn in ((mine, core), (other, 1 - core)):
        cells = projected(source[pl.ds(first, n_chip)].reshape(n_chip * shard, -1), row_weight)
        for k in range(n_chip):
            at = STEP + (2 * k + turn) * shard
            row_proj[pl.ds(pl.multiple_of(at, STEP), shard), :] = cells[k * shard : (k + 1) * shard]

    width = row_proj.shape[1]

    def pair_rows(start, count, kind):
        for part in range(0, count, STEP):
            rows = row_proj[pl.ds(pl.multiple_of(start + part, STEP), STEP), :]
            weight = pair_weight[(kind + part // STEP) % TAPS]
            for k in range(0, STEP, 2):
                spread = [jnp.broadcast_to(rows[k + e : k + e + 1], (STEP, width)) for e in range(2)]
                spread = jnp.concatenate(spread, axis=0).astype(bf16)
                cells = col_proj[...].reshape(tiles, TILE, width) + spread[None]
                act = jnp.maximum(cells, zero).reshape(tiles * TILE, width)
                hidden = jnp.dot(act, weight, preferred_element_type=f32)
                base[(start + part + k) // 2] = hidden.astype(bf16)

    lane = lax.broadcasted_iota(jnp.int32, (1, LANES), 1)
    pairs = STEP // 2
    cells_in = 2 * n_cols

    rest = TAPS * channels - LANES
    places = (channels, LANES + rest, LANES + rest + channels)

    def conv_rows(at):
        first = at * (GROUP // 2)
        for p in range(pairs):
            rows = [base[first + p + pairs * m] for m in range(WINDOWS)]
            low = jnp.where(lane < channels, rows[0], jnp.where(lane < 2 * channels, rows[1], rows[4]))
            high = jnp.where(lane < rest, rows[4], jnp.where(lane < rest + channels, rows[2], rows[3]))
            cells = jnp.concatenate([low, high], axis=1)
            act = jnp.maximum(cells, zero)
            shifted = [act[b * TILE : b * TILE + cells_in] for b in range(TAPS)]
            total = jnp.dot(
                jnp.concatenate(shifted, axis=1), conv_weight[...], preferred_element_type=f32
            )
            mid = jnp.maximum(total, 0.0).astype(bf16)
            mixed = jnp.dot(mid, mix_weight[...], preferred_element_type=f32)
            full = mixed + cells[TILE : TILE + cells_in].astype(f32)
            full = full.reshape(n_cols // STEP, 2, STEP, 2 * LANES)
            for e in range(2):
                turned = jnp.transpose(full[:, e].reshape(n_cols, 2 * LANES))
                for m in range(TAPS):
                    row_at = at * GROUP + 2 * p + e + STEP * m
                    result[pl.ds(pl.multiple_of(row_at * channels, STEP), channels), :] = turned[
                        places[m] : places[m] + channels
                    ]

    def turn_tiles(at):
        for k in range(2):
            start = jnp.minimum(at * GROUP // TILE + k, n_rows // TILE - 1) * TILE
            start = pl.multiple_of(start, TILE)
            for o in range(channels):
                cells = result[pl.ds(start * channels + o, TILE, stride=channels), :]
                out[o, pl.ds(start, TILE), :] = cells.astype(bf16)

    pair_rows(0, AHEAD, 0)

    def step(at, _):
        conv_rows(at)
        pair_rows(at * GROUP + AHEAD, GROUP, AHEAD // STEP)
        turn_tiles(at)
        return _

    lax.fori_loop(0, groups - 1, step, 0)
    conv_rows(groups - 1)
    turn_tiles(groups - 1)


def on_device(trunk, row_weight, column_weight, pair_map_weight, dilated_weight, mixing_weight):
    n_row, n_chip = lax.axis_size("row"), lax.axis_size("chip")
    shard, depth = trunk.shape
    n_rows, n_cols = shard * n_chip * 2, shard * n_row
    channels = pair_map_weight.shape[1]
    width = row_weight.shape[1]
    spare = LANES - 2 * channels
    rest = channels - spare
    def gap(size):
        return jnp.zeros((width, size), pair_map_weight.dtype)

    kinds = (
        (pair_map_weight, gap(rest), pair_map_weight),
        (pair_map_weight[:, :rest], gap(channels - rest), pair_map_weight, pair_map_weight[:, rest:]),
        (gap(rest), pair_map_weight),
    )
    pair = []
    for kind in kinds:
        kind = jnp.concatenate(kind, axis=1)
        pair.append(jnp.pad(kind, ((0, 0), (0, LANES - kind.shape[1]))))
    pair = jnp.stack(pair)
    taps = jnp.transpose(dilated_weight, (1, 0, 3, 2))
    rows = []
    for i in range(WINDOWS):
        blocks = [
            taps[:, i - m] if 0 <= i - m < TAPS else jnp.zeros_like(taps[:, 0]) for m in range(TAPS)
        ]
        rows.append(jnp.concatenate(blocks, axis=2))
    rows = [rows[0], rows[1], rows[4][:, rest:], rows[4][:, :rest], rows[2], rows[3]]
    conv = jnp.concatenate(rows, axis=1)
    free = 2 * LANES - conv.shape[1]
    conv = jnp.pad(conv, ((0, 0), (0, free), (0, 2 * LANES - TAPS * channels)))
    conv = conv.reshape(TAPS * 2 * LANES, 2 * LANES)
    mix = jnp.kron(jnp.eye(TAPS, dtype=mixing_weight.dtype), mixing_weight.T)
    between = jnp.zeros((mix.shape[0], spare), mix.dtype)
    mix = jnp.concatenate(
        [jnp.zeros_like(mix[:, :channels]), mix[:, :channels], between]
        + [jnp.zeros_like(mix[:, :rest]), mix[:, channels:]],
        axis=1,
    )
    mix = jnp.pad(mix, ((0, 2 * LANES - mix.shape[0]), (0, 2 * LANES - mix.shape[1])))

    copies = jnp.broadcast_to(trunk[None], (n_row * n_chip, shard, depth))
    mine = lax.all_to_all(copies, ("row", "chip"), 0, 0)
    other = lax.ppermute(mine, "core", [(0, 1), (1, 0)])
    groups = -(-n_rows // GROUP)
    padded = groups * GROUP + TILE
    return pl.pallas_call(
        functools.partial(kernel, n_row, n_chip),
        out_shape=jax.ShapeDtypeStruct((channels, n_rows, n_cols), jnp.bfloat16),
        scratch_shapes=[
            pltpu.VMEM((padded, width), jnp.float32),
            pltpu.VMEM((2 * (n_cols + TILE), width), jnp.bfloat16),
            pltpu.VMEM((padded // 2, 2 * (n_cols + TILE), LANES), jnp.bfloat16),
            pltpu.VMEM((groups * GROUP * channels, n_cols), jnp.float32),
        ],
        compiler_params=pltpu.CompilerParams(vmem_limit_bytes=52 * 2**20),
        name="pair_block",
    )(mine, other, row_weight, column_weight, pair, conv, mix)


def solution(mesh):
    n_row, n_col = mesh.devices.shape
    chips = Mesh(mesh.devices.reshape(n_row, n_col // 2, 2), ("row", "chip", "core"))
    return jax.shard_map(
        on_device,
        mesh=chips,
        in_specs=(P(("row", "chip", "core"), None), P(), P(), P(), P(), P()),
        out_specs=P(None, "row", ("chip", "core")),
        check_vma=False,
    )
```

```python
import functools

import jax
import jax.numpy as jnp
from jax import lax
from jax.experimental import pallas as pl
from jax.experimental.pallas import tpu as pltpu
from jax.sharding import Mesh
from jax.sharding import PartitionSpec as P

STEP = 8
TILE = 2 * STEP
TAPS = 3
WINDOWS = TAPS + 2
GROUP = TAPS * STEP
AHEAD = GROUP + TILE
OUTSIDE = -1e30
LANES = 128


def kernel(
    n_row,
    n_chip,
    mine,
    other,
    row_weight,
    col_weight,
    pair_weight,
    conv_weight,
    mix_weight,
    out,
    row_proj,
    col_proj,
    base,
    result,
):
    f32, bf16 = jnp.float32, jnp.bfloat16
    row, chip, core = (lax.axis_index(name) for name in ("row", "chip", "core"))
    channels, n_rows, n_cols = out.shape
    shard = mine.shape[1]
    tiles = n_cols // STEP + 2
    groups = -(-n_rows // GROUP)
    zero = jnp.zeros((), bf16)

    def projected(cells, weight):
        return jnp.dot(cells, weight[...], preferred_element_type=f32).astype(bf16).astype(f32)

    def last_bins(at, weight):
        tail = pl.ds(shard - TILE, TILE)
        at = jnp.maximum(at, 0)
        return projected(jnp.where(core == 1, mine[at, tail], other[at, tail]), weight)[STEP:]

    def first_bins(at, weight):
        head = pl.ds(0, TILE)
        at = jnp.minimum(at, n_row * n_chip - 1)
        return projected(jnp.where(core == 0, mine[at, head], other[at, head]), weight)[:STEP]

    first = chip * n_chip + core * (n_chip // 2)
    left = jnp.where((chip == 0) & (core == 0), OUTSIDE, last_bins(first - 1, col_weight))
    right = jnp.where(
        (chip == n_chip - 1) & (core == 1), OUTSIDE, first_bins(first + n_chip // 2, col_weight)
    )

    def put_columns(at, cells):
        size, width = cells.shape
        cells = cells.reshape(size // STEP, 1, STEP, width)
        cells = jnp.concatenate([cells, cells], axis=1).reshape(2 * size, width)
        col_proj[pl.ds(pl.multiple_of(2 * at, TILE), 2 * size), :] = cells.astype(bf16)

    put_columns(0, left)
    put_columns(STEP + n_cols, right)
    for source, turn in ((mine, core), (other, 1 - core)):
        count = n_chip // 2
        cells = source[pl.ds(first, count)].reshape(count * shard, -1)
        cells = projected(cells, col_weight)
        for k in range(count):
            put_columns(STEP + (2 * k + turn) * shard, cells[k * shard : (k + 1) * shard])

    first = row * n_chip
    row_proj[:STEP, :] = jnp.where(row == 0, OUTSIDE, last_bins(first - 1, row_weight))
    row_proj[STEP + n_rows : TILE + n_rows, :] = jnp.where(
        row == n_row - 1, OUTSIDE, first_bins(first + n_chip, row_weight)
    )
    spare = row_proj.shape[0] - TILE - n_rows
    row_proj[TILE + n_rows :, :] = jnp.full((spare, row_proj.shape[1]), OUTSIDE, f32)
    for source, turn in ((mine, core), (other, 1 - core)):
        cells = projected(source[pl.ds(first, n_chip)].reshape(n_chip * shard, -1), row_weight)
        for k in range(n_chip):
            at = STEP + (2 * k + turn) * shard
            row_proj[pl.ds(pl.multiple_of(at, STEP), shard), :] = cells[k * shard : (k + 1) * shard]

    width = row_proj.shape[1]

    def pair_rows(start, count, kind):
        for part in range(0, count, STEP):
            rows = row_proj[pl.ds(pl.multiple_of(start + part, STEP), STEP), :]
            weight = pair_weight[(kind + part // STEP) % TAPS]
            acts = []
            for k in range(0, STEP, 2):
                spread = [jnp.broadcast_to(rows[k + e : k + e + 1], (STEP, width)) for e in range(2)]
                spread = jnp.concatenate(spread, axis=0).astype(bf16)
                cells = col_proj[...].reshape(tiles, TILE, width) + spread[None]
                acts.append(jnp.maximum(cells, zero).reshape(tiles * TILE, width))
            act = jnp.concatenate(acts, axis=0)
            hidden = jnp.dot(act, weight, preferred_element_type=f32).astype(bf16)
            hidden = hidden.reshape(STEP // 2, tiles * TILE, LANES)
            base[pl.ds((start + part) // 2, STEP // 2)] = hidden

    lane = lax.broadcasted_iota(jnp.int32, (1, LANES), 1)
    pairs = STEP // 2
    cells_in = 2 * n_cols

    rest = TAPS * channels - LANES
    places = (channels, LANES + rest, LANES + rest + channels)

    def conv_rows(at):
        first = at * (GROUP // 2)
        cells, windows = [], []
        for p in range(pairs):
            rows = [base[first + p + pairs * m] for m in range(WINDOWS)]
            low = jnp.where(lane < channels, rows[0], jnp.where(lane < 2 * channels, rows[1], rows[4]))
            high = jnp.where(lane < rest, rows[4], jnp.where(lane < rest + channels, rows[2], rows[3]))
            cells.append(jnp.concatenate([low, high], axis=1))
            act = jnp.maximum(cells[-1], zero)
            shifted = [act[b * TILE : b * TILE + cells_in] for b in range(TAPS)]
            windows.append(jnp.concatenate(shifted, axis=1))
        total = jnp.dot(
            jnp.concatenate(windows, axis=0), conv_weight[...], preferred_element_type=f32
        )
        mid = jnp.maximum(total, 0.0).astype(bf16)
        mixed = jnp.dot(mid, mix_weight[...], preferred_element_type=f32)
        for p in range(pairs):
            full = mixed[p * cells_in : (p + 1) * cells_in]
            full = full + cells[p][TILE : TILE + cells_in].astype(f32)
            full = full.reshape(n_cols // STEP, 2, STEP, 2 * LANES)
            for e in range(2):
                turned = jnp.transpose(full[:, e].reshape(n_cols, 2 * LANES))
                for m in range(TAPS):
                    row_at = at * GROUP + 2 * p + e + STEP * m
                    result[pl.ds(pl.multiple_of(row_at * channels, STEP), channels), :] = turned[
                        places[m] : places[m] + channels
                    ]

    def turn_tiles(at):
        for k in range(2):
            start = jnp.minimum(at * GROUP // TILE + k, n_rows // TILE - 1) * TILE
            start = pl.multiple_of(start, TILE)
            for o in range(channels):
                cells = result[pl.ds(start * channels + o, TILE, stride=channels), :]
                out[o, pl.ds(start, TILE), :] = cells.astype(bf16)

    pair_rows(0, AHEAD, 0)

    def step(at, _):
        conv_rows(at)
        pair_rows(at * GROUP + AHEAD, GROUP, AHEAD // STEP)
        turn_tiles(at)
        return _

    lax.fori_loop(0, groups - 1, step, 0)
    conv_rows(groups - 1)
    turn_tiles(groups - 1)


def on_device(trunk, row_weight, column_weight, pair_map_weight, dilated_weight, mixing_weight):
    n_row, n_chip = lax.axis_size("row"), lax.axis_size("chip")
    shard, depth = trunk.shape
    n_rows, n_cols = shard * n_chip * 2, shard * n_row
    channels = pair_map_weight.shape[1]
    width = row_weight.shape[1]
    spare = LANES - 2 * channels
    rest = channels - spare
    def gap(size):
        return jnp.zeros((width, size), pair_map_weight.dtype)

    kinds = (
        (pair_map_weight, gap(rest), pair_map_weight),
        (pair_map_weight[:, :rest], gap(channels - rest), pair_map_weight, pair_map_weight[:, rest:]),
        (gap(rest), pair_map_weight),
    )
    pair = []
    for kind in kinds:
        kind = jnp.concatenate(kind, axis=1)
        pair.append(jnp.pad(kind, ((0, 0), (0, LANES - kind.shape[1]))))
    pair = jnp.stack(pair)
    taps = jnp.transpose(dilated_weight, (1, 0, 3, 2))
    rows = []
    for i in range(WINDOWS):
        blocks = [
            taps[:, i - m] if 0 <= i - m < TAPS else jnp.zeros_like(taps[:, 0]) for m in range(TAPS)
        ]
        rows.append(jnp.concatenate(blocks, axis=2))
    rows = [rows[0], rows[1], rows[4][:, rest:], rows[4][:, :rest], rows[2], rows[3]]
    conv = jnp.concatenate(rows, axis=1)
    free = 2 * LANES - conv.shape[1]
    conv = jnp.pad(conv, ((0, 0), (0, free), (0, 2 * LANES - TAPS * channels)))
    conv = conv.reshape(TAPS * 2 * LANES, 2 * LANES)
    mix = jnp.kron(jnp.eye(TAPS, dtype=mixing_weight.dtype), mixing_weight.T)
    between = jnp.zeros((mix.shape[0], spare), mix.dtype)
    mix = jnp.concatenate(
        [jnp.zeros_like(mix[:, :channels]), mix[:, :channels], between]
        + [jnp.zeros_like(mix[:, :rest]), mix[:, channels:]],
        axis=1,
    )
    mix = jnp.pad(mix, ((0, 2 * LANES - mix.shape[0]), (0, 2 * LANES - mix.shape[1])))

    copies = jnp.broadcast_to(trunk[None], (n_row * n_chip, shard, depth))
    mine = lax.all_to_all(copies, ("row", "chip"), 0, 0)
    other = lax.ppermute(mine, "core", [(0, 1), (1, 0)])
    groups = -(-n_rows // GROUP)
    padded = groups * GROUP + TILE
    return pl.pallas_call(
        functools.partial(kernel, n_row, n_chip),
        out_shape=jax.ShapeDtypeStruct((channels, n_rows, n_cols), jnp.bfloat16),
        scratch_shapes=[
            pltpu.VMEM((padded, width), jnp.float32),
            pltpu.VMEM((2 * (n_cols + TILE), width), jnp.bfloat16),
            pltpu.VMEM((padded // 2, 2 * (n_cols + TILE), LANES), jnp.bfloat16),
            pltpu.VMEM((groups * GROUP * channels, n_cols), jnp.float32),
        ],
        compiler_params=pltpu.CompilerParams(vmem_limit_bytes=52 * 2**20),
        name="pair_block",
    )(mine, other, row_weight, column_weight, pair, conv, mix)


def solution(mesh):
    n_row, n_col = mesh.devices.shape
    chips = Mesh(mesh.devices.reshape(n_row, n_col // 2, 2), ("row", "chip", "core"))
    return jax.shard_map(
        on_device,
        mesh=chips,
        in_specs=(P(("row", "chip", "core"), None), P(), P(), P(), P(), P()),
        out_specs=P(None, "row", ("chip", "core")),
        check_vma=False,
    )
```

```python
import functools

import jax
import jax.numpy as jnp
from jax import lax
from jax.experimental import pallas as pl
from jax.experimental.pallas import tpu as pltpu
from jax.sharding import Mesh
from jax.sharding import PartitionSpec as P

STEP = 8
TILE = 2 * STEP
TAPS = 3
WINDOWS = TAPS + 2
GROUP = TAPS * STEP
AHEAD = GROUP + TILE
OUTSIDE = -1e30
MATRIX = 256


def kernel(
    n_row,
    n_chip,
    mine,
    other,
    row_weight,
    col_weight,
    pair_weight,
    conv_weight,
    mix_weight,
    out,
    row_proj,
    col_proj,
    acts,
    base,
    result,
):
    f32, bf16 = jnp.float32, jnp.bfloat16
    row, chip, core = (lax.axis_index(name) for name in ("row", "chip", "core"))
    channels, n_rows, n_cols = out.shape
    shard = mine.shape[1]
    tiles = n_cols // TILE + 1
    groups = -(-n_rows // GROUP)
    zero = jnp.zeros((), bf16)

    def projected(cells, weight):
        return jnp.dot(cells, weight[...], preferred_element_type=f32).astype(bf16).astype(f32)

    def last_bins(at, weight):
        tail = pl.ds(shard - TILE, TILE)
        at = jnp.maximum(at, 0)
        return projected(jnp.where(core == 1, mine[at, tail], other[at, tail]), weight)[STEP:]

    def first_bins(at, weight):
        head = pl.ds(0, TILE)
        at = jnp.minimum(at, n_row * n_chip - 1)
        return projected(jnp.where(core == 0, mine[at, head], other[at, head]), weight)[:STEP]

    first = chip * n_chip + core * (n_chip // 2)
    left = jnp.where((chip == 0) & (core == 0), OUTSIDE, last_bins(first - 1, col_weight))
    right = jnp.where(
        (chip == n_chip - 1) & (core == 1), OUTSIDE, first_bins(first + n_chip // 2, col_weight)
    )

    col_proj[n_cols:, :] = jnp.concatenate([right, left], axis=0).astype(bf16)
    for source, turn in ((mine, core), (other, 1 - core)):
        count = n_chip // 2
        cells = source[pl.ds(first, count)].reshape(count * shard, -1)
        cells = projected(cells, col_weight).astype(bf16)
        for k in range(count):
            at = pl.multiple_of((2 * k + turn) * shard, TILE)
            col_proj[pl.ds(at, shard), :] = cells[k * shard : (k + 1) * shard]

    first = row * n_chip
    row_proj[:STEP, :] = jnp.where(row == 0, OUTSIDE, last_bins(first - 1, row_weight))
    row_proj[STEP + n_rows : TILE + n_rows, :] = jnp.where(
        row == n_row - 1, OUTSIDE, first_bins(first + n_chip, row_weight)
    )
    spare = row_proj.shape[0] - TILE - n_rows
    row_proj[TILE + n_rows :, :] = jnp.full((spare, row_proj.shape[1]), OUTSIDE, f32)
    for source, turn in ((mine, core), (other, 1 - core)):
        cells = projected(source[pl.ds(first, n_chip)].reshape(n_chip * shard, -1), row_weight)
        for k in range(n_chip):
            at = STEP + (2 * k + turn) * shard
            row_proj[pl.ds(pl.multiple_of(at, STEP), shard), :] = cells[k * shard : (k + 1) * shard]

    width = row_proj.shape[1]

    lane = lax.broadcasted_iota(jnp.int32, (1, n_cols), 1)
    transposed = (((1,), (1,)), ((), ()))

    def pair_rows(start, count):
        rows = row_proj[pl.ds(pl.multiple_of(start, STEP), count), :]
        inner, outer = [], []
        for k in range(count):
            spread = jnp.broadcast_to(rows[k : k + 1], (TILE, width)).astype(bf16)
            cells = col_proj[...].reshape(tiles, TILE, width) + spread[None]
            act = jnp.maximum(cells, zero)
            inner.append(act[:-1].reshape(n_cols, width))
            outer.append(act[-1])
        act = jnp.concatenate(inner + outer, axis=0)
        hidden = lax.dot_general(pair_weight[...], act, transposed, preferred_element_type=f32)
        for k in range(count):
            here = hidden[:, k * n_cols : (k + 1) * n_cols]
            at = count * n_cols + k * TILE // n_cols * n_cols
            sides = hidden[:, at : at + n_cols]
            sides = pltpu.roll(sides, (n_cols - STEP - k * TILE) % n_cols, 1)
            left = jnp.where(lane < STEP, sides, pltpu.roll(here, STEP, 1))
            right = jnp.where(lane >= n_cols - STEP, sides, pltpu.roll(here, n_cols - STEP, 1))
            here = here.astype(bf16)
            base[start + k] = here
            copies = [left.astype(bf16), here, right.astype(bf16)]
            acts[start + k] = jnp.maximum(jnp.concatenate(copies, axis=0), zero)

    def conv_rows(at):
        first = at * GROUP
        fill = jnp.zeros((conv_weight.shape[1] - WINDOWS * TAPS * channels, n_cols), bf16)
        cells = []
        for p in range(STEP):
            windows = [acts[first + p + STEP * m] for m in range(WINDOWS)]
            cells.append(jnp.concatenate(windows + [fill], axis=0))
        cells = jnp.concatenate(cells, axis=1)
        total = jnp.dot(conv_weight[...], cells, preferred_element_type=f32)
        mid = jnp.maximum(total, 0.0).astype(bf16)
        mixed = jnp.dot(mix_weight[...], mid, preferred_element_type=f32)
        for p in range(STEP):
            for m in range(TAPS):
                row_at = first + p + STEP * m
                here = mixed[m * channels : (m + 1) * channels, p * n_cols : (p + 1) * n_cols]
                here = here + base[row_at + STEP].astype(f32)
                result[pl.ds(pl.multiple_of(row_at * channels, STEP), channels), :] = here

    def turn_tiles(at):
        for k in range(2):
            start = jnp.minimum(at * GROUP // TILE + k, n_rows // TILE - 1) * TILE
            start = pl.multiple_of(start, TILE)
            for o in range(channels):
                cells = result[pl.ds(start * channels + o, TILE, stride=channels), :]
                out[o, pl.ds(start, TILE), :] = cells.astype(bf16)

    pair_rows(0, GROUP)
    pair_rows(GROUP, TILE)

    def step(at, _):
        conv_rows(at)
        pair_rows(at * GROUP + AHEAD, GROUP)
        turn_tiles(at)
        return _

    lax.fori_loop(0, groups - 1, step, 0)
    conv_rows(groups - 1)
    turn_tiles(groups - 1)


def on_device(trunk, row_weight, column_weight, pair_map_weight, dilated_weight, mixing_weight):
    n_row, n_chip = lax.axis_size("row"), lax.axis_size("chip")
    shard, depth = trunk.shape
    n_rows, n_cols = shard * n_chip * 2, shard * n_row
    channels = pair_map_weight.shape[1]
    width = row_weight.shape[1]
    taps = jnp.transpose(dilated_weight, (2, 0, 1, 3)).reshape(channels, TAPS * TAPS * channels)
    reach = TAPS * channels
    depth_in = -(-WINDOWS * reach // MATRIX) * MATRIX
    conv = jnp.concatenate(
        [jnp.pad(taps, ((0, 0), (m * reach, depth_in - (m + TAPS) * reach))) for m in range(TAPS)],
        axis=0,
    )
    mix = jnp.kron(jnp.eye(TAPS, dtype=mixing_weight.dtype), mixing_weight)

    copies = jnp.broadcast_to(trunk[None], (n_row * n_chip, shard, depth))
    mine = lax.all_to_all(copies, ("row", "chip"), 0, 0)
    other = lax.ppermute(mine, "core", [(0, 1), (1, 0)])
    groups = -(-n_rows // GROUP)
    padded = groups * GROUP + TILE
    return pl.pallas_call(
        functools.partial(kernel, n_row, n_chip),
        out_shape=jax.ShapeDtypeStruct((channels, n_rows, n_cols), jnp.bfloat16),
        scratch_shapes=[
            pltpu.VMEM((padded, width), jnp.float32),
            pltpu.VMEM((n_cols + TILE, width), jnp.bfloat16),
            pltpu.VMEM((padded, TAPS * channels, n_cols), jnp.bfloat16),
            pltpu.VMEM((padded, channels, n_cols), jnp.bfloat16),
            pltpu.VMEM((groups * GROUP * channels, n_cols), jnp.float32),
        ],
        compiler_params=pltpu.CompilerParams(vmem_limit_bytes=52 * 2**20),
        name="pair_block",
    )(mine, other, row_weight, column_weight, pair_map_weight.T, conv, mix)


def solution(mesh):
    n_row, n_col = mesh.devices.shape
    chips = Mesh(mesh.devices.reshape(n_row, n_col // 2, 2), ("row", "chip", "core"))
    return jax.shard_map(
        on_device,
        mesh=chips,
        in_specs=(P(("row", "chip", "core"), None), P(), P(), P(), P(), P()),
        out_specs=P(None, "row", ("chip", "core")),
        check_vma=False,
    )
```

```python
import functools

import jax
import jax.numpy as jnp
from jax import lax
from jax.experimental import pallas as pl
from jax.experimental.pallas import tpu as pltpu
from jax.sharding import Mesh
from jax.sharding import PartitionSpec as P

STEP = 8
TILE = 2 * STEP
TAPS = 3
WINDOWS = TAPS + 2
GROUP = TAPS * STEP
AHEAD = GROUP + TILE
OUTSIDE = -1e30
MATRIX = 256


def kernel(
    n_row,
    n_chip,
    mine,
    other,
    weights,
    conv_weight,
    mix_weight,
    out,
    row_proj,
    col_proj,
    col_turned,
    acts,
    base,
    result,
):
    depth = mine.shape[2]
    row_weight = weights.at[pl.ds(0, depth)]
    col_weight = weights.at[pl.ds(depth, depth)]
    pair_weight = weights.at[pl.ds(2 * depth, out.shape[0])]
    f32, bf16 = jnp.float32, jnp.bfloat16
    row, chip, core = (lax.axis_index(name) for name in ("row", "chip", "core"))
    channels, n_rows, n_cols = out.shape
    shard = mine.shape[1]
    groups = -(-n_rows // GROUP)
    zero = jnp.zeros((), bf16)

    def projected(cells, weight):
        return jnp.dot(cells, weight[...], preferred_element_type=f32).astype(bf16).astype(f32)

    def last_bins(at, weight):
        tail = pl.ds(shard - TILE, TILE)
        at = jnp.maximum(at, 0)
        return projected(jnp.where(core == 1, mine[at, tail], other[at, tail]), weight)[STEP:]

    def first_bins(at, weight):
        head = pl.ds(0, TILE)
        at = jnp.minimum(at, n_row * n_chip - 1)
        return projected(jnp.where(core == 0, mine[at, head], other[at, head]), weight)[:STEP]

    first = chip * n_chip + core * (n_chip // 2)
    left = jnp.where((chip == 0) & (core == 0), OUTSIDE, last_bins(first - 1, col_weight))
    right = jnp.where(
        (chip == n_chip - 1) & (core == 1), OUTSIDE, first_bins(first + n_chip // 2, col_weight)
    )

    col_proj[n_cols:, :] = jnp.concatenate([right, left], axis=0).astype(bf16)
    for source, turn in ((mine, core), (other, 1 - core)):
        count = n_chip // 2
        cells = source[pl.ds(first, count)].reshape(count * shard, -1)
        cells = projected(cells, col_weight).astype(bf16)
        for k in range(count):
            at = pl.multiple_of((2 * k + turn) * shard, TILE)
            col_proj[pl.ds(at, shard), :] = cells[k * shard : (k + 1) * shard]

    width = row_proj.shape[1]
    col_turned[:, :n_cols] = jnp.transpose(col_proj[:n_cols, :].astype(f32)).astype(bf16)
    sides = [col_proj[n_cols:, :].astype(f32)] * (n_cols // TILE)
    col_turned[:, n_cols:] = jnp.transpose(jnp.concatenate(sides, axis=0)).astype(bf16)

    first = row * n_chip
    row_proj[:STEP, :] = jnp.where(row == 0, OUTSIDE, last_bins(first - 1, row_weight))
    row_proj[STEP + n_rows : TILE + n_rows, :] = jnp.where(
        row == n_row - 1, OUTSIDE, first_bins(first + n_chip, row_weight)
    )
    spare = row_proj.shape[0] - TILE - n_rows
    row_proj[TILE + n_rows :, :] = jnp.full((spare, row_proj.shape[1]), OUTSIDE, f32)
    for source, turn in ((mine, core), (other, 1 - core)):
        cells = projected(source[pl.ds(first, n_chip)].reshape(n_chip * shard, -1), row_weight)
        for k in range(n_chip):
            at = STEP + (2 * k + turn) * shard
            row_proj[pl.ds(pl.multiple_of(at, STEP), shard), :] = cells[k * shard : (k + 1) * shard]

    lane = lax.broadcasted_iota(jnp.int32, (1, n_cols), 1)

    def pair_rows(start, count):
        rows = row_proj[pl.ds(pl.multiple_of(start, STEP), count), :]
        turned = jnp.transpose(rows).astype(bf16)
        inner, outer = [], []
        for k in range(count):
            spread = jnp.broadcast_to(turned[:, k : k + 1], (width, n_cols))
            inner.append(jnp.maximum(col_turned[:, :n_cols] + spread, zero))
            at = k * TILE % n_cols
            sides = spread if at == 0 else jnp.where(lane >= at, spread, sides)
            if at + TILE == n_cols:
                outer.append(jnp.maximum(col_turned[:, n_cols:] + sides, zero))
        act = jnp.concatenate(inner + outer, axis=1)
        hidden = jnp.dot(pair_weight[...], act, preferred_element_type=f32)
        for k in range(count):
            here = hidden[:, k * n_cols : (k + 1) * n_cols]
            at = count * n_cols + k * TILE // n_cols * n_cols
            sides = hidden[:, at : at + n_cols]
            sides = pltpu.roll(sides, (n_cols - STEP - k * TILE) % n_cols, 1)
            left = jnp.where(lane < STEP, sides, pltpu.roll(here, STEP, 1))
            right = jnp.where(lane >= n_cols - STEP, sides, pltpu.roll(here, n_cols - STEP, 1))
            here = here.astype(bf16)
            base[start + k] = here
            copies = [left.astype(bf16), here, right.astype(bf16)]
            acts[start + k] = jnp.maximum(jnp.concatenate(copies, axis=0), zero)

    def conv_rows(at):
        first = at * GROUP
        fill = jnp.zeros((conv_weight.shape[1] - WINDOWS * TAPS * channels, n_cols), bf16)
        cells = []
        for p in range(STEP):
            windows = [acts[first + p + STEP * m] for m in range(WINDOWS)]
            cells.append(jnp.concatenate(windows + [fill], axis=0))
        cells = jnp.concatenate(cells, axis=1)
        total = jnp.dot(conv_weight[...], cells, preferred_element_type=f32)
        mid = jnp.maximum(total, 0.0).astype(bf16)
        mixed = jnp.dot(mix_weight[...], mid, preferred_element_type=f32)
        for p in range(STEP):
            for m in range(TAPS):
                row_at = first + p + STEP * m
                here = mixed[m * channels : (m + 1) * channels, p * n_cols : (p + 1) * n_cols]
                here = here + base[row_at + STEP].astype(f32)
                result[pl.ds(pl.multiple_of(row_at * channels, STEP), channels), :] = here

    def turn_tiles(at):
        for k in range(2):
            start = jnp.minimum(at * GROUP // TILE + k, n_rows // TILE - 1) * TILE
            start = pl.multiple_of(start, TILE)
            for o in range(channels):
                cells = result[pl.ds(start * channels + o, TILE, stride=channels), :]
                out[o, pl.ds(start, TILE), :] = cells.astype(bf16)

    pair_rows(0, GROUP)
    pair_rows(GROUP, TILE)

    def step(at, _):
        conv_rows(at)
        pair_rows(at * GROUP + AHEAD, GROUP)
        turn_tiles(at)
        return _

    lax.fori_loop(0, groups - 1, step, 0)
    conv_rows(groups - 1)
    turn_tiles(groups - 1)


def on_device(trunk, row_weight, column_weight, pair_map_weight, dilated_weight, mixing_weight):
    n_row, n_chip = lax.axis_size("row"), lax.axis_size("chip")
    shard, depth = trunk.shape
    n_rows, n_cols = shard * n_chip * 2, shard * n_row
    channels = pair_map_weight.shape[1]
    width = row_weight.shape[1]
    taps = jnp.transpose(dilated_weight, (2, 0, 1, 3)).reshape(channels, TAPS * TAPS * channels)
    reach = TAPS * channels
    depth_in = -(-WINDOWS * reach // MATRIX) * MATRIX
    conv = jnp.concatenate(
        [jnp.pad(taps, ((0, 0), (m * reach, depth_in - (m + TAPS) * reach))) for m in range(TAPS)],
        axis=0,
    )
    mix = jnp.kron(jnp.eye(TAPS, dtype=mixing_weight.dtype), mixing_weight)

    weights = jnp.concatenate([row_weight, column_weight, pair_map_weight.T], axis=0)

    copies = jnp.broadcast_to(trunk[None], (n_row * n_chip, shard, depth))
    mine = lax.all_to_all(copies, ("row", "chip"), 0, 0)
    other = lax.ppermute(mine, "core", [(0, 1), (1, 0)])
    groups = -(-n_rows // GROUP)
    padded = groups * GROUP + TILE
    return pl.pallas_call(
        functools.partial(kernel, n_row, n_chip),
        out_shape=jax.ShapeDtypeStruct((channels, n_rows, n_cols), jnp.bfloat16),
        scratch_shapes=[
            pltpu.VMEM((padded, width), jnp.float32),
            pltpu.VMEM((n_cols + TILE, width), jnp.bfloat16),
            pltpu.VMEM((width, 2 * n_cols), jnp.bfloat16),
            pltpu.VMEM((padded, TAPS * channels, n_cols), jnp.bfloat16),
            pltpu.VMEM((padded, channels, n_cols), jnp.bfloat16),
            pltpu.VMEM((groups * GROUP * channels, n_cols), jnp.float32),
        ],
        compiler_params=pltpu.CompilerParams(vmem_limit_bytes=52 * 2**20),
        name="pair_block",
    )(mine, other, weights, conv, mix)


def solution(mesh):
    n_row, n_col = mesh.devices.shape
    chips = Mesh(mesh.devices.reshape(n_row, n_col // 2, 2), ("row", "chip", "core"))
    return jax.shard_map(
        on_device,
        mesh=chips,
        in_specs=(P(("row", "chip", "core"), None), P(), P(), P(), P(), P()),
        out_specs=P(None, "row", ("chip", "core")),
        check_vma=False,
    )
```

```python
import functools

import jax
import jax.numpy as jnp
from jax import lax
from jax.experimental import pallas as pl
from jax.experimental.pallas import tpu as pltpu
from jax.sharding import Mesh
from jax.sharding import PartitionSpec as P

STEP = 8
TILE = 2 * STEP
TAPS = 3
WINDOWS = TAPS + 2
GROUP = TAPS * STEP
OUTSIDE = -1e30


def kernel(
    n_row,
    n_chip,
    mine,
    other,
    weights,
    out,
    conv_weight,
    mix_weight,
    row_proj,
    col_proj,
    base,
    sides,
    result,
    staged,
    sems,
):
    depth = mine.shape[2]
    row_weight = weights.at[pl.ds(0, depth)]
    col_weight = weights.at[pl.ds(depth, depth)]
    pair_weight = weights.at[pl.ds(2 * depth, out.shape[0])]
    f32, bf16 = jnp.float32, jnp.bfloat16
    row, chip, core = (lax.axis_index(name) for name in ("row", "chip", "core"))
    channels, n_rows, n_cols = out.shape
    shard = mine.shape[1]

    span = conv_weight.shape[1]

    def block(at):
        cells = weights[pl.ds(2 * depth + (1 + at) * channels, channels), :span]
        return cells.astype(f32)

    taps = [[block(a * TAPS + b) for b in range(TAPS)] for a in range(TAPS)]
    mixing = block(TAPS * TAPS)
    for m in range(TAPS):
        for b in range(TAPS):
            moved = [pltpu.roll(taps[a][b], (m + a) * channels, 1) for a in range(TAPS)]
            rows = pl.ds((b * TAPS + m) * channels, channels)
            conv_weight[rows, :] = (moved[0] + moved[1] + moved[2]).astype(bf16)
        moved = pltpu.roll(mixing, m * channels, 1) if m else mixing
        mix_weight[pl.ds(m * channels, channels), :] = moved.astype(bf16)

    tiles = n_cols // TILE + 1
    zero = jnp.zeros((), bf16)

    def projected(cells, weight):
        return jnp.dot(cells, weight[...], preferred_element_type=f32).astype(bf16).astype(f32)

    def last_bins(at, weight):
        tail = pl.ds(shard - TILE, TILE)
        at = jnp.maximum(at, 0)
        return projected(jnp.where(core == 1, mine[at, tail], other[at, tail]), weight)[STEP:]

    def first_bins(at, weight):
        head = pl.ds(0, TILE)
        at = jnp.minimum(at, n_row * n_chip - 1)
        return projected(jnp.where(core == 0, mine[at, head], other[at, head]), weight)[:STEP]

    first = chip * n_chip + core * (n_chip // 2)
    left = jnp.where((chip == 0) & (core == 0), OUTSIDE, last_bins(first - 1, col_weight))
    right = jnp.where(
        (chip == n_chip - 1) & (core == 1), OUTSIDE, first_bins(first + n_chip // 2, col_weight)
    )

    col_proj[n_cols:, :] = jnp.concatenate([right, left], axis=0).astype(bf16)
    for source, turn in ((mine, core), (other, 1 - core)):
        count = n_chip // 2
        cells = source[pl.ds(first, count)].reshape(count * shard, -1)
        cells = projected(cells, col_weight).astype(bf16)
        for k in range(count):
            at = pl.multiple_of((2 * k + turn) * shard, TILE)
            col_proj[pl.ds(at, shard), :] = cells[k * shard : (k + 1) * shard]

    first = row * n_chip
    row_proj[:STEP, :] = jnp.where(row == 0, OUTSIDE, last_bins(first - 1, row_weight))
    row_proj[STEP + n_rows : TILE + n_rows, :] = jnp.where(
        row == n_row - 1, OUTSIDE, first_bins(first + n_chip, row_weight)
    )
    spare = row_proj.shape[0] - TILE - n_rows
    row_proj[TILE + n_rows :, :] = jnp.full((spare, row_proj.shape[1]), OUTSIDE, f32)
    for source, turn in ((mine, core), (other, 1 - core)):
        cells = projected(source[pl.ds(first, n_chip)].reshape(n_chip * shard, -1), row_weight)
        for k in range(n_chip):
            at = STEP + (2 * k + turn) * shard
            row_proj[pl.ds(pl.multiple_of(at, STEP), shard), :] = cells[k * shard : (k + 1) * shard]

    width = row_proj.shape[1]

    lane = lax.broadcasted_iota(jnp.int32, (1, n_cols), 1)
    transposed = (((1,), (1,)), ((), ()))

    def pair_rows(start, count):
        rows = row_proj[pl.ds(pl.multiple_of(start, STEP), count), :]
        inner, outer = [], []
        for k in range(count):
            spread = jnp.broadcast_to(rows[k : k + 1], (TILE, width)).astype(bf16)
            cells = col_proj[...].reshape(tiles, TILE, width) + spread[None]
            act = jnp.maximum(cells, zero)
            inner.append(act[:-1].reshape(n_cols, width))
            outer.append(act[-1])
        act = jnp.concatenate(inner + outer, axis=0)
        hidden = lax.dot_general(pair_weight[...], act, transposed, preferred_element_type=f32)
        hidden = hidden.astype(bf16)
        for k in range(count):
            base[start + k] = hidden[:, k * n_cols : (k + 1) * n_cols]
        for k in range(count // STEP):
            at = (count + k) * n_cols
            sides[start // STEP + k] = hidden[:, at : at + n_cols]

    reach = TAPS * channels

    def conv_rows(at):
        first = at * GROUP
        fill = [jnp.zeros((span - WINDOWS * channels, n_cols), bf16)]
        cells = []
        for p in range(STEP):
            windows = [base[first + p + STEP * m] for m in range(WINDOWS)]
            cells.append(jnp.concatenate(windows + fill, axis=0))
        windows = [sides[at * TAPS + m] for m in range(WINDOWS)]
        cells.append(jnp.concatenate(windows + fill, axis=0))
        cells = jnp.maximum(jnp.concatenate(cells, axis=1), zero)
        parts = jnp.dot(conv_weight[...], cells, preferred_element_type=f32)
        ends = jnp.where(
            lane % TILE >= STEP, parts[:reach, STEP * n_cols :], parts[2 * reach :, STEP * n_cols :]
        )
        mids = []
        for p in range(STEP):
            here = parts[:, p * n_cols : (p + 1) * n_cols]
            end = pltpu.roll(ends, (n_cols - STEP - p * TILE) % n_cols, 1)
            left = jnp.where(lane < STEP, end, pltpu.roll(here[:reach], STEP, 1))
            right = pltpu.roll(here[2 * reach :], n_cols - STEP, 1)
            right = jnp.where(lane >= n_cols - STEP, end, right)
            total = here[reach : 2 * reach] + left + right
            mids.append(jnp.maximum(total, 0.0).astype(bf16))
        mixed = jnp.dot(
            mix_weight[:, :reach], jnp.concatenate(mids, axis=1), preferred_element_type=f32
        )
        for p in range(STEP):
            for m in range(TAPS):
                row_at = first + p + STEP * m
                here = mixed[m * channels : (m + 1) * channels, p * n_cols : (p + 1) * n_cols]
                here = here + base[row_at + STEP].astype(f32)
                result[pl.ds(pl.multiple_of(row_at * channels, STEP), channels), :] = here

    def finish(start, count, sem):
        start = pl.multiple_of(start, TILE)
        for o in range(channels):
            cells = result[pl.ds(start * channels + o, count, stride=channels), :]
            staged[o, pl.ds(start, count), :] = cells.astype(bf16)
        rows = pl.ds(start, count)
        return pltpu.make_async_copy(staged.at[:, rows], out.at[:, rows], sem)

    per_step = 2 * GROUP
    steps = n_rows // per_step - 1
    ahead = per_step + TILE
    for start in range(0, ahead, TILE):
        pair_rows(start, TILE)

    def step(at, _):
        conv_rows(2 * at)
        conv_rows(2 * at + 1)
        pair_rows(at * per_step + ahead, GROUP)
        pair_rows(at * per_step + ahead + GROUP, GROUP)
        finish(at * per_step, per_step, sems.at[at]).start()
        return _

    lax.fori_loop(0, steps, step, 0)
    groups = -(-n_rows // GROUP)
    for at in range(2 * steps, groups):
        start = 2 * steps * GROUP + ahead + (at - 2 * steps) * GROUP
        conv_rows(at)
        if start < row_proj.shape[0]:
            pair_rows(start, GROUP)
    last = finish(steps * per_step, n_rows - steps * per_step, sems.at[steps])
    last.start()
    for at in range(steps):
        rows = pl.ds(at * per_step, per_step)
        pltpu.make_async_copy(staged.at[:, rows], out.at[:, rows], sems.at[at]).wait()
    last.wait()


def on_device(trunk, row_weight, column_weight, pair_map_weight, dilated_weight, mixing_weight):
    n_row, n_chip = lax.axis_size("row"), lax.axis_size("chip")
    shard, depth = trunk.shape
    n_rows, n_cols = shard * n_chip * 2, shard * n_row
    channels = pair_map_weight.shape[1]
    width = row_weight.shape[1]
    small = jnp.concatenate([dilated_weight.reshape(-1, channels), mixing_weight], axis=0)
    small = jnp.pad(small, ((0, 0), (0, width - channels)))
    weights = jnp.concatenate([row_weight, column_weight, pair_map_weight.T, small], axis=0)

    copies = jnp.broadcast_to(trunk[None], (n_row * n_chip, shard, depth))
    mine = lax.all_to_all(copies, ("row", "chip"), 0, 0)
    other = lax.ppermute(mine, "core", [(0, 1), (1, 0)])
    span = -(-WINDOWS * channels // n_cols) * n_cols
    groups = -(-n_rows // GROUP)
    padded = groups * GROUP + TILE
    return pl.pallas_call(
        functools.partial(kernel, n_row, n_chip),
        out_shape=jax.ShapeDtypeStruct((channels, n_rows, n_cols), jnp.bfloat16),
        out_specs=pl.BlockSpec(memory_space=pl.ANY),
        scratch_shapes=[
            pltpu.VMEM((TAPS * TAPS * channels, span), jnp.bfloat16),
            pltpu.VMEM((TAPS * channels, span), jnp.bfloat16),
            pltpu.VMEM((padded, width), jnp.float32),
            pltpu.VMEM((n_cols + TILE, width), jnp.bfloat16),
            pltpu.VMEM((padded, channels, n_cols), jnp.bfloat16),
            pltpu.VMEM((padded // STEP, channels, n_cols), jnp.bfloat16),
            pltpu.VMEM((groups * GROUP * channels, n_cols), jnp.float32),
            pltpu.VMEM((channels, n_rows, n_cols), jnp.bfloat16),
            pltpu.SemaphoreType.DMA((n_rows // (2 * GROUP),)),
        ],
        compiler_params=pltpu.CompilerParams(vmem_limit_bytes=52 * 2**20),
        name="pair_block",
    )(mine, other, weights)


def solution(mesh):
    n_row, n_col = mesh.devices.shape
    chips = Mesh(mesh.devices.reshape(n_row, n_col // 2, 2), ("row", "chip", "core"))
    return jax.shard_map(
        on_device,
        mesh=chips,
        in_specs=(P(("row", "chip", "core"), None), P(), P(), P(), P(), P()),
        out_specs=P(None, "row", ("chip", "core")),
        check_vma=False,
    )
```

```python
import functools

import jax
import jax.numpy as jnp
from jax import lax
from jax.experimental import pallas as pl
from jax.experimental.pallas import tpu as pltpu
from jax.sharding import Mesh
from jax.sharding import PartitionSpec as P

STEP = 8
TILE = 2 * STEP
TAPS = 3
WINDOWS = TAPS + 2
GROUP = TAPS * STEP


def kernel(
    n_row,
    n_chip,
    mine,
    other,
    weights,
    out,
    conv_weight,
    mix_weight,
    row_proj,
    col_proj,
    base,
    sides,
    result,
    staged,
    sems,
):
    depth = mine.shape[2]
    row_weight = weights.at[pl.ds(0, depth)]
    col_weight = weights.at[pl.ds(depth, depth)]
    pair_weight = weights.at[pl.ds(2 * depth, out.shape[0])]
    f32, bf16 = jnp.float32, jnp.bfloat16
    row, chip, core = (lax.axis_index(name) for name in ("row", "chip", "core"))
    channels, n_rows, n_cols = out.shape
    shard = mine.shape[1]

    span = conv_weight.shape[1]

    def block(at):
        cells = weights[pl.ds(2 * depth + (1 + at) * channels, channels), :span]
        return cells.astype(f32)

    taps = [[block(a * TAPS + b) for b in range(TAPS)] for a in range(TAPS)]
    mixing = block(TAPS * TAPS)
    for m in range(TAPS):
        for b in range(TAPS):
            moved = [pltpu.roll(taps[a][b], (m + a) * channels, 1) for a in range(TAPS)]
            rows = pl.ds((b * TAPS + m) * channels, channels)
            conv_weight[rows, :] = (moved[0] + moved[1] + moved[2]).astype(bf16)
        moved = pltpu.roll(mixing, m * channels, 1) if m else mixing
        mix_weight[pl.ds(m * channels, channels), :] = moved.astype(bf16)

    tiles = n_cols // TILE + 1
    zero = jnp.zeros((), bf16)

    def projected(cells, weight):
        return jnp.dot(cells, weight[...], preferred_element_type=f32).astype(bf16).astype(f32)

    def last_bins(at, weight):
        tail = pl.ds(shard - TILE, TILE)
        at = jnp.maximum(at, 0)
        return projected(jnp.where(core == 1, mine[at, tail], other[at, tail]), weight)[STEP:]

    def first_bins(at, weight):
        head = pl.ds(0, TILE)
        at = jnp.minimum(at, n_row * n_chip - 1)
        return projected(jnp.where(core == 0, mine[at, head], other[at, head]), weight)[:STEP]

    first = chip * n_chip + core * (n_chip // 2)
    left = last_bins(first - 1, col_weight)
    right = first_bins(first + n_chip // 2, col_weight)

    col_proj[n_cols:, :] = -jnp.concatenate([right, left], axis=0).astype(bf16)
    for source, turn in ((mine, core), (other, 1 - core)):
        count = n_chip // 2
        cells = source[pl.ds(first, count)].reshape(count * shard, -1)
        cells = projected(cells, col_weight).astype(bf16)
        for k in range(count):
            at = pl.multiple_of((2 * k + turn) * shard, TILE)
            col_proj[pl.ds(at, shard), :] = -cells[k * shard : (k + 1) * shard]

    first = row * n_chip
    row_proj[:STEP, :] = last_bins(first - 1, row_weight)
    row_proj[STEP + n_rows : TILE + n_rows, :] = first_bins(first + n_chip, row_weight)
    row_proj[TILE + n_rows :, :] = jnp.zeros_like(row_proj[TILE + n_rows :, :])
    for source, turn in ((mine, core), (other, 1 - core)):
        cells = projected(source[pl.ds(first, n_chip)].reshape(n_chip * shard, -1), row_weight)
        for k in range(n_chip):
            at = STEP + (2 * k + turn) * shard
            row_proj[pl.ds(pl.multiple_of(at, STEP), shard), :] = cells[k * shard : (k + 1) * shard]

    width = row_proj.shape[1]

    lane = lax.broadcasted_iota(jnp.int32, (1, n_cols), 1)
    transposed = (((1,), (1,)), ((), ()))

    outer = jnp.concatenate([col_proj[n_cols:, :]] * (n_cols // TILE), axis=0)
    shift_in, shift_out = (
        -lax.dot_general(pair_weight[...], cells, transposed, preferred_element_type=f32)
        for cells in (col_proj[:n_cols, :], outer)
    )
    off_map = (lane % TILE >= STEP) & (chip == 0) & (core == 0)
    off_map |= (lane % TILE < STEP) & (chip == n_chip - 1) & (core == 1)

    def pair_rows(start, count):
        rows = row_proj[pl.ds(pl.multiple_of(start, STEP), count), :]
        inner, outer = [], []
        for k in range(count):
            spread = jnp.broadcast_to(rows[k : k + 1], (TILE, width)).astype(bf16)
            act = jnp.maximum(col_proj[...].reshape(tiles, TILE, width), spread[None])
            inner.append(act[:-1].reshape(n_cols, width))
            outer.append(act[-1])
        act = jnp.concatenate(inner + outer, axis=0)
        hidden = lax.dot_general(pair_weight[...], act, transposed, preferred_element_type=f32)
        for k in range(count):
            base[start + k] = (hidden[:, k * n_cols : (k + 1) * n_cols] + shift_in).astype(bf16)
        for k in range(count // STEP):
            at = (count + k) * n_cols
            cells = jnp.where(off_map, 0.0, hidden[:, at : at + n_cols] + shift_out)
            sides[start // STEP + k] = cells.astype(bf16)

    def clear(off, start):
        rows = pl.ds(start, STEP)
        base[rows] = jnp.where(off, zero, base[rows])
        sides[start // STEP] = jnp.where(off, zero, sides[start // STEP])

    reach = TAPS * channels

    def conv_rows(at):
        first = at * GROUP
        fill = [jnp.zeros((span - WINDOWS * channels, n_cols), bf16)]
        cells = []
        for p in range(STEP):
            windows = [base[first + p + STEP * m] for m in range(WINDOWS)]
            cells.append(jnp.concatenate(windows + fill, axis=0))
        windows = [sides[at * TAPS + m] for m in range(WINDOWS)]
        cells.append(jnp.concatenate(windows + fill, axis=0))
        cells = jnp.maximum(jnp.concatenate(cells, axis=1), zero)
        parts = jnp.dot(conv_weight[...], cells, preferred_element_type=f32)
        ends = jnp.where(
            lane % TILE >= STEP, parts[:reach, STEP * n_cols :], parts[2 * reach :, STEP * n_cols :]
        )
        mids = []
        for p in range(STEP):
            here = parts[:, p * n_cols : (p + 1) * n_cols]
            end = pltpu.roll(ends, (n_cols - STEP - p * TILE) % n_cols, 1)
            left = jnp.where(lane < STEP, end, pltpu.roll(here[:reach], STEP, 1))
            right = pltpu.roll(here[2 * reach :], n_cols - STEP, 1)
            right = jnp.where(lane >= n_cols - STEP, end, right)
            total = here[reach : 2 * reach] + left + right
            mids.append(jnp.maximum(total, 0.0).astype(bf16))
        mixed = jnp.dot(
            mix_weight[:, :reach], jnp.concatenate(mids, axis=1), preferred_element_type=f32
        )
        for p in range(STEP):
            for m in range(TAPS):
                row_at = first + p + STEP * m
                here = mixed[m * channels : (m + 1) * channels, p * n_cols : (p + 1) * n_cols]
                here = here + base[row_at + STEP].astype(f32)
                result[pl.ds(pl.multiple_of(row_at * channels, STEP), channels), :] = here

    def finish(start, count, sem):
        start = pl.multiple_of(start, TILE)
        for o in range(channels):
            cells = result[pl.ds(start * channels + o, count, stride=channels), :]
            staged[o, pl.ds(start, count), :] = cells.astype(bf16)
        rows = pl.ds(start, count)
        return pltpu.make_async_copy(staged.at[:, rows], out.at[:, rows], sem)

    per_step = 2 * GROUP
    steps = n_rows // per_step - 1
    ahead = per_step + TILE
    for start in range(0, ahead, TILE):
        pair_rows(start, TILE)
    clear(row == 0, 0)

    def step(at, _):
        conv_rows(2 * at)
        conv_rows(2 * at + 1)
        pair_rows(at * per_step + ahead, GROUP)
        pair_rows(at * per_step + ahead + GROUP, GROUP)
        finish(at * per_step, per_step, sems.at[at]).start()
        return _

    lax.fori_loop(0, steps, step, 0)
    groups = -(-n_rows // GROUP)
    for at in range(2 * steps, groups):
        start = 2 * steps * GROUP + ahead + (at - 2 * steps) * GROUP
        conv_rows(at)
        if start < row_proj.shape[0]:
            pair_rows(start, GROUP)
            clear(row == n_row - 1, n_rows + STEP)
    last = finish(steps * per_step, n_rows - steps * per_step, sems.at[steps])
    last.start()
    for at in range(steps):
        rows = pl.ds(at * per_step, per_step)
        pltpu.make_async_copy(staged.at[:, rows], out.at[:, rows], sems.at[at]).wait()
    last.wait()


def on_device(trunk, row_weight, column_weight, pair_map_weight, dilated_weight, mixing_weight):
    n_row, n_chip = lax.axis_size("row"), lax.axis_size("chip")
    shard, depth = trunk.shape
    n_rows, n_cols = shard * n_chip * 2, shard * n_row
    channels = pair_map_weight.shape[1]
    width = row_weight.shape[1]
    small = jnp.concatenate([dilated_weight.reshape(-1, channels), mixing_weight], axis=0)
    small = jnp.pad(small, ((0, 0), (0, width - channels)))
    weights = jnp.concatenate([row_weight, column_weight, pair_map_weight.T, small], axis=0)

    copies = jnp.broadcast_to(trunk[None], (n_row * n_chip, shard, depth))
    mine = lax.all_to_all(copies, ("row", "chip"), 0, 0)
    other = lax.ppermute(mine, "core", [(0, 1), (1, 0)])
    span = -(-WINDOWS * channels // n_cols) * n_cols
    groups = -(-n_rows // GROUP)
    padded = groups * GROUP + TILE
    return pl.pallas_call(
        functools.partial(kernel, n_row, n_chip),
        out_shape=jax.ShapeDtypeStruct((channels, n_rows, n_cols), jnp.bfloat16),
        out_specs=pl.BlockSpec(memory_space=pl.ANY),
        scratch_shapes=[
            pltpu.VMEM((TAPS * TAPS * channels, span), jnp.bfloat16),
            pltpu.VMEM((TAPS * channels, span), jnp.bfloat16),
            pltpu.VMEM((padded, width), jnp.float32),
            pltpu.VMEM((n_cols + TILE, width), jnp.bfloat16),
            pltpu.VMEM((padded, channels, n_cols), jnp.bfloat16),
            pltpu.VMEM((padded // STEP, channels, n_cols), jnp.bfloat16),
            pltpu.VMEM((groups * GROUP * channels, n_cols), jnp.float32),
            pltpu.VMEM((channels, n_rows, n_cols), jnp.bfloat16),
            pltpu.SemaphoreType.DMA((n_rows // (2 * GROUP),)),
        ],
        compiler_params=pltpu.CompilerParams(vmem_limit_bytes=52 * 2**20),
        name="pair_block",
    )(mine, other, weights)


def solution(mesh):
    n_row, n_col = mesh.devices.shape
    chips = Mesh(mesh.devices.reshape(n_row, n_col // 2, 2), ("row", "chip", "core"))
    return jax.shard_map(
        on_device,
        mesh=chips,
        in_specs=(P(("row", "chip", "core"), None), P(), P(), P(), P(), P()),
        out_specs=P(None, "row", ("chip", "core")),
        check_vma=False,
    )
```

```python
import functools

import jax
import jax.numpy as jnp
from jax import lax
from jax.experimental import pallas as pl
from jax.experimental.pallas import tpu as pltpu
from jax.sharding import Mesh
from jax.sharding import PartitionSpec as P

STEP = 8
TILE = 2 * STEP
TAPS = 3
WINDOWS = TAPS + 2
GROUP = TAPS * STEP
OUTSIDE = -1e30


def kernel(
    n_row,
    n_chip,
    mine,
    other,
    weights,
    out,
    conv_weight,
    mix_weight,
    row_proj,
    col_proj,
    base,
    sides,
    result,
    staged,
    sems,
):
    depth = mine.shape[2]
    row_weight = weights.at[pl.ds(0, depth)]
    col_weight = weights.at[pl.ds(depth, depth)]
    pair_weight = weights.at[pl.ds(2 * depth, out.shape[0])]
    f32, bf16 = jnp.float32, jnp.bfloat16
    row, chip, core = (lax.axis_index(name) for name in ("row", "chip", "core"))
    channels, n_rows, n_cols = out.shape
    shard = mine.shape[1]

    span = conv_weight.shape[1]

    def block(at):
        cells = weights[pl.ds(2 * depth + (1 + at) * channels, channels), :span]
        return cells.astype(f32)

    taps = [[block(a * TAPS + b) for b in range(TAPS)] for a in range(TAPS)]
    mixing = block(TAPS * TAPS)
    for m in range(TAPS):
        for b in range(TAPS):
            moved = [pltpu.roll(taps[a][b], (m + a) * channels, 1) for a in range(TAPS)]
            rows = pl.ds((b * TAPS + m) * channels, channels)
            conv_weight[rows, :] = (moved[0] + moved[1] + moved[2]).astype(bf16)
        moved = pltpu.roll(mixing, m * channels, 1) if m else mixing
        mix_weight[pl.ds(m * channels, channels), :] = moved.astype(bf16)

    tiles = n_cols // TILE + 1
    zero = jnp.zeros((), bf16)

    def projected(cells, weight):
        return jnp.dot(cells, weight[...], preferred_element_type=f32).astype(bf16).astype(f32)

    def last_bins(at, weight):
        tail = pl.ds(shard - TILE, TILE)
        at = jnp.maximum(at, 0)
        return projected(jnp.where(core == 1, mine[at, tail], other[at, tail]), weight)[STEP:]

    def first_bins(at, weight):
        head = pl.ds(0, TILE)
        at = jnp.minimum(at, n_row * n_chip - 1)
        return projected(jnp.where(core == 0, mine[at, head], other[at, head]), weight)[:STEP]

    first = chip * n_chip + core * (n_chip // 2)
    left = jnp.where((chip == 0) & (core == 0), OUTSIDE, last_bins(first - 1, col_weight))
    right = jnp.where(
        (chip == n_chip - 1) & (core == 1), OUTSIDE, first_bins(first + n_chip // 2, col_weight)
    )

    col_proj[n_cols:, :] = jnp.concatenate([right, left], axis=0).astype(bf16)
    for source, turn in ((mine, core), (other, 1 - core)):
        count = n_chip // 2
        cells = source[pl.ds(first, count)].reshape(count * shard, -1)
        cells = projected(cells, col_weight).astype(bf16)
        for k in range(count):
            at = pl.multiple_of((2 * k + turn) * shard, TILE)
            col_proj[pl.ds(at, shard), :] = cells[k * shard : (k + 1) * shard]

    first = row * n_chip
    row_proj[:STEP, :] = jnp.where(row == 0, OUTSIDE, last_bins(first - 1, row_weight))
    row_proj[STEP + n_rows : TILE + n_rows, :] = jnp.where(
        row == n_row - 1, OUTSIDE, first_bins(first + n_chip, row_weight)
    )
    for source, turn in ((mine, core), (other, 1 - core)):
        cells = projected(source[pl.ds(first, n_chip)].reshape(n_chip * shard, -1), row_weight)
        for k in range(n_chip):
            at = STEP + (2 * k + turn) * shard
            row_proj[pl.ds(pl.multiple_of(at, STEP), shard), :] = cells[k * shard : (k + 1) * shard]

    width = row_proj.shape[1]

    lane = lax.broadcasted_iota(jnp.int32, (1, n_cols), 1)
    transposed = (((1,), (1,)), ((), ()))

    def pair_rows(start, count):
        rows = row_proj[pl.ds(pl.multiple_of(start, STEP), count), :]
        inner, outer = [], []
        for k in range(count):
            spread = jnp.broadcast_to(rows[k : k + 1], (TILE, width)).astype(bf16)
            cells = col_proj[...].reshape(tiles, TILE, width) + spread[None]
            act = jnp.maximum(cells, zero)
            inner.append(act[:-1].reshape(n_cols, width))
            outer.append(act[-1])
        act = jnp.concatenate(inner + outer, axis=0)
        hidden = lax.dot_general(pair_weight[...], act, transposed, preferred_element_type=f32)
        hidden = hidden.astype(bf16)
        for k in range(count):
            base[start + k] = hidden[:, k * n_cols : (k + 1) * n_cols]
        for k in range(count // STEP):
            at = (count + k) * n_cols
            sides[start // STEP + k] = hidden[:, at : at + n_cols]

    reach = TAPS * channels

    def conv_rows(at):
        first = at * GROUP
        fill = [jnp.zeros((span - WINDOWS * channels, n_cols), bf16)]
        cells = []
        for p in range(STEP):
            windows = [base[first + p + STEP * m] for m in range(WINDOWS)]
            cells.append(jnp.concatenate(windows + fill, axis=0))
        windows = [sides[at * TAPS + m] for m in range(WINDOWS)]
        cells.append(jnp.concatenate(windows + fill, axis=0))
        cells = jnp.maximum(jnp.concatenate(cells, axis=1), zero)
        parts = jnp.dot(conv_weight[...], cells, preferred_element_type=f32)
        ends = jnp.where(
            lane % TILE >= STEP, parts[:reach, STEP * n_cols :], parts[2 * reach :, STEP * n_cols :]
        )
        mids = []
        for p in range(STEP):
            here = parts[:, p * n_cols : (p + 1) * n_cols]
            end = pltpu.roll(ends, (n_cols - STEP - p * TILE) % n_cols, 1)
            left = jnp.where(lane < STEP, end, pltpu.roll(here[:reach], STEP, 1))
            right = pltpu.roll(here[2 * reach :], n_cols - STEP, 1)
            right = jnp.where(lane >= n_cols - STEP, end, right)
            total = here[reach : 2 * reach] + left + right
            mids.append(jnp.maximum(total, 0.0).astype(bf16))
        mixed = jnp.dot(
            mix_weight[:, :reach], jnp.concatenate(mids, axis=1), preferred_element_type=f32
        )
        for p in range(STEP):
            for m in range(TAPS):
                row_at = first + p + STEP * m
                here = mixed[m * channels : (m + 1) * channels, p * n_cols : (p + 1) * n_cols]
                here = here + base[row_at + STEP].astype(f32)
                result[pl.ds(pl.multiple_of(row_at * channels, STEP), channels), :] = here

    def finish(start, count, sem):
        start = pl.multiple_of(start, TILE)
        for o in range(channels):
            cells = result[pl.ds(start * channels + o, count, stride=channels), :]
            staged[o, pl.ds(start, count), :] = cells.astype(bf16)
        rows = pl.ds(start, count)
        return pltpu.make_async_copy(staged.at[:, rows], out.at[:, rows], sem)

    def pair_step(at, _):
        pair_rows(at * TILE, TILE)
        return _

    lax.fori_loop(0, (n_rows + TILE) // TILE, pair_step, 0)
    spare = pl.ds(n_rows + TILE, STEP)
    base[spare] = jnp.zeros_like(base[spare])
    sides[(n_rows + TILE) // STEP] = jnp.zeros_like(sides[0])

    per_step = 2 * GROUP
    steps = n_rows // per_step

    def step(at, _):
        conv_rows(2 * at)
        conv_rows(2 * at + 1)
        finish(at * per_step, per_step, sems.at[at]).start()
        return _

    lax.fori_loop(0, steps, step, 0)
    conv_rows(2 * steps)
    last = finish(steps * per_step, n_rows - steps * per_step, sems.at[steps])
    last.start()
    for at in range(steps):
        rows = pl.ds(at * per_step, per_step)
        pltpu.make_async_copy(staged.at[:, rows], out.at[:, rows], sems.at[at]).wait()
    last.wait()


def on_device(trunk, row_weight, column_weight, pair_map_weight, dilated_weight, mixing_weight):
    n_row, n_chip = lax.axis_size("row"), lax.axis_size("chip")
    shard, depth = trunk.shape
    n_rows, n_cols = shard * n_chip * 2, shard * n_row
    channels = pair_map_weight.shape[1]
    width = row_weight.shape[1]
    small = jnp.concatenate([dilated_weight.reshape(-1, channels), mixing_weight], axis=0)
    small = jnp.pad(small, ((0, 0), (0, width - channels)))
    weights = jnp.concatenate([row_weight, column_weight, pair_map_weight.T, small], axis=0)

    copies = jnp.broadcast_to(trunk[None], (n_row * n_chip, shard, depth))
    mine = lax.all_to_all(copies, ("row", "chip"), 0, 0)
    other = lax.ppermute(mine, "core", [(0, 1), (1, 0)])
    span = -(-WINDOWS * channels // n_cols) * n_cols
    groups = -(-n_rows // GROUP)
    padded = groups * GROUP + TILE
    return pl.pallas_call(
        functools.partial(kernel, n_row, n_chip),
        out_shape=jax.ShapeDtypeStruct((channels, n_rows, n_cols), jnp.bfloat16),
        out_specs=pl.BlockSpec(memory_space=pl.ANY),
        scratch_shapes=[
            pltpu.VMEM((TAPS * TAPS * channels, span), jnp.bfloat16),
            pltpu.VMEM((TAPS * channels, span), jnp.bfloat16),
            pltpu.VMEM((n_rows + TILE, width), jnp.float32),
            pltpu.VMEM((n_cols + TILE, width), jnp.bfloat16),
            pltpu.VMEM((padded, channels, n_cols), jnp.bfloat16),
            pltpu.VMEM((padded // STEP, channels, n_cols), jnp.bfloat16),
            pltpu.VMEM((groups * GROUP * channels, n_cols), jnp.float32),
            pltpu.VMEM((channels, n_rows, n_cols), jnp.bfloat16),
            pltpu.SemaphoreType.DMA((n_rows // (2 * GROUP) + 1,)),
        ],
        compiler_params=pltpu.CompilerParams(vmem_limit_bytes=52 * 2**20),
        name="pair_block",
    )(mine, other, weights)


def solution(mesh):
    n_row, n_col = mesh.devices.shape
    chips = Mesh(mesh.devices.reshape(n_row, n_col // 2, 2), ("row", "chip", "core"))
    return jax.shard_map(
        on_device,
        mesh=chips,
        in_specs=(P(("row", "chip", "core"), None), P(), P(), P(), P(), P()),
        out_specs=P(None, "row", ("chip", "core")),
        check_vma=False,
    )
```

```python
import functools

import jax
import jax.numpy as jnp
from jax import lax
from jax.experimental import pallas as pl
from jax.experimental.pallas import tpu as pltpu
from jax.sharding import Mesh
from jax.sharding import PartitionSpec as P

STEP = 8
TILE = 2 * STEP
TAPS = 3
WINDOWS = TAPS + 2
GROUP = TAPS * STEP
OUTSIDE = -1e30


def kernel(
    n_row,
    n_chip,
    mine,
    other,
    weights,
    out,
    conv_weight,
    mix_weight,
    row_proj,
    col_proj,
    base,
    sides,
    result,
    staged,
    sems,
):
    depth = mine.shape[2]
    row_weight = weights.at[pl.ds(0, depth)]
    col_weight = weights.at[pl.ds(depth, depth)]
    pair_weight = weights.at[pl.ds(2 * depth, out.shape[0])]
    f32, bf16 = jnp.float32, jnp.bfloat16
    row, chip, core = (lax.axis_index(name) for name in ("row", "chip", "core"))
    channels, n_rows, n_cols = out.shape
    shard = mine.shape[1]

    span = conv_weight.shape[1]

    def block(at):
        cells = weights[pl.ds(2 * depth + (1 + at) * channels, channels), :span]
        return cells.astype(f32)

    taps = [[block(a * TAPS + b) for b in range(TAPS)] for a in range(TAPS)]
    mixing = block(TAPS * TAPS)
    for m in range(TAPS):
        for b in range(TAPS):
            moved = [pltpu.roll(taps[a][b], (m + a) * channels, 1) for a in range(TAPS)]
            rows = pl.ds((b * TAPS + m) * channels, channels)
            conv_weight[rows, :] = (moved[0] + moved[1] + moved[2]).astype(bf16)
        moved = pltpu.roll(mixing, m * channels, 1) if m else mixing
        mix_weight[pl.ds(m * channels, channels), :] = moved.astype(bf16)

    tiles = n_cols // TILE + 1
    zero = jnp.zeros((), bf16)

    def projected(cells, weight):
        return jnp.dot(cells, weight[...], preferred_element_type=f32).astype(bf16).astype(f32)

    def last_bins(at, weight):
        tail = pl.ds(shard - TILE, TILE)
        at = jnp.maximum(at, 0)
        return projected(jnp.where(core == 1, mine[at, tail], other[at, tail]), weight)[STEP:]

    def first_bins(at, weight):
        head = pl.ds(0, TILE)
        at = jnp.minimum(at, n_row * n_chip - 1)
        return projected(jnp.where(core == 0, mine[at, head], other[at, head]), weight)[:STEP]

    first = chip * n_chip + core * (n_chip // 2)
    left = jnp.where((chip == 0) & (core == 0), OUTSIDE, last_bins(first - 1, col_weight))
    right = jnp.where(
        (chip == n_chip - 1) & (core == 1), OUTSIDE, first_bins(first + n_chip // 2, col_weight)
    )

    col_proj[n_cols:, :] = jnp.concatenate([right, left], axis=0).astype(bf16)
    for source, turn in ((mine, core), (other, 1 - core)):
        count = n_chip // 2
        cells = source[pl.ds(first, count)].reshape(count * shard, -1)
        cells = projected(cells, col_weight).astype(bf16)
        for k in range(count):
            at = pl.multiple_of((2 * k + turn) * shard, TILE)
            col_proj[pl.ds(at, shard), :] = cells[k * shard : (k + 1) * shard]

    first = row * n_chip
    row_proj[:STEP, :] = jnp.where(row == 0, OUTSIDE, last_bins(first - 1, row_weight))
    row_proj[STEP + n_rows : TILE + n_rows, :] = jnp.where(
        row == n_row - 1, OUTSIDE, first_bins(first + n_chip, row_weight)
    )
    spare = row_proj.shape[0] - TILE - n_rows
    row_proj[TILE + n_rows :, :] = jnp.full((spare, row_proj.shape[1]), OUTSIDE, f32)
    for source, turn in ((mine, core), (other, 1 - core)):
        cells = projected(source[pl.ds(first, n_chip)].reshape(n_chip * shard, -1), row_weight)
        for k in range(n_chip):
            at = STEP + (2 * k + turn) * shard
            row_proj[pl.ds(pl.multiple_of(at, STEP), shard), :] = cells[k * shard : (k + 1) * shard]

    width = row_proj.shape[1]

    lane = lax.broadcasted_iota(jnp.int32, (1, n_cols), 1)
    transposed = (((1,), (1,)), ((), ()))

    def pair_cells(acts):
        act = jnp.concatenate(acts, axis=0)
        hidden = lax.dot_general(pair_weight[...], act, transposed, preferred_element_type=f32)
        return hidden.astype(bf16)

    def pair_rows(start, count):
        rows = row_proj[pl.ds(pl.multiple_of(start, STEP), count), :]
        inner, outer = [], []
        for k in range(count):
            spread = jnp.broadcast_to(rows[k : k + 1], (TILE, width)).astype(bf16)
            cells = col_proj[:n_cols, :].reshape(tiles - 1, TILE, width) + spread[None]
            inner.append(jnp.maximum(cells, zero).reshape(n_cols, width))
            outer.append(jnp.maximum(col_proj[n_cols:, :] + spread, zero))
            if k % 2:
                hidden = pair_cells(inner)
                base[start + k - 1] = hidden[:, :n_cols]
                base[start + k] = hidden[:, n_cols:]
                inner = []
            if k % STEP == STEP - 1:
                sides[(start + k) // STEP] = pair_cells(outer)
                outer = []

    reach = TAPS * channels

    def conv_rows(at):
        first = at * GROUP
        fill = [jnp.zeros((span - WINDOWS * channels, n_cols), bf16)]

        def parts_of(blocks):
            cells = [
                jnp.concatenate([block(m) for m in range(WINDOWS)] + fill, axis=0)
                for block in blocks
            ]
            cells = jnp.maximum(jnp.concatenate(cells, axis=1), zero)
            return jnp.dot(conv_weight[...], cells, preferred_element_type=f32)

        parts = parts_of([lambda m: sides[at * TAPS + m]])
        ends = jnp.where(lane % TILE >= STEP, parts[:reach], parts[2 * reach :])
        for q in range(0, STEP, 2):
            parts = parts_of(
                [lambda m, p=p: base[first + p + STEP * m] for p in (q, q + 1)]
            )
            mids = []
            for p in (q, q + 1):
                here = parts[:, (p - q) * n_cols : (p - q + 1) * n_cols]
                end = pltpu.roll(ends, (n_cols - STEP - p * TILE) % n_cols, 1)
                left = jnp.where(lane < STEP, end, pltpu.roll(here[:reach], STEP, 1))
                right = pltpu.roll(here[2 * reach :], n_cols - STEP, 1)
                right = jnp.where(lane >= n_cols - STEP, end, right)
                total = here[reach : 2 * reach] + left + right
                mids.append(jnp.maximum(total, 0.0).astype(bf16))
            mixed = jnp.dot(
                mix_weight[:, :reach], jnp.concatenate(mids, axis=1), preferred_element_type=f32
            )
            for p in (q, q + 1):
                for m in range(TAPS):
                    row_at = first + p + STEP * m
                    here = mixed[m * channels : (m + 1) * channels]
                    here = here[:, (p - q) * n_cols : (p - q + 1) * n_cols]
                    here = here + base[row_at + STEP].astype(f32)
                    result[pl.ds(pl.multiple_of(row_at * channels, STEP), channels), :] = here

    def finish(start, count, sem):
        start = pl.multiple_of(start, TILE)
        for o in range(channels):
            cells = result[pl.ds(start * channels + o, count, stride=channels), :]
            staged[o, pl.ds(start, count), :] = cells.astype(bf16)
        rows = pl.ds(start, count)
        return pltpu.make_async_copy(staged.at[:, rows], out.at[:, rows], sem)

    per_step = 2 * GROUP
    steps = n_rows // per_step - 1
    ahead = per_step + TILE
    for start in range(0, ahead, TILE):
        pair_rows(start, TILE)

    def step(at, _):
        conv_rows(2 * at)
        conv_rows(2 * at + 1)
        pair_rows(at * per_step + ahead, GROUP)
        pair_rows(at * per_step + ahead + GROUP, GROUP)
        finish(at * per_step, per_step, sems.at[at]).start()
        return _

    lax.fori_loop(0, steps, step, 0)
    groups = -(-n_rows // GROUP)
    for at in range(2 * steps, groups):
        start = 2 * steps * GROUP + ahead + (at - 2 * steps) * GROUP
        conv_rows(at)
        if start < row_proj.shape[0]:
            pair_rows(start, GROUP)
    last = finish(steps * per_step, n_rows - steps * per_step, sems.at[steps])
    last.start()
    for at in range(steps):
        rows = pl.ds(at * per_step, per_step)
        pltpu.make_async_copy(staged.at[:, rows], out.at[:, rows], sems.at[at]).wait()
    last.wait()


def on_device(trunk, row_weight, column_weight, pair_map_weight, dilated_weight, mixing_weight):
    n_row, n_chip = lax.axis_size("row"), lax.axis_size("chip")
    shard, depth = trunk.shape
    n_rows, n_cols = shard * n_chip * 2, shard * n_row
    channels = pair_map_weight.shape[1]
    width = row_weight.shape[1]
    small = jnp.concatenate([dilated_weight.reshape(-1, channels), mixing_weight], axis=0)
    small = jnp.pad(small, ((0, 0), (0, width - channels)))
    weights = jnp.concatenate([row_weight, column_weight, pair_map_weight.T, small], axis=0)

    copies = jnp.broadcast_to(trunk[None], (n_row * n_chip, shard, depth))
    mine = lax.all_to_all(copies, ("row", "chip"), 0, 0)
    other = lax.ppermute(mine, "core", [(0, 1), (1, 0)])
    span = -(-WINDOWS * channels // n_cols) * n_cols
    groups = -(-n_rows // GROUP)
    padded = groups * GROUP + TILE
    return pl.pallas_call(
        functools.partial(kernel, n_row, n_chip),
        out_shape=jax.ShapeDtypeStruct((channels, n_rows, n_cols), jnp.bfloat16),
        out_specs=pl.BlockSpec(memory_space=pl.ANY),
        scratch_shapes=[
            pltpu.VMEM((TAPS * TAPS * channels, span), jnp.bfloat16),
            pltpu.VMEM((TAPS * channels, span), jnp.bfloat16),
            pltpu.VMEM((padded, width), jnp.float32),
            pltpu.VMEM((n_cols + TILE, width), jnp.bfloat16),
            pltpu.VMEM((padded, channels, n_cols), jnp.bfloat16),
            pltpu.VMEM((padded // STEP, channels, n_cols), jnp.bfloat16),
            pltpu.VMEM((groups * GROUP * channels, n_cols), jnp.float32),
            pltpu.VMEM((channels, n_rows, n_cols), jnp.bfloat16),
            pltpu.SemaphoreType.DMA((n_rows // (2 * GROUP),)),
        ],
        compiler_params=pltpu.CompilerParams(vmem_limit_bytes=52 * 2**20),
        name="pair_block",
    )(mine, other, weights)


def solution(mesh):
    n_row, n_col = mesh.devices.shape
    chips = Mesh(mesh.devices.reshape(n_row, n_col // 2, 2), ("row", "chip", "core"))
    return jax.shard_map(
        on_device,
        mesh=chips,
        in_specs=(P(("row", "chip", "core"), None), P(), P(), P(), P(), P()),
        out_specs=P(None, "row", ("chip", "core")),
        check_vma=False,
    )
```

```python
import functools

import jax
import jax.numpy as jnp
from jax import lax
from jax.experimental import pallas as pl
from jax.experimental.pallas import tpu as pltpu
from jax.sharding import Mesh
from jax.sharding import PartitionSpec as P

STEP = 8
TILE = 2 * STEP
TAPS = 3
WINDOWS = TAPS + 2
GROUP = TAPS * STEP
OUTSIDE = -1e30


def kernel(
    n_row,
    n_chip,
    mine,
    other,
    weights,
    out,
    conv_weight,
    mix_weight,
    row_proj,
    col_proj,
    base,
    sides,
    result,
    staged,
    sems,
):
    depth = mine.shape[2]
    row_weight = weights.at[pl.ds(0, depth)]
    col_weight = weights.at[pl.ds(depth, depth)]
    pair_weight = weights.at[pl.ds(2 * depth, out.shape[0])]
    f32, bf16 = jnp.float32, jnp.bfloat16
    row, chip, core = (lax.axis_index(name) for name in ("row", "chip", "core"))
    channels, n_rows, n_cols = out.shape
    shard = mine.shape[1]

    span = conv_weight.shape[1]

    def block(at):
        cells = weights[pl.ds(2 * depth + (1 + at) * channels, channels), :span]
        return cells.astype(f32)

    taps = [[block(a * TAPS + b) for b in range(TAPS)] for a in range(TAPS)]
    mixing = block(TAPS * TAPS)
    for m in range(TAPS):
        for b in range(TAPS):
            moved = [pltpu.roll(taps[a][b], (m + a) * channels, 1) for a in range(TAPS)]
            rows = pl.ds((b * TAPS + m) * channels, channels)
            conv_weight[rows, :] = (moved[0] + moved[1] + moved[2]).astype(bf16)
        moved = pltpu.roll(mixing, m * channels, 1) if m else mixing
        mix_weight[pl.ds(m * channels, channels), :] = moved.astype(bf16)

    tiles = n_cols // TILE + 1
    zero = jnp.zeros((), bf16)

    def tail(at):
        at = jnp.maximum(at, 0)
        rows = pl.ds(shard - TILE, TILE)
        return jnp.where(core == 1, mine[at, rows], other[at, rows])

    def head(at):
        at = jnp.minimum(at, n_row * n_chip - 1)
        rows = pl.ds(0, TILE)
        return jnp.where(core == 0, mine[at, rows], other[at, rows])

    def projected(first, count, weight):
        sources = [mine[pl.ds(first, count)], other[pl.ds(first, count)]]
        sources = [source.reshape(count * shard, depth) for source in sources]
        cells = jnp.concatenate(sources + [tail(first - 1), head(first + count)], axis=0)
        cells = jnp.dot(cells, weight[...], preferred_element_type=f32).astype(bf16).astype(f32)
        ends = cells[2 * count * shard :]
        shards = []
        for k in range(count):
            for turn, place in ((0, core), (1, 1 - core)):
                at = (turn * count + k) * shard
                shards.append(((2 * k + place) * shard, cells[at : at + shard]))
        return shards, ends[STEP:TILE], ends[TILE : TILE + STEP]

    width = row_proj.shape[1]

    half = n_chip // 2
    shards, left, right = projected(chip * n_chip + core * half, half, col_weight)
    for at, cells in shards:
        col_proj[pl.ds(pl.multiple_of(at, TILE), shard), :] = cells.astype(bf16)
    left = jnp.where((chip == 0) & (core == 0), OUTSIDE, left)
    right = jnp.where((chip == n_chip - 1) & (core == 1), OUTSIDE, right)
    col_proj[n_cols:, :] = jnp.concatenate([right, left], axis=0).astype(bf16)

    shards, left, right = projected(row * n_chip, n_chip, row_weight)
    for at, cells in shards:
        row_proj[pl.ds(pl.multiple_of(STEP + at, STEP), shard), :] = cells
    row_proj[:STEP, :] = jnp.where(row == 0, OUTSIDE, left)
    row_proj[STEP + n_rows : TILE + n_rows, :] = jnp.where(row == n_row - 1, OUTSIDE, right)
    spare = row_proj.shape[0] - TILE - n_rows
    row_proj[TILE + n_rows :, :] = jnp.full((spare, width), OUTSIDE, f32)

    lane = lax.broadcasted_iota(jnp.int32, (1, n_cols), 1)
    transposed = (((1,), (1,)), ((), ()))

    def pair_rows(start, count):
        rows = row_proj[pl.ds(pl.multiple_of(start, STEP), count), :]
        inner, outer = [], []
        for k in range(count):
            spread = jnp.broadcast_to(rows[k : k + 1], (TILE, width)).astype(bf16)
            cells = col_proj[...].reshape(tiles, TILE, width) + spread[None]
            act = jnp.maximum(cells, zero)
            inner.append(act[:-1].reshape(n_cols, width))
            outer.append(act[-1])
        act = jnp.concatenate(inner + outer, axis=0)
        hidden = lax.dot_general(pair_weight[...], act, transposed, preferred_element_type=f32)
        return hidden.astype(bf16)

    def put_rows(start, count, hidden):
        for k in range(count):
            base[start + k] = hidden[:, k * n_cols : (k + 1) * n_cols]
        for k in range(count // STEP):
            at = (count + k) * n_cols
            sides[start // STEP + k] = hidden[:, at : at + n_cols]

    reach = TAPS * channels
    fill = [jnp.zeros((span - WINDOWS * channels, n_cols), bf16)]
    wide = (STEP + 1) * n_cols

    def conv_parts(groups):
        cells = []
        for at in groups:
            for p in range(STEP):
                windows = [base[at * GROUP + p + STEP * m] for m in range(WINDOWS)]
                cells.append(jnp.concatenate(windows + fill, axis=0))
            windows = [sides[at * TAPS + m] for m in range(WINDOWS)]
            cells.append(jnp.concatenate(windows + fill, axis=0))
        cells = jnp.maximum(jnp.concatenate(cells, axis=1), zero)
        return jnp.dot(conv_weight[...], cells, preferred_element_type=f32)

    def shifted(parts):
        mids = []
        for low in range(0, parts.shape[1], wide):
            ends = parts[:, low + STEP * n_cols : low + wide]
            ends = jnp.where(lane % TILE >= STEP, ends[:reach], ends[2 * reach :])
            for p in range(STEP):
                here = parts[:, low + p * n_cols : low + (p + 1) * n_cols]
                end = pltpu.roll(ends, (n_cols - STEP - p * TILE) % n_cols, 1)
                left = jnp.where(lane < STEP, end, pltpu.roll(here[:reach], STEP, 1))
                right = pltpu.roll(here[2 * reach :], n_cols - STEP, 1)
                right = jnp.where(lane >= n_cols - STEP, end, right)
                total = here[reach : 2 * reach] + left + right
                mids.append(jnp.maximum(total, 0.0).astype(bf16))
        return jnp.concatenate(mids, axis=1)

    def mixed_rows(groups, mid):
        mixed = jnp.dot(mix_weight[:, :reach], mid, preferred_element_type=f32)
        for n, at in enumerate(groups):
            for p in range(STEP):
                for m in range(TAPS):
                    row_at = at * GROUP + p + STEP * m
                    low = (n * STEP + p) * n_cols
                    here = mixed[m * channels : (m + 1) * channels, low : low + n_cols]
                    here = here + base[row_at + STEP].astype(f32)
                    result[pl.ds(pl.multiple_of(row_at * channels, STEP), channels), :] = here

    def turn_rows(start, count):
        start = pl.multiple_of(start, TILE)
        for o in range(channels):
            cells = result[pl.ds(start * channels + o, count, stride=channels), :]
            staged[o, pl.ds(start, count), :] = cells.astype(bf16)

    def to_out(start, count, sem):
        rows = pl.ds(pl.multiple_of(start, TILE), count)
        return pltpu.make_async_copy(staged.at[:, rows], out.at[:, rows], sem)

    per_step = 2 * GROUP
    steps = n_rows // per_step - 1
    ahead = per_step + TILE
    put_rows(0, ahead, pair_rows(0, ahead))

    def step(at, _):
        groups = (2 * at, 2 * at + 1)
        start = at * per_step + ahead
        before = jnp.maximum(at - 1, 0)
        parts = conv_parts(groups)
        one = pair_rows(start, GROUP)
        mid = shifted(parts)
        turn_rows(before * per_step, per_step)
        two = pair_rows(start + GROUP, GROUP)
        mixed_rows(groups, mid)
        put_rows(start, GROUP, one)
        put_rows(start + GROUP, GROUP, two)

        @pl.when(at > 0)
        def _send():
            to_out(before * per_step, per_step, sems.at[before]).start()

        return _

    lax.fori_loop(0, steps, step, 0)
    done = steps * per_step
    groups = tuple(range(2 * steps, -(-n_rows // GROUP)))
    parts = conv_parts(groups[:2])
    hidden = pair_rows(done + ahead, GROUP)
    turn_rows(done - per_step, per_step)
    to_out(done - per_step, per_step, sems.at[steps - 1]).start()
    mid = shifted(parts)
    put_rows(done + ahead, GROUP, hidden)
    parts = conv_parts(groups[2:])
    mixed_rows(groups[:2], mid)
    mixed_rows(groups[2:], shifted(parts))
    turn_rows(done, n_rows - done)
    last = to_out(done, n_rows - done, sems.at[steps])
    last.start()
    for at in range(steps):
        to_out(at * per_step, per_step, sems.at[at]).wait()
    last.wait()


def on_device(trunk, row_weight, column_weight, pair_map_weight, dilated_weight, mixing_weight):
    n_row, n_chip = lax.axis_size("row"), lax.axis_size("chip")
    shard, depth = trunk.shape
    n_rows, n_cols = shard * n_chip * 2, shard * n_row
    channels = pair_map_weight.shape[1]
    width = row_weight.shape[1]
    small = jnp.concatenate([dilated_weight.reshape(-1, channels), mixing_weight], axis=0)
    small = jnp.pad(small, ((0, 0), (0, width - channels)))
    weights = jnp.concatenate([row_weight, column_weight, pair_map_weight.T, small], axis=0)

    copies = jnp.broadcast_to(trunk[None], (n_row * n_chip, shard, depth))
    mine = lax.all_to_all(copies, ("row", "chip"), 0, 0)
    other = lax.ppermute(mine, "core", [(0, 1), (1, 0)])
    span = -(-WINDOWS * channels // n_cols) * n_cols
    groups = -(-n_rows // GROUP)
    padded = groups * GROUP + TILE
    return pl.pallas_call(
        functools.partial(kernel, n_row, n_chip),
        out_shape=jax.ShapeDtypeStruct((channels, n_rows, n_cols), jnp.bfloat16),
        out_specs=pl.BlockSpec(memory_space=pl.ANY),
        scratch_shapes=[
            pltpu.VMEM((TAPS * TAPS * channels, span), jnp.bfloat16),
            pltpu.VMEM((TAPS * channels, span), jnp.bfloat16),
            pltpu.VMEM((padded, width), jnp.float32),
            pltpu.VMEM((n_cols + TILE, width), jnp.bfloat16),
            pltpu.VMEM((padded, channels, n_cols), jnp.bfloat16),
            pltpu.VMEM((padded // STEP, channels, n_cols), jnp.bfloat16),
            pltpu.VMEM((groups * GROUP * channels, n_cols), jnp.float32),
            pltpu.VMEM((channels, n_rows, n_cols), jnp.bfloat16),
            pltpu.SemaphoreType.DMA((n_rows // (2 * GROUP),)),
        ],
        compiler_params=pltpu.CompilerParams(vmem_limit_bytes=52 * 2**20),
        name="pair_block",
    )(mine, other, weights)


def solution(mesh):
    n_row, n_col = mesh.devices.shape
    chips = Mesh(mesh.devices.reshape(n_row, n_col // 2, 2), ("row", "chip", "core"))
    return jax.shard_map(
        on_device,
        mesh=chips,
        in_specs=(P(("row", "chip", "core"), None), P(), P(), P(), P(), P()),
        out_specs=P(None, "row", ("chip", "core")),
        check_vma=False,
    )
```

```python
import functools

import jax
import jax.numpy as jnp
from jax import lax
from jax.experimental import pallas as pl
from jax.experimental.pallas import tpu as pltpu
from jax.sharding import Mesh
from jax.sharding import PartitionSpec as P

STEP = 8
TILE = 2 * STEP
TAPS = 3
WINDOWS = TAPS + 2
GROUP = TAPS * STEP
OUTSIDE = -1e30


def kernel(
    n_row,
    n_chip,
    mine,
    other,
    weights,
    out,
    conv_weight,
    mix_weight,
    row_proj,
    col_proj,
    base,
    sides,
    result,
    staged,
    sems,
):
    depth = 2 * mine.shape[1]
    row_weight = weights.at[pl.ds(0, depth)]
    col_weight = weights.at[pl.ds(depth, depth)]
    pair_weight = weights.at[pl.ds(2 * depth, out.shape[0])]
    f32, bf16 = jnp.float32, jnp.bfloat16
    row, chip, core = (lax.axis_index(name) for name in ("row", "chip", "core"))
    channels, n_rows, n_cols = out.shape

    span = conv_weight.shape[1]

    def block(at):
        cells = weights[pl.ds(2 * depth + (1 + at) * channels, channels), :span]
        return cells.astype(f32)

    taps = [[block(a * TAPS + b) for b in range(TAPS)] for a in range(TAPS)]
    mixing = block(TAPS * TAPS)
    for m in range(TAPS):
        for b in range(TAPS):
            moved = [pltpu.roll(taps[a][b], (m + a) * channels, 1) for a in range(TAPS)]
            rows = pl.ds((b * TAPS + m) * channels, channels)
            conv_weight[rows, :] = (moved[0] + moved[1] + moved[2]).astype(bf16)
        moved = pltpu.roll(mixing, m * channels, 1) if m else mixing
        mix_weight[pl.ds(m * channels, channels), :] = moved.astype(bf16)

    tiles = n_cols // TILE + 1
    zero = jnp.zeros((), bf16)

    def projected(start, size, weight):
        ends = (jnp.maximum(start - TILE, 0), jnp.minimum(start + size, mine.shape[0] - TILE))
        spans = [pl.ds(pl.multiple_of(start, TILE), size)]
        spans += [pl.ds(pl.multiple_of(end, TILE), TILE) for end in ends]
        halves = [jnp.concatenate([half[rows] for rows in spans], axis=0) for half in (mine, other)]
        cells = jnp.concatenate(
            [jnp.where(core == k, halves[0], halves[1]) for k in range(2)], axis=1
        )
        cells = jnp.dot(cells, weight[...], preferred_element_type=f32).astype(bf16).astype(f32)
        return cells[:size], cells[size + STEP : size + TILE], cells[size + TILE : size + TILE + STEP]

    width = row_proj.shape[1]

    cells, left, right = projected((chip * 2 + core) * n_cols, n_cols, col_weight)
    col_proj[:n_cols, :] = cells.astype(bf16)
    left = jnp.where((chip == 0) & (core == 0), OUTSIDE, left)
    right = jnp.where((chip == n_chip - 1) & (core == 1), OUTSIDE, right)
    col_proj[n_cols:, :] = jnp.concatenate([right, left], axis=0).astype(bf16)

    cells, left, right = projected(row * n_rows, n_rows, row_weight)
    row_proj[:STEP, :] = jnp.where(row == 0, OUTSIDE, left)
    row_proj[STEP : STEP + n_rows, :] = cells
    row_proj[STEP + n_rows : TILE + n_rows, :] = jnp.where(row == n_row - 1, OUTSIDE, right)
    spare = row_proj.shape[0] - TILE - n_rows
    row_proj[TILE + n_rows :, :] = jnp.full((spare, width), OUTSIDE, f32)

    lane = lax.broadcasted_iota(jnp.int32, (1, n_cols), 1)
    transposed = (((1,), (1,)), ((), ()))

    def pair_acts(start, count):
        rows = row_proj[pl.ds(pl.multiple_of(start, STEP), count), :]
        inner, outer = [], []
        for k in range(count):
            spread = jnp.broadcast_to(rows[k : k + 1], (TILE, width)).astype(bf16)
            cells = col_proj[...].reshape(tiles, TILE, width) + spread[None]
            act = jnp.maximum(cells, zero)
            inner.append(act[:-1].reshape(n_cols, width))
            outer.append(act[-1])
        return jnp.concatenate(inner + outer, axis=0)

    def pair_rows(act):
        hidden = lax.dot_general(pair_weight[...], act, transposed, preferred_element_type=f32)
        return hidden.astype(bf16)

    def put_rows(start, count, hidden):
        for k in range(count):
            base[start + k] = hidden[:, k * n_cols : (k + 1) * n_cols]
        for k in range(count // STEP):
            at = (count + k) * n_cols
            sides[start // STEP + k] = hidden[:, at : at + n_cols]

    reach = TAPS * channels
    fill = [jnp.zeros((span - WINDOWS * channels, n_cols), bf16)]
    wide = (STEP + 1) * n_cols

    def conv_parts(groups):
        cells = []
        for at in groups:
            for p in range(STEP):
                windows = [base[at * GROUP + p + STEP * m] for m in range(WINDOWS)]
                cells.append(jnp.concatenate(windows + fill, axis=0))
            windows = [sides[at * TAPS + m] for m in range(WINDOWS)]
            cells.append(jnp.concatenate(windows + fill, axis=0))
        cells = jnp.maximum(jnp.concatenate(cells, axis=1), zero)
        return jnp.dot(conv_weight[...], cells, preferred_element_type=f32)

    def shifted(parts):
        mids = []
        for low in range(0, parts.shape[1], wide):
            ends = parts[:, low + STEP * n_cols : low + wide]
            ends = jnp.where(lane % TILE >= STEP, ends[:reach], ends[2 * reach :])
            for p in range(STEP):
                here = parts[:, low + p * n_cols : low + (p + 1) * n_cols]
                end = pltpu.roll(ends, (n_cols - STEP - p * TILE) % n_cols, 1)
                left = jnp.where(lane < STEP, end, pltpu.roll(here[:reach], STEP, 1))
                right = pltpu.roll(here[2 * reach :], n_cols - STEP, 1)
                right = jnp.where(lane >= n_cols - STEP, end, right)
                total = here[reach : 2 * reach] + left + right
                mids.append(jnp.maximum(total, 0.0).astype(bf16))
        return jnp.concatenate(mids, axis=1)

    def mixed_rows(groups, mid):
        mixed = jnp.dot(mix_weight[:, :reach], mid, preferred_element_type=f32)
        for n, at in enumerate(groups):
            for p in range(STEP):
                for m in range(TAPS):
                    row_at = at * GROUP + p + STEP * m
                    low = (n * STEP + p) * n_cols
                    here = mixed[m * channels : (m + 1) * channels, low : low + n_cols]
                    here = here + base[row_at + STEP].astype(f32)
                    result[pl.ds(pl.multiple_of(row_at * channels, STEP), channels), :] = here

    def turn_rows(start, count):
        start = pl.multiple_of(start, TILE)
        for o in range(channels):
            cells = result[pl.ds(start * channels + o, count, stride=channels), :]
            staged[o, pl.ds(start, count), :] = cells.astype(bf16)

    def to_out(start, count, sem):
        rows = pl.ds(pl.multiple_of(start, TILE), count)
        return pltpu.make_async_copy(staged.at[:, rows], out.at[:, rows], sem)

    per_step = 2 * GROUP
    steps = n_rows // per_step - 1
    ahead = per_step + TILE
    put_rows(0, ahead, pair_rows(pair_acts(0, ahead)))

    def step(at, _):
        groups = (2 * at, 2 * at + 1)
        start = at * per_step + ahead
        before = jnp.maximum(at - 1, 0)
        one = pair_acts(start, GROUP)
        parts = conv_parts(groups)
        two = pair_acts(start + GROUP, GROUP)
        one = pair_rows(one)
        mid = shifted(parts)
        two = pair_rows(two)
        turn_rows(before * per_step, per_step)
        mixed_rows(groups, mid)
        put_rows(start, GROUP, one)
        put_rows(start + GROUP, GROUP, two)

        @pl.when(at > 0)
        def _send():
            to_out(before * per_step, per_step, sems.at[before]).start()

        return _

    lax.fori_loop(0, steps, step, 0)
    done = steps * per_step
    groups = tuple(range(2 * steps, -(-n_rows // GROUP)))
    parts = conv_parts(groups[:2])
    hidden = pair_rows(pair_acts(done + ahead, GROUP))
    turn_rows(done - per_step, per_step)
    to_out(done - per_step, per_step, sems.at[steps - 1]).start()
    mid = shifted(parts)
    put_rows(done + ahead, GROUP, hidden)
    parts = conv_parts(groups[2:])
    mixed_rows(groups[:2], mid)
    mixed_rows(groups[2:], shifted(parts))
    turn_rows(done, n_rows - done)
    last = to_out(done, n_rows - done, sems.at[steps])
    last.start()
    for at in range(steps):
        to_out(at * per_step, per_step, sems.at[at]).wait()
    last.wait()


def on_device(trunk, row_weight, column_weight, pair_map_weight, dilated_weight, mixing_weight):
    n_row, n_chip = lax.axis_size("row"), lax.axis_size("chip")
    shard, depth = trunk.shape
    n_rows, n_cols = shard * n_chip * 2, shard * n_row
    channels = pair_map_weight.shape[1]
    width = row_weight.shape[1]
    small = jnp.concatenate([dilated_weight.reshape(-1, channels), mixing_weight], axis=0)
    small = jnp.pad(small, ((0, 0), (0, width - channels)))
    weights = jnp.concatenate([row_weight, column_weight, pair_map_weight.T, small], axis=0)

    half = depth // 2
    to = lax.broadcasted_iota(jnp.int32, (n_row * n_chip * 2, shard, half), 0)
    copies = jnp.where(to % 2 == 0, trunk[None, :, :half], trunk[None, :, half:])
    mine = lax.all_to_all(copies, ("row", "chip", "core"), 0, 0).reshape(-1, half)
    other = lax.ppermute(mine, "core", [(0, 1), (1, 0)])
    span = -(-WINDOWS * channels // n_cols) * n_cols
    groups = -(-n_rows // GROUP)
    padded = groups * GROUP + TILE
    return pl.pallas_call(
        functools.partial(kernel, n_row, n_chip),
        out_shape=jax.ShapeDtypeStruct((channels, n_rows, n_cols), jnp.bfloat16),
        out_specs=pl.BlockSpec(memory_space=pl.ANY),
        scratch_shapes=[
            pltpu.VMEM((TAPS * TAPS * channels, span), jnp.bfloat16),
            pltpu.VMEM((TAPS * channels, span), jnp.bfloat16),
            pltpu.VMEM((padded, width), jnp.float32),
            pltpu.VMEM((n_cols + TILE, width), jnp.bfloat16),
            pltpu.VMEM((padded, channels, n_cols), jnp.bfloat16),
            pltpu.VMEM((padded // STEP, channels, n_cols), jnp.bfloat16),
            pltpu.VMEM((groups * GROUP * channels, n_cols), jnp.float32),
            pltpu.VMEM((channels, n_rows, n_cols), jnp.bfloat16),
            pltpu.SemaphoreType.DMA((n_rows // (2 * GROUP),)),
        ],
        compiler_params=pltpu.CompilerParams(vmem_limit_bytes=52 * 2**20),
        name="pair_block",
    )(mine, other, weights)


def solution(mesh):
    n_row, n_col = mesh.devices.shape
    chips = Mesh(mesh.devices.reshape(n_row, n_col // 2, 2), ("row", "chip", "core"))
    return jax.shard_map(
        on_device,
        mesh=chips,
        in_specs=(P(("row", "chip", "core"), None), P(), P(), P(), P(), P()),
        out_specs=P(None, "row", ("chip", "core")),
        check_vma=False,
    )
```

```python
import functools

import jax
import jax.numpy as jnp
from jax import lax
from jax.experimental import pallas as pl
from jax.experimental.pallas import tpu as pltpu
from jax.sharding import Mesh
from jax.sharding import PartitionSpec as P

STEP = 8
TILE = 2 * STEP
TAPS = 3
PART = 4
WINDOWS = TAPS + 2
GROUP = TAPS * STEP
OUTSIDE = -1e30


def kernel(
    n_row,
    n_chip,
    mine,
    other,
    weights,
    out,
    conv_weight,
    mix_weight,
    row_proj,
    col_proj,
    base,
    sides,
    result,
    staged,
    sems,
):
    depth = 2 * mine.shape[1]
    row_weight = weights.at[pl.ds(0, depth)]
    col_weight = weights.at[pl.ds(depth, depth)]
    pair_weight = weights.at[pl.ds(2 * depth, out.shape[0])]
    f32, bf16 = jnp.float32, jnp.bfloat16
    row, chip, core = (lax.axis_index(name) for name in ("row", "chip", "core"))
    channels, n_rows, n_cols = out.shape

    span = conv_weight.shape[1]

    def block(at):
        cells = weights[pl.ds(2 * depth + (1 + at) * channels, channels), :span]
        return cells.astype(f32)

    taps = [[block(a * TAPS + b) for b in range(TAPS)] for a in range(TAPS)]
    mixing = block(TAPS * TAPS)
    for m in range(TAPS):
        for b in range(TAPS):
            moved = [pltpu.roll(taps[a][b], (m + a) * channels, 1) for a in range(TAPS)]
            rows = pl.ds((b * TAPS + m) * channels, channels)
            conv_weight[rows, :] = (moved[0] + moved[1] + moved[2]).astype(bf16)
        moved = pltpu.roll(mixing, m * channels, 1) if m else mixing
        mix_weight[pl.ds(m * channels, channels), :] = moved.astype(bf16)

    tiles = n_cols // TILE + 1
    zero = jnp.zeros((), bf16)

    def projected(start, size, weight):
        ends = (jnp.maximum(start - TILE, 0), jnp.minimum(start + size, mine.shape[0] - TILE))
        spans = [pl.ds(pl.multiple_of(start, TILE), size)]
        spans += [pl.ds(pl.multiple_of(end, TILE), TILE) for end in ends]
        halves = [jnp.concatenate([half[rows] for rows in spans], axis=0) for half in (mine, other)]
        cells = jnp.concatenate(
            [jnp.where(core == k, halves[0], halves[1]) for k in range(2)], axis=1
        )
        cells = jnp.dot(cells, weight[...], preferred_element_type=f32).astype(bf16).astype(f32)
        return cells[:size], cells[size + STEP : size + TILE], cells[size + TILE : size + TILE + STEP]

    width = row_proj.shape[1]

    cells, left, right = projected((chip * 2 + core) * n_cols, n_cols, col_weight)
    col_proj[:n_cols, :] = cells.astype(bf16)
    left = jnp.where((chip == 0) & (core == 0), OUTSIDE, left)
    right = jnp.where((chip == n_chip - 1) & (core == 1), OUTSIDE, right)
    col_proj[n_cols:, :] = jnp.concatenate([right, left], axis=0).astype(bf16)

    cells, left, right = projected(row * n_rows, n_rows, row_weight)
    row_proj[:STEP, :] = jnp.where(row == 0, OUTSIDE, left)
    row_proj[STEP : STEP + n_rows, :] = cells
    row_proj[STEP + n_rows : TILE + n_rows, :] = jnp.where(row == n_row - 1, OUTSIDE, right)
    spare = row_proj.shape[0] - TILE - n_rows
    row_proj[TILE + n_rows :, :] = jnp.full((spare, width), OUTSIDE, f32)

    lane = lax.broadcasted_iota(jnp.int32, (1, n_cols), 1)
    transposed = (((1,), (1,)), ((), ()))

    def pair_cells(acts):
        act = jnp.concatenate(acts, axis=0)
        hidden = lax.dot_general(pair_weight[...], act, transposed, preferred_element_type=f32)
        return hidden.astype(bf16)

    def pair_rows(start, count, outer):
        rows = row_proj[pl.ds(pl.multiple_of(start, STEP), count), :]
        hidden = []
        for low in range(0, count, PART):
            inner = []
            for k in range(low, low + PART):
                spread = jnp.broadcast_to(rows[k : k + 1], (TILE, width)).astype(bf16)
                cells = col_proj[...].reshape(tiles, TILE, width) + spread[None]
                act = jnp.maximum(cells, zero)
                inner.append(act[:-1].reshape(n_cols, width))
                outer.append(act[-1])
            hidden.append(pair_cells(inner))
        return hidden

    def put_rows(start, hidden):
        for n, cells in enumerate(hidden):
            for k in range(PART):
                base[start + n * PART + k] = cells[:, k * n_cols : (k + 1) * n_cols]

    def put_sides(start, cells):
        for k in range(cells.shape[1] // n_cols):
            sides[start // STEP + k] = cells[:, k * n_cols : (k + 1) * n_cols]

    reach = TAPS * channels
    pitch = channels + STEP
    fill = [jnp.zeros((span - WINDOWS * channels, n_cols), bf16)]
    wide = (STEP + 1) * n_cols

    def conv_parts(groups):
        cells = []
        for at in groups:
            for p in range(STEP):
                windows = [base[at * GROUP + p + STEP * m] for m in range(WINDOWS)]
                cells.append(jnp.concatenate(windows + fill, axis=0))
            windows = [sides[at * TAPS + m] for m in range(WINDOWS)]
            cells.append(jnp.concatenate(windows + fill, axis=0))
        cells = jnp.maximum(jnp.concatenate(cells, axis=1), zero)
        return jnp.dot(conv_weight[...], cells, preferred_element_type=f32)

    def shifted(parts):
        mids = []
        for low in range(0, parts.shape[1], wide):
            ends = parts[:, low + STEP * n_cols : low + wide]
            ends = jnp.where(lane % TILE >= STEP, ends[:reach], ends[2 * reach :])
            for p in range(STEP):
                here = parts[:, low + p * n_cols : low + (p + 1) * n_cols]
                end = pltpu.roll(ends, (n_cols - STEP - p * TILE) % n_cols, 1)
                left = jnp.where(lane < STEP, end, pltpu.roll(here[:reach], STEP, 1))
                right = pltpu.roll(here[2 * reach :], n_cols - STEP, 1)
                right = jnp.where(lane >= n_cols - STEP, end, right)
                total = here[reach : 2 * reach] + left + right
                mids.append(jnp.maximum(total, 0.0).astype(bf16))
        return jnp.concatenate(mids, axis=1)

    def mixed_rows(groups, mid):
        mixed = jnp.dot(mix_weight[:, :reach], mid, preferred_element_type=f32)
        for n, at in enumerate(groups):
            for p in range(STEP):
                for m in range(TAPS):
                    row_at = at * GROUP + p + STEP * m
                    low = (n * STEP + p) * n_cols
                    here = mixed[m * channels : (m + 1) * channels, low : low + n_cols]
                    here = here + base[row_at + STEP].astype(f32)
                    result[pl.ds(pl.multiple_of(row_at * pitch, STEP), channels), :] = here

    def turn_rows(start, count):
        start = pl.multiple_of(start, TILE)
        for o in range(channels):
            cells = result[pl.ds(start * pitch + o, count, stride=pitch), :]
            staged[o, pl.ds(start, count), :] = cells.astype(bf16)

    def to_out(start, count, sem):
        rows = pl.ds(pl.multiple_of(start, TILE), count)
        return pltpu.make_async_copy(staged.at[:, rows], out.at[:, rows], sem)

    per_step = 2 * GROUP
    steps = n_rows // per_step - 1
    ahead = per_step + TILE
    outer = []
    put_rows(0, pair_rows(0, ahead, outer))
    put_sides(0, pair_cells(outer))

    def step(at, _):
        groups = (2 * at, 2 * at + 1)
        start = at * per_step + ahead
        before = jnp.maximum(at - 1, 0)
        parts = conv_parts(groups)
        outer = []
        one = pair_rows(start, GROUP, outer)
        mid = shifted(parts)
        two = pair_rows(start + GROUP, GROUP, outer)
        outer = pair_cells(outer)
        turn_rows(before * per_step, per_step)
        mixed_rows(groups, mid)
        put_rows(start, one + two)
        put_sides(start, outer)

        @pl.when(at > 0)
        def _send():
            to_out(before * per_step, per_step, sems.at[before]).start()

        return _

    lax.fori_loop(0, steps, step, 0)
    done = steps * per_step
    groups = tuple(range(2 * steps, -(-n_rows // GROUP)))
    parts = conv_parts(groups[:2])
    outer = []
    hidden = pair_rows(done + ahead, GROUP, outer)
    outer = pair_cells(outer)
    turn_rows(done - per_step, per_step)
    to_out(done - per_step, per_step, sems.at[steps - 1]).start()
    mid = shifted(parts)
    put_rows(done + ahead, hidden)
    put_sides(done + ahead, outer)
    parts = conv_parts(groups[2:])
    mixed_rows(groups[:2], mid)
    mixed_rows(groups[2:], shifted(parts))
    turn_rows(done, n_rows - done)
    last = to_out(done, n_rows - done, sems.at[steps])
    last.start()
    for at in range(steps):
        to_out(at * per_step, per_step, sems.at[at]).wait()
    last.wait()


def on_device(trunk, row_weight, column_weight, pair_map_weight, dilated_weight, mixing_weight):
    n_row, n_chip = lax.axis_size("row"), lax.axis_size("chip")
    shard, depth = trunk.shape
    n_rows, n_cols = shard * n_chip * 2, shard * n_row
    channels = pair_map_weight.shape[1]
    width = row_weight.shape[1]
    small = jnp.concatenate([dilated_weight.reshape(-1, channels), mixing_weight], axis=0)
    small = jnp.pad(small, ((0, 0), (0, width - channels)))
    weights = jnp.concatenate([row_weight, column_weight, pair_map_weight.T, small], axis=0)

    half = depth // 2
    to = lax.broadcasted_iota(jnp.int32, (n_row * n_chip * 2, shard, half), 0)
    copies = jnp.where(to % 2 == 0, trunk[None, :, :half], trunk[None, :, half:])
    mine = lax.all_to_all(copies, ("row", "chip", "core"), 0, 0).reshape(-1, half)
    other = lax.ppermute(mine, "core", [(0, 1), (1, 0)])
    span = -(-WINDOWS * channels // n_cols) * n_cols
    groups = -(-n_rows // GROUP)
    padded = groups * GROUP + TILE
    return pl.pallas_call(
        functools.partial(kernel, n_row, n_chip),
        out_shape=jax.ShapeDtypeStruct((channels, n_rows, n_cols), jnp.bfloat16),
        out_specs=pl.BlockSpec(memory_space=pl.ANY),
        scratch_shapes=[
            pltpu.VMEM((TAPS * TAPS * channels, span), jnp.bfloat16),
            pltpu.VMEM((TAPS * channels, span), jnp.bfloat16),
            pltpu.VMEM((padded, width), jnp.float32),
            pltpu.VMEM((n_cols + TILE, width), jnp.bfloat16),
            pltpu.VMEM((padded, channels, n_cols), jnp.bfloat16),
            pltpu.VMEM((padded // STEP, channels, n_cols), jnp.bfloat16),
            pltpu.VMEM((groups * GROUP * (channels + STEP), n_cols), jnp.float32),
            pltpu.VMEM((channels, n_rows, n_cols), jnp.bfloat16),
            pltpu.SemaphoreType.DMA((n_rows // (2 * GROUP),)),
        ],
        compiler_params=pltpu.CompilerParams(vmem_limit_bytes=52 * 2**20),
        name="pair_block",
    )(mine, other, weights)


def solution(mesh):
    n_row, n_col = mesh.devices.shape
    chips = Mesh(mesh.devices.reshape(n_row, n_col // 2, 2), ("row", "chip", "core"))
    return jax.shard_map(
        on_device,
        mesh=chips,
        in_specs=(P(("row", "chip", "core"), None), P(), P(), P(), P(), P()),
        out_specs=P(None, "row", ("chip", "core")),
        check_vma=False,
    )
```

```python
import functools

import jax
import jax.numpy as jnp
from jax import lax
from jax.experimental import pallas as pl
from jax.experimental.pallas import tpu as pltpu
from jax.sharding import Mesh
from jax.sharding import PartitionSpec as P

STEP = 8
TILE = 2 * STEP
TAPS = 3
PART = 4
WINDOWS = TAPS + 2
GROUP = TAPS * STEP
OUTSIDE = -1e30


def kernel(
    n_row,
    n_chip,
    mine,
    other,
    weights,
    out,
    conv_weight,
    mix_weight,
    row_proj,
    col_proj,
    base,
    sides,
    result,
    staged,
    sems,
):
    depth = 2 * mine.shape[1]
    row_weight = weights.at[pl.ds(0, depth)]
    col_weight = weights.at[pl.ds(depth, depth)]
    pair_weight = weights.at[pl.ds(2 * depth, out.shape[0])]
    f32, bf16 = jnp.float32, jnp.bfloat16
    row, chip, core = (lax.axis_index(name) for name in ("row", "chip", "core"))
    channels, n_rows, n_cols = out.shape

    span = conv_weight.shape[1]

    def block(at):
        cells = weights[pl.ds(2 * depth + (1 + at) * channels, channels), :span]
        return cells.astype(f32)

    taps = [[block(a * TAPS + b) for b in range(TAPS)] for a in range(TAPS)]
    mixing = block(TAPS * TAPS)
    for m in range(TAPS):
        for b in range(TAPS):
            moved = [pltpu.roll(taps[a][b], (m + a) * channels, 1) for a in range(TAPS)]
            rows = pl.ds((b * TAPS + m) * channels, channels)
            conv_weight[rows, :] = (moved[0] + moved[1] + moved[2]).astype(bf16)
        moved = pltpu.roll(mixing, m * channels, 1) if m else mixing
        mix_weight[pl.ds(m * channels, channels), :] = moved.astype(bf16)

    tiles = n_cols // TILE + 1
    zero = jnp.zeros((), bf16)

    def projected(start, size, weight):
        ends = (jnp.maximum(start - TILE, 0), jnp.minimum(start + size, mine.shape[0] - TILE))
        spans = [pl.ds(pl.multiple_of(start, TILE), size)]
        spans += [pl.ds(pl.multiple_of(end, TILE), TILE) for end in ends]
        halves = [jnp.concatenate([half[rows] for rows in spans], axis=0) for half in (mine, other)]
        cells = jnp.concatenate(
            [jnp.where(core == k, halves[0], halves[1]) for k in range(2)], axis=1
        )
        cells = jnp.dot(cells, weight[...], preferred_element_type=f32).astype(bf16).astype(f32)
        return cells[:size], cells[size + STEP : size + TILE], cells[size + TILE : size + TILE + STEP]

    width = row_proj.shape[1]

    cells, left, right = projected((chip * 2 + core) * n_cols, n_cols, col_weight)
    col_proj[:n_cols, :] = cells.astype(bf16)
    left = jnp.where((chip == 0) & (core == 0), OUTSIDE, left)
    right = jnp.where((chip == n_chip - 1) & (core == 1), OUTSIDE, right)
    col_proj[n_cols:, :] = jnp.concatenate([right, left], axis=0).astype(bf16)

    cells, left, right = projected(row * n_rows, n_rows, row_weight)
    row_proj[:STEP, :] = jnp.where(row == 0, OUTSIDE, left)
    row_proj[STEP : STEP + n_rows, :] = cells
    row_proj[STEP + n_rows : TILE + n_rows, :] = jnp.where(row == n_row - 1, OUTSIDE, right)
    spare = row_proj.shape[0] - TILE - n_rows
    row_proj[TILE + n_rows :, :] = jnp.full((spare, width), OUTSIDE, f32)

    lane = lax.broadcasted_iota(jnp.int32, (1, n_cols), 1)
    transposed = (((1,), (1,)), ((), ()))

    def pair_cells(acts):
        act = jnp.concatenate(acts, axis=0)
        hidden = lax.dot_general(pair_weight[...], act, transposed, preferred_element_type=f32)
        return hidden.astype(bf16)

    def pair_rows(rows, outer):
        hidden = []
        for low in range(0, rows.shape[0], PART):
            inner = []
            for k in range(low, low + PART):
                spread = jnp.broadcast_to(rows[k : k + 1], (TILE, width)).astype(bf16)
                cells = col_proj[...].reshape(tiles, TILE, width) + spread[None]
                act = jnp.maximum(cells, zero)
                inner.append(act[:-1].reshape(n_cols, width))
                outer.append(act[-1])
            hidden.append(pair_cells(inner))
        return hidden

    def put_rows(start, hidden):
        for n, cells in enumerate(hidden):
            for k in range(PART):
                base[start + n * PART + k] = cells[:, k * n_cols : (k + 1) * n_cols]

    def put_sides(start, cells):
        for k in range(cells.shape[1] // n_cols):
            sides[start // STEP + k] = cells[:, k * n_cols : (k + 1) * n_cols]

    reach = TAPS * channels
    pitch = channels + STEP
    fill = [jnp.zeros((span - WINDOWS * channels, n_cols), bf16)]

    def conv_cells(blocks):
        cells = [jnp.concatenate(windows + fill, axis=0) for windows in blocks]
        cells = jnp.maximum(jnp.concatenate(cells, axis=1), zero)
        return jnp.dot(conv_weight[...], cells, preferred_element_type=f32)

    def conv_ends(groups):
        parts = conv_cells([[sides[at * TAPS + m] for m in range(WINDOWS)] for at in groups])
        ends = []
        for n in range(len(groups)):
            part = parts[:, n * n_cols : (n + 1) * n_cols]
            ends.append(jnp.where(lane % TILE >= STEP, part[:reach], part[2 * reach :]))
        return ends

    def conv_parts(at, low):
        places = [at * GROUP + p for p in range(low, low + PART)]
        return conv_cells([[base[p + STEP * m] for m in range(WINDOWS)] for p in places])

    def shifted(parts, ends, low):
        mids = []
        for k in range(PART):
            here = parts[:, k * n_cols : (k + 1) * n_cols]
            end = pltpu.roll(ends, (n_cols - STEP - (low + k) * TILE) % n_cols, 1)
            left = jnp.where(lane < STEP, end, pltpu.roll(here[:reach], STEP, 1))
            right = pltpu.roll(here[2 * reach :], n_cols - STEP, 1)
            right = jnp.where(lane >= n_cols - STEP, end, right)
            total = here[reach : 2 * reach] + left + right
            mids.append(jnp.maximum(total, 0.0).astype(bf16))
        return jnp.concatenate(mids, axis=1)

    def mixed_rows(at, low, mid):
        mixed = jnp.dot(mix_weight[:, :reach], mid, preferred_element_type=f32)
        for k in range(PART):
            for m in range(TAPS):
                row_at = at * GROUP + low + k + STEP * m
                here = mixed[m * channels : (m + 1) * channels, k * n_cols : (k + 1) * n_cols]
                here = here + base[row_at + STEP].astype(f32)
                result[pl.ds(pl.multiple_of(row_at * pitch, STEP), channels), :] = here

    def turn_rows(start, count):
        start = pl.multiple_of(start, TILE)
        for o in range(channels):
            cells = result[pl.ds(start * pitch + o, count, stride=pitch), :]
            staged[o, pl.ds(start, count), :] = cells.astype(bf16)

    def to_out(start, count, sem):
        rows = pl.ds(pl.multiple_of(start, TILE), count)
        return pltpu.make_async_copy(staged.at[:, rows], out.at[:, rows], sem)

    per_step = 2 * GROUP
    steps = n_rows // per_step - 1
    ahead = per_step + TILE
    outer = []
    put_rows(0, pair_rows(row_proj[:ahead, :], outer))
    put_sides(0, pair_cells(outer))

    def rounds(groups, start, count, turn):
        ends = conv_ends(groups)
        places = [(n, low) for n in range(len(groups)) for low in range(0, STEP, PART)]
        share = -(-count // (PART * len(places))) * PART
        hidden, outer, mid = [], [], None
        rows = row_proj[pl.ds(pl.multiple_of(start, STEP), count), :]
        for n, (group, low) in enumerate(places):
            parts = conv_parts(groups[group], low)
            if n == 0:
                turn()
            hidden += pair_rows(rows[n * share : (n + 1) * share], outer)
            if n:
                mixed_rows(groups[places[n - 1][0]], places[n - 1][1], mid)
            mid = shifted(parts, ends[group], low)
        outer = pair_cells(outer)
        mixed_rows(groups[-1], places[-1][1], mid)
        put_rows(start, hidden)
        put_sides(start, outer)

    def step(at, _):
        before = jnp.maximum(at - 1, 0)
        rounds(
            (2 * at, 2 * at + 1),
            at * per_step + ahead,
            per_step,
            lambda: turn_rows(before * per_step, per_step),
        )

        @pl.when(at > 0)
        def _send():
            to_out(before * per_step, per_step, sems.at[before]).start()

        return _

    lax.fori_loop(0, steps, step, 0)
    done = steps * per_step
    rounds(
        (2 * steps, 2 * steps + 1),
        done + ahead,
        GROUP,
        lambda: turn_rows(done - per_step, per_step),
    )
    to_out(done - per_step, per_step, sems.at[steps - 1]).start()
    for at in range(2 * steps + 2, -(-n_rows // GROUP)):
        (ends,) = conv_ends((at,))
        mids = [(low, shifted(conv_parts(at, low), ends, low)) for low in range(0, STEP, PART)]
        for low, mid in mids:
            mixed_rows(at, low, mid)
    turn_rows(done, n_rows - done)
    last = to_out(done, n_rows - done, sems.at[steps])
    last.start()
    for at in range(steps):
        to_out(at * per_step, per_step, sems.at[at]).wait()
    last.wait()


def on_device(trunk, row_weight, column_weight, pair_map_weight, dilated_weight, mixing_weight):
    n_row, n_chip = lax.axis_size("row"), lax.axis_size("chip")
    shard, depth = trunk.shape
    n_rows, n_cols = shard * n_chip * 2, shard * n_row
    channels = pair_map_weight.shape[1]
    width = row_weight.shape[1]
    small = jnp.concatenate([dilated_weight.reshape(-1, channels), mixing_weight], axis=0)
    small = jnp.pad(small, ((0, 0), (0, width - channels)))
    weights = jnp.concatenate([row_weight, column_weight, pair_map_weight.T, small], axis=0)

    half = depth // 2
    to = lax.broadcasted_iota(jnp.int32, (n_row * n_chip * 2, shard, half), 0)
    copies = jnp.where(to % 2 == 0, trunk[None, :, :half], trunk[None, :, half:])
    mine = lax.all_to_all(copies, ("row", "chip", "core"), 0, 0).reshape(-1, half)
    other = lax.ppermute(mine, "core", [(0, 1), (1, 0)])
    span = -(-WINDOWS * channels // n_cols) * n_cols
    groups = -(-n_rows // GROUP)
    padded = groups * GROUP + TILE
    return pl.pallas_call(
        functools.partial(kernel, n_row, n_chip),
        out_shape=jax.ShapeDtypeStruct((channels, n_rows, n_cols), jnp.bfloat16),
        out_specs=pl.BlockSpec(memory_space=pl.ANY),
        scratch_shapes=[
            pltpu.VMEM((TAPS * TAPS * channels, span), jnp.bfloat16),
            pltpu.VMEM((TAPS * channels, span), jnp.bfloat16),
            pltpu.VMEM((padded, width), jnp.float32),
            pltpu.VMEM((n_cols + TILE, width), jnp.bfloat16),
            pltpu.VMEM((padded, channels, n_cols), jnp.bfloat16),
            pltpu.VMEM((padded // STEP, channels, n_cols), jnp.bfloat16),
            pltpu.VMEM((groups * GROUP * (channels + STEP), n_cols), jnp.float32),
            pltpu.VMEM((channels, n_rows, n_cols), jnp.bfloat16),
            pltpu.SemaphoreType.DMA((n_rows // (2 * GROUP),)),
        ],
        compiler_params=pltpu.CompilerParams(vmem_limit_bytes=52 * 2**20),
        name="pair_block",
    )(mine, other, weights)


def solution(mesh):
    n_row, n_col = mesh.devices.shape
    chips = Mesh(mesh.devices.reshape(n_row, n_col // 2, 2), ("row", "chip", "core"))
    return jax.shard_map(
        on_device,
        mesh=chips,
        in_specs=(P(("row", "chip", "core"), None), P(), P(), P(), P(), P()),
        out_specs=P(None, "row", ("chip", "core")),
        check_vma=False,
    )
```

```python
import functools

import jax
import jax.numpy as jnp
from jax import lax
from jax.experimental import pallas as pl
from jax.experimental.pallas import tpu as pltpu
from jax.sharding import Mesh
from jax.sharding import PartitionSpec as P

STEP = 8
TILE = 2 * STEP
TAPS = 3
PART = 4
WINDOWS = TAPS + 2
GROUP = TAPS * STEP
OUTSIDE = -1e30


def kernel(
    n_row,
    n_chip,
    mine,
    other,
    weights,
    out,
    conv_weight,
    mix_weight,
    row_proj,
    col_proj,
    base,
    sides,
    result,
    staged,
    sems,
):
    depth = 2 * mine.shape[1]
    row_weight = weights.at[pl.ds(0, depth)]
    col_weight = weights.at[pl.ds(depth, depth)]
    pair_weight = weights.at[pl.ds(2 * depth, out.shape[0])]
    f32, bf16 = jnp.float32, jnp.bfloat16
    row, chip, core = (lax.axis_index(name) for name in ("row", "chip", "core"))
    channels, n_rows, n_cols = out.shape

    span = conv_weight.shape[1]

    def block(at):
        cells = weights[pl.ds(2 * depth + (1 + at) * channels, channels), :span]
        return cells.astype(f32)

    taps = [[block(a * TAPS + b) for b in range(TAPS)] for a in range(TAPS)]
    mixing = block(TAPS * TAPS)
    for m in range(TAPS):
        for b in range(TAPS):
            moved = [pltpu.roll(taps[a][b], (m + a) * channels, 1) for a in range(TAPS)]
            rows = pl.ds((b * TAPS + m) * channels, channels)
            conv_weight[rows, :] = (moved[0] + moved[1] + moved[2]).astype(bf16)
        moved = pltpu.roll(mixing, m * channels, 1) if m else mixing
        mix_weight[pl.ds(m * channels, channels), :] = moved.astype(bf16)

    tiles = n_cols // TILE + 1
    zero = jnp.zeros((), bf16)

    def projected(start, size, weight):
        ends = (jnp.maximum(start - TILE, 0), jnp.minimum(start + size, mine.shape[0] - TILE))
        spans = [pl.ds(pl.multiple_of(start, TILE), size)]
        spans += [pl.ds(pl.multiple_of(end, TILE), TILE) for end in ends]
        halves = [jnp.concatenate([half[rows] for rows in spans], axis=0) for half in (mine, other)]
        cells = jnp.concatenate(
            [jnp.where(core == k, halves[0], halves[1]) for k in range(2)], axis=1
        )
        cells = jnp.dot(cells, weight[...], preferred_element_type=f32).astype(bf16).astype(f32)
        return cells[:size], cells[size + STEP : size + TILE], cells[size + TILE : size + TILE + STEP]

    width = row_proj.shape[1]

    cells, left, right = projected((chip * 2 + core) * n_cols, n_cols, col_weight)
    col_proj[:n_cols, :] = cells.astype(bf16)
    left = jnp.where((chip == 0) & (core == 0), OUTSIDE, left)
    right = jnp.where((chip == n_chip - 1) & (core == 1), OUTSIDE, right)
    col_proj[n_cols:, :] = jnp.concatenate([right, left], axis=0).astype(bf16)

    cells, left, right = projected(row * n_rows, n_rows, row_weight)
    row_proj[:STEP, :] = jnp.where(row == 0, OUTSIDE, left)
    row_proj[STEP : STEP + n_rows, :] = cells
    row_proj[STEP + n_rows : TILE + n_rows, :] = jnp.where(row == n_row - 1, OUTSIDE, right)

    lane = lax.broadcasted_iota(jnp.int32, (1, n_cols), 1)
    transposed = (((1,), (1,)), ((), ()))

    def pair_cells(acts):
        act = jnp.concatenate(acts, axis=0)
        hidden = lax.dot_general(pair_weight[...], act, transposed, preferred_element_type=f32)
        return hidden.astype(bf16)

    def pair_rows(rows, outer):
        hidden = []
        for low in range(0, rows.shape[0], PART):
            inner = []
            for k in range(low, low + PART):
                spread = jnp.broadcast_to(rows[k : k + 1], (TILE, width)).astype(bf16)
                cells = col_proj[...].reshape(tiles, TILE, width) + spread[None]
                act = jnp.maximum(cells, zero)
                inner.append(act[:-1].reshape(n_cols, width))
                outer.append(act[-1])
            hidden.append(pair_cells(inner))
        return hidden

    def put_rows(start, hidden):
        for n, cells in enumerate(hidden):
            for k in range(PART):
                base[start + n * PART + k] = cells[:, k * n_cols : (k + 1) * n_cols]

    def put_sides(start, cells):
        for k in range(cells.shape[1] // n_cols):
            sides[start // STEP + k] = cells[:, k * n_cols : (k + 1) * n_cols]

    reach = TAPS * channels
    pitch = channels + STEP
    fill = [jnp.zeros((span - WINDOWS * channels, n_cols), bf16)]

    def conv_cells(blocks):
        cells = [jnp.concatenate(windows + fill, axis=0) for windows in blocks]
        cells = jnp.maximum(jnp.concatenate(cells, axis=1), zero)
        return jnp.dot(conv_weight[...], cells, preferred_element_type=f32)

    def conv_ends(groups):
        parts = conv_cells([[sides[at * TAPS + m] for m in range(WINDOWS)] for at in groups])
        ends = []
        for n in range(len(groups)):
            part = parts[:, n * n_cols : (n + 1) * n_cols]
            ends.append(jnp.where(lane % TILE >= STEP, part[:reach], part[2 * reach :]))
        return ends

    def conv_parts(at, low):
        places = [at * GROUP + p for p in range(low, low + PART)]
        return conv_cells([[base[p + STEP * m] for m in range(WINDOWS)] for p in places])

    def shifted(parts, ends, low):
        mids = []
        for k in range(PART):
            here = parts[:, k * n_cols : (k + 1) * n_cols]
            end = pltpu.roll(ends, (n_cols - STEP - (low + k) * TILE) % n_cols, 1)
            left = jnp.where(lane < STEP, end, pltpu.roll(here[:reach], STEP, 1))
            right = pltpu.roll(here[2 * reach :], n_cols - STEP, 1)
            right = jnp.where(lane >= n_cols - STEP, end, right)
            total = here[reach : 2 * reach] + left + right
            mids.append(jnp.maximum(total, 0.0).astype(bf16))
        return jnp.concatenate(mids, axis=1)

    def mixed_rows(at, low, mid):
        mixed = jnp.dot(mix_weight[:, :reach], mid, preferred_element_type=f32)
        for k in range(PART):
            for m in range(TAPS):
                row_at = at * GROUP + low + k + STEP * m
                here = mixed[m * channels : (m + 1) * channels, k * n_cols : (k + 1) * n_cols]
                here = here + base[row_at + STEP].astype(f32)
                result[pl.ds(pl.multiple_of(row_at * pitch, STEP), channels), :] = here

    def turn_rows(start, count):
        start = pl.multiple_of(start, TILE)
        for o in range(channels):
            cells = result[pl.ds(start * pitch + o, count, stride=pitch), :]
            staged[o, pl.ds(start, count), :] = cells.astype(bf16)

    def to_out(start, count, sem):
        rows = pl.ds(pl.multiple_of(start, TILE), count)
        return pltpu.make_async_copy(staged.at[:, rows], out.at[:, rows], sem)

    per_step = 2 * GROUP
    steps = n_rows // per_step - 1
    ahead = per_step + TILE
    outer = []
    put_rows(0, pair_rows(row_proj[:ahead, :], outer))
    put_sides(0, pair_cells(outer))

    def rounds(groups, start, count, turn):
        ends = conv_ends(groups)
        places = [(n, low) for n in range(len(groups)) for low in range(0, STEP, PART)]
        share = -(-count // (PART * len(places))) * PART
        hidden, outer, mid = [], [], None
        rows = row_proj[pl.ds(pl.multiple_of(start, STEP), count), :]
        for n, (group, low) in enumerate(places):
            parts = conv_parts(groups[group], low)
            if n == 0:
                turn()
            hidden += pair_rows(rows[n * share : (n + 1) * share], outer)
            if n:
                mixed_rows(groups[places[n - 1][0]], places[n - 1][1], mid)
            mid = shifted(parts, ends[group], low)
        outer = pair_cells(outer)
        mixed_rows(groups[-1], places[-1][1], mid)
        put_rows(start, hidden)
        put_sides(start, outer)

    def step(at, _):
        before = jnp.maximum(at - 1, 0)
        rounds(
            (2 * at, 2 * at + 1),
            at * per_step + ahead,
            per_step,
            lambda: turn_rows(before * per_step, per_step),
        )

        @pl.when(at > 0)
        def _send():
            to_out(before * per_step, per_step, sems.at[before]).start()

        return _

    spare = pl.ds(n_rows + TILE, STEP)
    base[spare] = jnp.zeros_like(base[spare])
    sides[(n_rows + TILE) // STEP] = jnp.zeros_like(sides[0])
    lax.fori_loop(0, steps, step, 0)

    done = steps * per_step
    rounds(
        (2 * steps, 2 * steps + 1),
        done + ahead,
        TILE,
        lambda: turn_rows(done - per_step, per_step),
    )
    to_out(done - per_step, per_step, sems.at[steps - 1]).start()
    at = 2 * steps + 2
    (ends,) = conv_ends((at,))
    lows = range(0, STEP, PART)
    parts = [conv_parts(at, low) for low in lows]
    turn_rows(done, per_step)
    to_out(done, per_step, sems.at[steps]).start()
    for low, part in zip(lows, parts):
        mixed_rows(at, low, shifted(part, ends, low))
    done += per_step
    turn_rows(done, n_rows - done)
    last = to_out(done, n_rows - done, sems.at[steps + 1])
    last.start()
    for at in range(steps + 1):
        to_out(at * per_step, per_step, sems.at[at]).wait()
    last.wait()


def on_device(trunk, row_weight, column_weight, pair_map_weight, dilated_weight, mixing_weight):
    n_row, n_chip = lax.axis_size("row"), lax.axis_size("chip")
    shard, depth = trunk.shape
    n_rows, n_cols = shard * n_chip * 2, shard * n_row
    channels = pair_map_weight.shape[1]
    width = row_weight.shape[1]
    small = jnp.concatenate([dilated_weight.reshape(-1, channels), mixing_weight], axis=0)
    small = jnp.pad(small, ((0, 0), (0, width - channels)))
    weights = jnp.concatenate([row_weight, column_weight, pair_map_weight.T, small], axis=0)

    half = depth // 2
    to = lax.broadcasted_iota(jnp.int32, (n_row * n_chip * 2, shard, half), 0)
    copies = jnp.where(to % 2 == 0, trunk[None, :, :half], trunk[None, :, half:])
    mine = lax.all_to_all(copies, ("row", "chip", "core"), 0, 0).reshape(-1, half)
    other = lax.ppermute(mine, "core", [(0, 1), (1, 0)])
    span = -(-WINDOWS * channels // n_cols) * n_cols
    groups = -(-n_rows // GROUP)
    padded = groups * GROUP + TILE
    return pl.pallas_call(
        functools.partial(kernel, n_row, n_chip),
        out_shape=jax.ShapeDtypeStruct((channels, n_rows, n_cols), jnp.bfloat16),
        out_specs=pl.BlockSpec(memory_space=pl.ANY),
        scratch_shapes=[
            pltpu.VMEM((TAPS * TAPS * channels, span), jnp.bfloat16),
            pltpu.VMEM((TAPS * channels, span), jnp.bfloat16),
            pltpu.VMEM((n_rows + TILE, width), jnp.float32),
            pltpu.VMEM((n_cols + TILE, width), jnp.bfloat16),
            pltpu.VMEM((padded, channels, n_cols), jnp.bfloat16),
            pltpu.VMEM((padded // STEP, channels, n_cols), jnp.bfloat16),
            pltpu.VMEM((groups * GROUP * (channels + STEP), n_cols), jnp.float32),
            pltpu.VMEM((channels, n_rows, n_cols), jnp.bfloat16),
            pltpu.SemaphoreType.DMA((n_rows // (2 * GROUP) + 1,)),
        ],
        compiler_params=pltpu.CompilerParams(vmem_limit_bytes=52 * 2**20),
        name="pair_block",
    )(mine, other, weights)


def solution(mesh):
    n_row, n_col = mesh.devices.shape
    chips = Mesh(mesh.devices.reshape(n_row, n_col // 2, 2), ("row", "chip", "core"))
    return jax.shard_map(
        on_device,
        mesh=chips,
        in_specs=(P(("row", "chip", "core"), None), P(), P(), P(), P(), P()),
        out_specs=P(None, "row", ("chip", "core")),
        check_vma=False,
    )
```

```python
import functools

import jax
import jax.numpy as jnp
from jax import lax
from jax.experimental import pallas as pl
from jax.experimental.pallas import tpu as pltpu
from jax.sharding import Mesh
from jax.sharding import PartitionSpec as P

STEP = 8
TILE = 2 * STEP
TAPS = 3
PART = 4
WINDOWS = TAPS + 2
GROUP = TAPS * STEP
OUTSIDE = -1e30


def kernel(
    n_row,
    n_chip,
    mine,
    other,
    weights,
    out,
    conv_weight,
    mix_weight,
    row_proj,
    col_proj,
    base,
    sides,
    result,
    staged,
    sems,
):
    depth = 2 * mine.shape[1]
    row_weight = weights.at[pl.ds(0, depth)]
    col_weight = weights.at[pl.ds(depth, depth)]
    pair_weight = weights.at[pl.ds(2 * depth, out.shape[0])]
    f32, bf16 = jnp.float32, jnp.bfloat16
    row, chip, core = (lax.axis_index(name) for name in ("row", "chip", "core"))
    channels, n_rows, n_cols = out.shape

    span = conv_weight.shape[1]

    def block(at):
        cells = weights[pl.ds(2 * depth + (1 + at) * channels, channels), :span]
        return cells.astype(f32)

    taps = [[block(a * TAPS + b) for b in range(TAPS)] for a in range(TAPS)]
    mixing = block(TAPS * TAPS)
    for m in range(TAPS):
        for b in range(TAPS):
            moved = [pltpu.roll(taps[a][b], (m + a) * channels, 1) for a in range(TAPS)]
            rows = pl.ds((b * TAPS + m) * channels, channels)
            conv_weight[rows, :] = (moved[0] + moved[1] + moved[2]).astype(bf16)
        moved = pltpu.roll(mixing, m * channels, 1) if m else mixing
        mix_weight[pl.ds(m * channels, channels), :] = moved.astype(bf16)

    tiles = n_cols // TILE + 1
    zero = jnp.zeros((), bf16)

    def projected(start, size, weight):
        ends = (jnp.maximum(start - TILE, 0), jnp.minimum(start + size, mine.shape[0] - TILE))
        spans = [pl.ds(pl.multiple_of(start, TILE), size)]
        spans += [pl.ds(pl.multiple_of(end, TILE), TILE) for end in ends]
        halves = [jnp.concatenate([half[rows] for rows in spans], axis=0) for half in (mine, other)]
        cells = jnp.concatenate(
            [jnp.where(core == k, halves[0], halves[1]) for k in range(2)], axis=1
        )
        cells = jnp.dot(cells, weight[...], preferred_element_type=f32).astype(bf16).astype(f32)
        return cells[:size], cells[size + STEP : size + TILE], cells[size + TILE : size + TILE + STEP]

    width = row_proj.shape[1]

    cells, left, right = projected((chip * 2 + core) * n_cols, n_cols, col_weight)
    col_proj[:n_cols, :] = cells.astype(bf16)
    left = jnp.where((chip == 0) & (core == 0), OUTSIDE, left)
    right = jnp.where((chip == n_chip - 1) & (core == 1), OUTSIDE, right)
    col_proj[n_cols:, :] = jnp.concatenate([right, left], axis=0).astype(bf16)

    cells, left, right = projected(row * n_rows, n_rows, row_weight)
    row_proj[:STEP, :] = jnp.where(row == 0, OUTSIDE, left)
    row_proj[STEP : STEP + n_rows, :] = cells
    row_proj[STEP + n_rows : TILE + n_rows, :] = jnp.where(row == n_row - 1, OUTSIDE, right)

    lane = lax.broadcasted_iota(jnp.int32, (1, n_cols), 1)
    transposed = (((1,), (1,)), ((), ()))

    def pair_cells(acts):
        act = jnp.concatenate(acts, axis=0)
        hidden = lax.dot_general(pair_weight[...], act, transposed, preferred_element_type=f32)
        return hidden.astype(bf16)

    def pair_acts(rows, outer):
        inner = []
        for k in range(PART):
            spread = jnp.broadcast_to(rows[k : k + 1], (TILE, width)).astype(bf16)
            cells = col_proj[...].reshape(tiles, TILE, width) + spread[None]
            act = jnp.maximum(cells, zero)
            inner.append(act[:-1].reshape(n_cols, width))
            outer.append(act[-1])
        return inner

    def pair_rows(rows, outer):
        hidden, acts = [], None
        for low in range(0, rows.shape[0], PART):
            ahead_acts = pair_acts(rows[low : low + PART], outer)
            if acts is not None:
                hidden.append(pair_cells(acts))
            acts = ahead_acts
        if acts is not None:
            hidden.append(pair_cells(acts))
        return hidden

    def put_rows(start, hidden):
        for n, cells in enumerate(hidden):
            for k in range(PART):
                base[start + n * PART + k] = cells[:, k * n_cols : (k + 1) * n_cols]

    def put_sides(start, cells):
        for k in range(cells.shape[1] // n_cols):
            sides[start // STEP + k] = cells[:, k * n_cols : (k + 1) * n_cols]

    reach = TAPS * channels
    pitch = channels + STEP
    fill = [jnp.zeros((span - WINDOWS * channels, n_cols), bf16)]

    def conv_cells(blocks):
        cells = [jnp.concatenate(windows + fill, axis=0) for windows in blocks]
        cells = jnp.maximum(jnp.concatenate(cells, axis=1), zero)
        return jnp.dot(conv_weight[...], cells, preferred_element_type=f32)

    def conv_ends(groups):
        parts = conv_cells([[sides[at * TAPS + m] for m in range(WINDOWS)] for at in groups])
        ends = []
        for n in range(len(groups)):
            part = parts[:, n * n_cols : (n + 1) * n_cols]
            ends.append(jnp.where(lane % TILE >= STEP, part[:reach], part[2 * reach :]))
        return ends

    def conv_parts(at, low):
        places = [at * GROUP + p for p in range(low, low + PART)]
        return conv_cells([[base[p + STEP * m] for m in range(WINDOWS)] for p in places])

    def shifted(parts, ends, low):
        mids = []
        for k in range(PART):
            here = parts[:, k * n_cols : (k + 1) * n_cols]
            end = pltpu.roll(ends, (n_cols - STEP - (low + k) * TILE) % n_cols, 1)
            left = jnp.where(lane < STEP, end, pltpu.roll(here[:reach], STEP, 1))
            right = pltpu.roll(here[2 * reach :], n_cols - STEP, 1)
            right = jnp.where(lane >= n_cols - STEP, end, right)
            total = here[reach : 2 * reach] + left + right
            mids.append(jnp.maximum(total, 0.0).astype(bf16))
        return jnp.concatenate(mids, axis=1)

    def mixed_rows(at, low, mid):
        mixed = jnp.dot(mix_weight[:, :reach], mid, preferred_element_type=f32)
        for k in range(PART):
            for m in range(TAPS):
                row_at = at * GROUP + low + k + STEP * m
                here = mixed[m * channels : (m + 1) * channels, k * n_cols : (k + 1) * n_cols]
                here = here + base[row_at + STEP].astype(f32)
                result[pl.ds(pl.multiple_of(row_at * pitch, STEP), channels), :] = here

    def turn_rows(start, count):
        start = pl.multiple_of(start, TILE)
        for o in range(channels):
            cells = result[pl.ds(start * pitch + o, count, stride=pitch), :]
            staged[o, pl.ds(start, count), :] = cells.astype(bf16)

    def to_out(start, count, sem):
        rows = pl.ds(pl.multiple_of(start, TILE), count)
        return pltpu.make_async_copy(staged.at[:, rows], out.at[:, rows], sem)

    per_step = 2 * GROUP
    steps = n_rows // per_step - 1
    ahead = per_step + TILE
    outer = []
    put_rows(0, pair_rows(row_proj[:ahead, :], outer))
    put_sides(0, pair_cells(outer))

    def rounds(groups, start, count, turn):
        ends = conv_ends(groups)
        places = [(n, low) for n in range(len(groups)) for low in range(0, STEP, PART)]
        share = -(-count // (PART * len(places))) * PART
        hidden, outer, mid = [], [], None
        rows = row_proj[pl.ds(pl.multiple_of(start, STEP), count), :]
        for n, (group, low) in enumerate(places):
            parts = conv_parts(groups[group], low)
            if n == 0:
                turn()
            hidden += pair_rows(rows[n * share : (n + 1) * share], outer)
            if n:
                mixed_rows(groups[places[n - 1][0]], places[n - 1][1], mid)
            mid = shifted(parts, ends[group], low)
        outer = pair_cells(outer)
        mixed_rows(groups[-1], places[-1][1], mid)
        put_rows(start, hidden)
        put_sides(start, outer)

    def step(at, _):
        before = jnp.maximum(at - 1, 0)
        rounds(
            (2 * at, 2 * at + 1),
            at * per_step + ahead,
            per_step,
            lambda: turn_rows(before * per_step, per_step),
        )

        @pl.when(at > 0)
        def _send():
            to_out(before * per_step, per_step, sems.at[before]).start()

        return _

    spare = pl.ds(n_rows + TILE, STEP)
    base[spare] = jnp.zeros_like(base[spare])
    sides[(n_rows + TILE) // STEP] = jnp.zeros_like(sides[0])
    lax.fori_loop(0, steps, step, 0)

    done = steps * per_step
    rounds(
        (2 * steps, 2 * steps + 1),
        done + ahead,
        TILE,
        lambda: turn_rows(done - per_step, per_step),
    )
    to_out(done - per_step, per_step, sems.at[steps - 1]).start()
    at = 2 * steps + 2
    (ends,) = conv_ends((at,))
    lows = range(0, STEP, PART)
    parts = [conv_parts(at, low) for low in lows]
    turn_rows(done, per_step)
    to_out(done, per_step, sems.at[steps]).start()
    for low, part in zip(lows, parts):
        mixed_rows(at, low, shifted(part, ends, low))
    done += per_step
    turn_rows(done, n_rows - done)
    last = to_out(done, n_rows - done, sems.at[steps + 1])
    last.start()
    for at in range(steps + 1):
        to_out(at * per_step, per_step, sems.at[at]).wait()
    last.wait()


def on_device(trunk, row_weight, column_weight, pair_map_weight, dilated_weight, mixing_weight):
    n_row, n_chip = lax.axis_size("row"), lax.axis_size("chip")
    shard, depth = trunk.shape
    n_rows, n_cols = shard * n_chip * 2, shard * n_row
    channels = pair_map_weight.shape[1]
    width = row_weight.shape[1]
    small = jnp.concatenate([dilated_weight.reshape(-1, channels), mixing_weight], axis=0)
    small = jnp.pad(small, ((0, 0), (0, width - channels)))
    weights = jnp.concatenate([row_weight, column_weight, pair_map_weight.T, small], axis=0)

    half = depth // 2
    to = lax.broadcasted_iota(jnp.int32, (n_row * n_chip * 2, shard, half), 0)
    copies = jnp.where(to % 2 == 0, trunk[None, :, :half], trunk[None, :, half:])
    mine = lax.all_to_all(copies, ("row", "chip", "core"), 0, 0).reshape(-1, half)
    other = lax.ppermute(mine, "core", [(0, 1), (1, 0)])
    span = -(-WINDOWS * channels // n_cols) * n_cols
    groups = -(-n_rows // GROUP)
    padded = groups * GROUP + TILE
    return pl.pallas_call(
        functools.partial(kernel, n_row, n_chip),
        out_shape=jax.ShapeDtypeStruct((channels, n_rows, n_cols), jnp.bfloat16),
        out_specs=pl.BlockSpec(memory_space=pl.ANY),
        scratch_shapes=[
            pltpu.VMEM((TAPS * TAPS * channels, span), jnp.bfloat16),
            pltpu.VMEM((TAPS * channels, span), jnp.bfloat16),
            pltpu.VMEM((n_rows + TILE, width), jnp.float32),
            pltpu.VMEM((n_cols + TILE, width), jnp.bfloat16),
            pltpu.VMEM((padded, channels, n_cols), jnp.bfloat16),
            pltpu.VMEM((padded // STEP, channels, n_cols), jnp.bfloat16),
            pltpu.VMEM((groups * GROUP * (channels + STEP), n_cols), jnp.float32),
            pltpu.VMEM((channels, n_rows, n_cols), jnp.bfloat16),
            pltpu.SemaphoreType.DMA((n_rows // (2 * GROUP) + 1,)),
        ],
        compiler_params=pltpu.CompilerParams(vmem_limit_bytes=52 * 2**20),
        name="pair_block",
    )(mine, other, weights)


def solution(mesh):
    n_row, n_col = mesh.devices.shape
    chips = Mesh(mesh.devices.reshape(n_row, n_col // 2, 2), ("row", "chip", "core"))
    return jax.shard_map(
        on_device,
        mesh=chips,
        in_specs=(P(("row", "chip", "core"), None), P(), P(), P(), P(), P()),
        out_specs=P(None, "row", ("chip", "core")),
        check_vma=False,
    )
```

```python
import functools

import jax
import jax.numpy as jnp
from jax import lax
from jax.experimental import pallas as pl
from jax.experimental.pallas import tpu as pltpu
from jax.sharding import Mesh
from jax.sharding import PartitionSpec as P

STEP = 8
TILE = 2 * STEP
TAPS = 3
PART = 4
WINDOWS = TAPS + 2
GROUP = TAPS * STEP
OUTSIDE = -1e30


def kernel(
    n_row,
    n_chip,
    mine,
    other,
    weights,
    out,
    conv_weight,
    mix_weight,
    row_proj,
    col_proj,
    base,
    sides,
    result,
    staged,
    sems,
):
    depth = 2 * mine.shape[1]
    row_weight = weights.at[pl.ds(0, depth)]
    col_weight = weights.at[pl.ds(depth, depth)]
    pair_weight = weights.at[pl.ds(2 * depth, out.shape[0])]
    f32, bf16 = jnp.float32, jnp.bfloat16
    row, chip, core = (lax.axis_index(name) for name in ("row", "chip", "core"))
    channels, n_rows, n_cols = out.shape

    span = conv_weight.shape[1]

    def block(at):
        cells = weights[pl.ds(2 * depth + (1 + at) * channels, channels), :span]
        return cells.astype(f32)

    taps = [[block(a * TAPS + b) for b in range(TAPS)] for a in range(TAPS)]
    mixing = block(TAPS * TAPS)
    for m in range(TAPS):
        for b in range(TAPS):
            moved = [pltpu.roll(taps[a][b], (m + a) * channels, 1) for a in range(TAPS)]
            rows = pl.ds((b * TAPS + m) * channels, channels)
            conv_weight[rows, :] = (moved[0] + moved[1] + moved[2]).astype(bf16)
        moved = pltpu.roll(mixing, m * channels, 1) if m else mixing
        mix_weight[pl.ds(m * channels, channels), :] = moved.astype(bf16)

    tiles = n_cols // TILE + 1
    zero = jnp.zeros((), bf16)

    def projected(start, size, weight):
        ends = (jnp.maximum(start - TILE, 0), jnp.minimum(start + size, mine.shape[0] - TILE))
        spans = [pl.ds(pl.multiple_of(start, TILE), size)]
        spans += [pl.ds(pl.multiple_of(end, TILE), TILE) for end in ends]
        halves = [jnp.concatenate([half[rows] for rows in spans], axis=0) for half in (mine, other)]
        cells = jnp.concatenate(
            [jnp.where(core == k, halves[0], halves[1]) for k in range(2)], axis=1
        )
        cells = jnp.dot(cells, weight[...], preferred_element_type=f32).astype(bf16).astype(f32)
        return cells[:size], cells[size + STEP : size + TILE], cells[size + TILE : size + TILE + STEP]

    width = row_proj.shape[1]

    cells, left, right = projected((chip * 2 + core) * n_cols, n_cols, col_weight)
    col_proj[:n_cols, :] = cells.astype(bf16)
    left = jnp.where((chip == 0) & (core == 0), OUTSIDE, left)
    right = jnp.where((chip == n_chip - 1) & (core == 1), OUTSIDE, right)
    col_proj[n_cols:, :] = jnp.concatenate([right, left], axis=0).astype(bf16)

    cells, left, right = projected(row * n_rows, n_rows, row_weight)
    row_proj[:STEP, :] = jnp.where(row == 0, OUTSIDE, left)
    row_proj[STEP : STEP + n_rows, :] = cells
    row_proj[STEP + n_rows : TILE + n_rows, :] = jnp.where(row == n_row - 1, OUTSIDE, right)

    lane = lax.broadcasted_iota(jnp.int32, (1, n_cols), 1)
    transposed = (((1,), (1,)), ((), ()))

    def pair_cells(acts):
        act = jnp.concatenate(acts, axis=0)
        hidden = lax.dot_general(pair_weight[...], act, transposed, preferred_element_type=f32)
        return hidden.astype(bf16)

    def pair_acts(rows, outer):
        inner = []
        for k in range(PART):
            spread = jnp.broadcast_to(rows[k : k + 1], (TILE, width)).astype(bf16)
            cells = col_proj[...].reshape(tiles, TILE, width) + spread[None]
            act = jnp.maximum(cells, zero)
            inner.append(act[:-1].reshape(n_cols, width))
            outer.append(act[-1])
        return inner

    def pair_rows(rows, outer):
        hidden, acts = [], None
        for low in range(0, rows.shape[0], PART):
            ahead_acts = pair_acts(rows[low : low + PART], outer)
            if acts is not None:
                hidden.append(pair_cells(acts))
            acts = ahead_acts
        if acts is not None:
            hidden.append(pair_cells(acts))
        return hidden

    def put_rows(start, hidden):
        for n, cells in enumerate(hidden):
            for k in range(PART):
                base[start + n * PART + k] = cells[:, k * n_cols : (k + 1) * n_cols]

    def put_sides(start, cells):
        for k in range(cells.shape[1] // n_cols):
            sides[start // STEP + k] = cells[:, k * n_cols : (k + 1) * n_cols]

    reach = TAPS * channels
    pitch = channels + STEP
    fill = [jnp.zeros((span - WINDOWS * channels, n_cols), bf16)]

    def conv_cells(blocks):
        cells = [jnp.concatenate(windows + fill, axis=0) for windows in blocks]
        cells = jnp.maximum(jnp.concatenate(cells, axis=1), zero)
        return jnp.dot(conv_weight[...], cells, preferred_element_type=f32)

    def conv_ends(groups):
        parts = conv_cells([[sides[at * TAPS + m] for m in range(WINDOWS)] for at in groups])
        ends = []
        for n in range(len(groups)):
            part = parts[:, n * n_cols : (n + 1) * n_cols]
            ends.append(jnp.where(lane % TILE >= STEP, part[:reach], part[2 * reach :]))
        return ends

    def conv_parts(at, low):
        places = [at * GROUP + p for p in range(low, low + PART)]
        return conv_cells([[base[p + STEP * m] for m in range(WINDOWS)] for p in places])

    def shifted(parts, ends, low):
        mids = []
        for k in range(PART):
            here = parts[:, k * n_cols : (k + 1) * n_cols]
            end = pltpu.roll(ends, (n_cols - STEP - (low + k) * TILE) % n_cols, 1)
            left = jnp.where(lane < STEP, end, pltpu.roll(here[:reach], STEP, 1))
            right = pltpu.roll(here[2 * reach :], n_cols - STEP, 1)
            right = jnp.where(lane >= n_cols - STEP, end, right)
            total = here[reach : 2 * reach] + left + right
            mids.append(jnp.maximum(total, 0.0).astype(bf16))
        return jnp.concatenate(mids, axis=1)

    def mixed_rows(at, low, mid):
        mixed = jnp.dot(mix_weight[:, :reach], mid, preferred_element_type=f32)
        for k in range(PART):
            for m in range(TAPS):
                row_at = at * GROUP + low + k + STEP * m
                here = mixed[m * channels : (m + 1) * channels, k * n_cols : (k + 1) * n_cols]
                here = here + base[row_at + STEP].astype(f32)
                result[pl.ds(pl.multiple_of(row_at * pitch, STEP), channels), :] = here

    def turn_rows(start, count):
        start = pl.multiple_of(start, TILE)
        for o in range(channels):
            cells = result[pl.ds(start * pitch + o, count, stride=pitch), :]
            staged[o, pl.ds(start, count), :] = cells.astype(bf16)

    def to_out(start, count, sem):
        rows = pl.ds(pl.multiple_of(start, TILE), count)
        return pltpu.make_async_copy(staged.at[:, rows], out.at[:, rows], sem)

    per_step = 2 * GROUP
    steps = n_rows // per_step - 1
    ahead = per_step + TILE
    outer = []
    put_rows(0, pair_rows(row_proj[:ahead, :], outer))
    put_sides(0, pair_cells(outer))

    def rounds(groups, start, count, turn):
        ends = conv_ends(groups)
        places = [(n, low) for n in range(len(groups)) for low in range(0, STEP, PART)]
        hidden, outer, waiting = [], [], []
        rows = row_proj[pl.ds(pl.multiple_of(start, STEP), count), :]
        chunks = [rows[k : k + PART] for k in range(0, count, PART)]

        def feed():
            if chunks:
                waiting.append(pair_acts(chunks.pop(0), outer))
            if len(waiting) > 1 or (waiting and not chunks):
                hidden.append(pair_cells(waiting.pop(0)))

        for n, (group, low) in enumerate(places):
            parts = conv_parts(groups[group], low)
            if n == 0:
                turn()
            feed()
            mid = shifted(parts, ends[group], low)
            feed()
            mixed_rows(groups[group], low, mid)
            feed()
        while chunks or waiting:
            feed()
        outer = pair_cells(outer)
        put_rows(start, hidden)
        put_sides(start, outer)

    def step(at, _):
        before = jnp.maximum(at - 1, 0)
        rounds(
            (2 * at, 2 * at + 1),
            at * per_step + ahead,
            per_step,
            lambda: turn_rows(before * per_step, per_step),
        )

        @pl.when(at > 0)
        def _send():
            to_out(before * per_step, per_step, sems.at[before]).start()

        return _

    spare = pl.ds(n_rows + TILE, STEP)
    base[spare] = jnp.zeros_like(base[spare])
    sides[(n_rows + TILE) // STEP] = jnp.zeros_like(sides[0])
    lax.fori_loop(0, steps, step, 0)

    done = steps * per_step
    rounds(
        (2 * steps, 2 * steps + 1),
        done + ahead,
        TILE,
        lambda: turn_rows(done - per_step, per_step),
    )
    to_out(done - per_step, per_step, sems.at[steps - 1]).start()
    at = 2 * steps + 2
    (ends,) = conv_ends((at,))
    lows = range(0, STEP, PART)
    parts = [conv_parts(at, low) for low in lows]
    turn_rows(done, per_step)
    to_out(done, per_step, sems.at[steps]).start()
    for low, part in zip(lows, parts):
        mixed_rows(at, low, shifted(part, ends, low))
    done += per_step
    turn_rows(done, n_rows - done)
    last = to_out(done, n_rows - done, sems.at[steps + 1])
    last.start()
    for at in range(steps + 1):
        to_out(at * per_step, per_step, sems.at[at]).wait()
    last.wait()


def on_device(trunk, row_weight, column_weight, pair_map_weight, dilated_weight, mixing_weight):
    n_row, n_chip = lax.axis_size("row"), lax.axis_size("chip")
    shard, depth = trunk.shape
    n_rows, n_cols = shard * n_chip * 2, shard * n_row
    channels = pair_map_weight.shape[1]
    width = row_weight.shape[1]
    small = jnp.concatenate([dilated_weight.reshape(-1, channels), mixing_weight], axis=0)
    small = jnp.pad(small, ((0, 0), (0, width - channels)))
    weights = jnp.concatenate([row_weight, column_weight, pair_map_weight.T, small], axis=0)

    half = depth // 2
    to = lax.broadcasted_iota(jnp.int32, (n_row * n_chip * 2, shard, half), 0)
    copies = jnp.where(to % 2 == 0, trunk[None, :, :half], trunk[None, :, half:])
    mine = lax.all_to_all(copies, ("row", "chip", "core"), 0, 0).reshape(-1, half)
    other = lax.ppermute(mine, "core", [(0, 1), (1, 0)])
    span = -(-WINDOWS * channels // n_cols) * n_cols
    groups = -(-n_rows // GROUP)
    padded = groups * GROUP + TILE
    return pl.pallas_call(
        functools.partial(kernel, n_row, n_chip),
        out_shape=jax.ShapeDtypeStruct((channels, n_rows, n_cols), jnp.bfloat16),
        out_specs=pl.BlockSpec(memory_space=pl.ANY),
        scratch_shapes=[
            pltpu.VMEM((TAPS * TAPS * channels, span), jnp.bfloat16),
            pltpu.VMEM((TAPS * channels, span), jnp.bfloat16),
            pltpu.VMEM((n_rows + TILE, width), jnp.float32),
            pltpu.VMEM((n_cols + TILE, width), jnp.bfloat16),
            pltpu.VMEM((padded, channels, n_cols), jnp.bfloat16),
            pltpu.VMEM((padded // STEP, channels, n_cols), jnp.bfloat16),
            pltpu.VMEM((groups * GROUP * (channels + STEP), n_cols), jnp.float32),
            pltpu.VMEM((channels, n_rows, n_cols), jnp.bfloat16),
            pltpu.SemaphoreType.DMA((n_rows // (2 * GROUP) + 1,)),
        ],
        compiler_params=pltpu.CompilerParams(vmem_limit_bytes=52 * 2**20),
        name="pair_block",
    )(mine, other, weights)


def solution(mesh):
    n_row, n_col = mesh.devices.shape
    chips = Mesh(mesh.devices.reshape(n_row, n_col // 2, 2), ("row", "chip", "core"))
    return jax.shard_map(
        on_device,
        mesh=chips,
        in_specs=(P(("row", "chip", "core"), None), P(), P(), P(), P(), P()),
        out_specs=P(None, "row", ("chip", "core")),
        check_vma=False,
    )
```

```python
import functools

import jax
import jax.numpy as jnp
from jax import lax
from jax.experimental import pallas as pl
from jax.experimental.pallas import tpu as pltpu
from jax.sharding import Mesh
from jax.sharding import PartitionSpec as P

STEP = 8
TILE = 2 * STEP
TAPS = 3
PART = 4
WINDOWS = TAPS + 2
GROUP = TAPS * STEP
OUTSIDE = -1e30


def kernel(
    n_row,
    n_chip,
    mine,
    other,
    weights,
    out,
    conv_weight,
    mix_weight,
    row_proj,
    col_proj,
    base,
    sides,
    result,
    staged,
    sems,
):
    depth = 2 * mine.shape[1]
    row_weight = weights.at[pl.ds(0, depth)]
    col_weight = weights.at[pl.ds(depth, depth)]
    pair_weight = weights.at[pl.ds(2 * depth, out.shape[0])]
    f32, bf16 = jnp.float32, jnp.bfloat16
    row, chip, core = (lax.axis_index(name) for name in ("row", "chip", "core"))
    channels, n_rows, n_cols = out.shape

    span = conv_weight.shape[1]

    def block(at):
        cells = weights[pl.ds(2 * depth + (1 + at) * channels, channels), :span]
        return cells.astype(f32)

    taps = [[block(a * TAPS + b) for b in range(TAPS)] for a in range(TAPS)]
    mixing = block(TAPS * TAPS)
    for m in range(TAPS):
        for b in range(TAPS):
            moved = [pltpu.roll(taps[a][b], (m + a) * channels, 1) for a in range(TAPS)]
            rows = pl.ds((b * TAPS + m) * channels, channels)
            conv_weight[rows, :] = (moved[0] + moved[1] + moved[2]).astype(bf16)
        moved = pltpu.roll(mixing, m * channels, 1) if m else mixing
        mix_weight[pl.ds(m * channels, channels), :] = moved.astype(bf16)

    tiles = n_cols // TILE + 1
    zero = jnp.zeros((), bf16)

    def projected(start, size, weight):
        ends = (jnp.maximum(start - TILE, 0), jnp.minimum(start + size, mine.shape[0] - TILE))
        spans = [pl.ds(pl.multiple_of(start, TILE), size)]
        spans += [pl.ds(pl.multiple_of(end, TILE), TILE) for end in ends]
        halves = [jnp.concatenate([half[rows] for rows in spans], axis=0) for half in (mine, other)]
        cells = jnp.concatenate(
            [jnp.where(core == k, halves[0], halves[1]) for k in range(2)], axis=1
        )
        cells = jnp.dot(cells, weight[...], preferred_element_type=f32).astype(bf16).astype(f32)
        return cells[:size], cells[size + STEP : size + TILE], cells[size + TILE : size + TILE + STEP]

    width = row_proj.shape[1]

    cells, left, right = projected((chip * 2 + core) * n_cols, n_cols, col_weight)
    col_proj[:n_cols, :] = cells.astype(bf16)
    left = jnp.where((chip == 0) & (core == 0), OUTSIDE, left)
    right = jnp.where((chip == n_chip - 1) & (core == 1), OUTSIDE, right)
    col_proj[n_cols:, :] = jnp.concatenate([right, left], axis=0).astype(bf16)

    cells, left, right = projected(row * n_rows, n_rows, row_weight)
    row_proj[:STEP, :] = jnp.where(row == 0, OUTSIDE, left)
    row_proj[STEP : STEP + n_rows, :] = cells
    row_proj[STEP + n_rows : TILE + n_rows, :] = jnp.where(row == n_row - 1, OUTSIDE, right)

    lane = lax.broadcasted_iota(jnp.int32, (1, n_cols), 1)
    transposed = (((1,), (1,)), ((), ()))

    def pair_cells(acts):
        act = jnp.concatenate(acts, axis=0)
        return lax.dot_general(pair_weight[...], act, transposed, preferred_element_type=f32)

    def pair_acts(rows, outer):
        inner = []
        for k in range(PART):
            spread = jnp.broadcast_to(rows[k : k + 1], (TILE, width)).astype(bf16)
            cells = col_proj[...].reshape(tiles, TILE, width) + spread[None]
            act = jnp.maximum(cells, zero)
            inner.append(act[:-1].reshape(n_cols, width))
            outer.append(act[-1])
        return inner

    def pair_stream(rows):
        chunks = [rows[low : low + PART] for low in range(0, rows.shape[0], PART)]
        acts, raw, hidden, outer = [], [], [], []

        def feed():
            if chunks:
                acts.append(pair_acts(chunks.pop(0), outer))
            if len(acts) > 1 or (acts and not chunks):
                raw.append(pair_cells(acts.pop(0)))
            if len(raw) > 1 or (raw and not chunks and not acts):
                hidden.append(raw.pop(0).astype(bf16))

        def finish():
            while chunks or acts:
                feed()
            ends = pair_cells(outer)
            while raw:
                feed()
            return hidden, ends.astype(bf16)

        return feed, finish

    def put_rows(start, hidden):
        for n, cells in enumerate(hidden):
            for k in range(PART):
                base[start + n * PART + k] = cells[:, k * n_cols : (k + 1) * n_cols]

    def put_sides(start, cells):
        for k in range(cells.shape[1] // n_cols):
            sides[start // STEP + k] = cells[:, k * n_cols : (k + 1) * n_cols]

    reach = TAPS * channels
    pitch = channels + STEP
    fill = [jnp.zeros((span - WINDOWS * channels, n_cols), bf16)]

    def conv_cells(blocks):
        cells = [jnp.concatenate(windows + fill, axis=0) for windows in blocks]
        cells = jnp.maximum(jnp.concatenate(cells, axis=1), zero)
        return jnp.dot(conv_weight[...], cells, preferred_element_type=f32)

    def conv_sides(groups):
        return conv_cells([[sides[at * TAPS + m] for m in range(WINDOWS)] for at in groups])

    def ends_of(parts):
        ends = []
        for low in range(0, parts.shape[1], n_cols):
            part = parts[:, low : low + n_cols]
            ends.append(jnp.where(lane % TILE >= STEP, part[:reach], part[2 * reach :]))
        return ends

    def conv_parts(at, low):
        places = [at * GROUP + p for p in range(low, low + PART)]
        return conv_cells([[base[p + STEP * m] for m in range(WINDOWS)] for p in places])

    def shifted(parts, ends, low):
        mids = []
        for k in range(PART):
            here = parts[:, k * n_cols : (k + 1) * n_cols]
            end = pltpu.roll(ends, (n_cols - STEP - (low + k) * TILE) % n_cols, 1)
            left = jnp.where(lane < STEP, end, pltpu.roll(here[:reach], STEP, 1))
            right = pltpu.roll(here[2 * reach :], n_cols - STEP, 1)
            right = jnp.where(lane >= n_cols - STEP, end, right)
            total = here[reach : 2 * reach] + left + right
            mids.append(jnp.maximum(total, 0.0).astype(bf16))
        return jnp.concatenate(mids, axis=1)

    def mix(mid):
        return jnp.dot(mix_weight[:, :reach], mid, preferred_element_type=f32)

    def put_mixed(at, low, mixed):
        for k in range(PART):
            for m in range(TAPS):
                row_at = at * GROUP + low + k + STEP * m
                here = mixed[m * channels : (m + 1) * channels, k * n_cols : (k + 1) * n_cols]
                here = here + base[row_at + STEP].astype(f32)
                result[pl.ds(pl.multiple_of(row_at * pitch, STEP), channels), :] = here

    def turn_rows(start, count):
        start = pl.multiple_of(start, TILE)
        for o in range(channels):
            cells = result[pl.ds(start * pitch + o, count, stride=pitch), :]
            staged[o, pl.ds(start, count), :] = cells.astype(bf16)

    def to_out(start, count, sem):
        rows = pl.ds(pl.multiple_of(start, TILE), count)
        return pltpu.make_async_copy(staged.at[:, rows], out.at[:, rows], sem)

    per_step = 2 * GROUP
    steps = n_rows // per_step - 1
    ahead = per_step + TILE
    hidden, ends = pair_stream(row_proj[:ahead, :])[1]()
    put_rows(0, hidden)
    put_sides(0, ends)

    def rounds(groups, start, count, turn):
        feed, finish = pair_stream(row_proj[pl.ds(pl.multiple_of(start, STEP), count), :])
        side_parts = conv_sides(groups)
        places = [(at, n, low) for n, at in enumerate(groups) for low in range(0, STEP, PART)]
        before = ends = None
        for at, n, low in places:
            parts = conv_parts(at, low)
            if before is None:
                turn()
                ends = ends_of(side_parts)
            feed()
            if before is not None:
                mixed = mix(before[2])
            feed()
            if before is not None:
                put_mixed(before[0], before[1], mixed)
            feed()
            before = (at, low, shifted(parts, ends[n], low))
        mixed = mix(before[2])
        hidden, ends = finish()
        put_mixed(before[0], before[1], mixed)
        put_rows(start, hidden)
        put_sides(start, ends)

    def step(at, _):
        before = jnp.maximum(at - 1, 0)
        rounds(
            (2 * at, 2 * at + 1),
            at * per_step + ahead,
            per_step,
            lambda: turn_rows(before * per_step, per_step),
        )

        @pl.when(at > 0)
        def _send():
            to_out(before * per_step, per_step, sems.at[before]).start()

        return _

    spare = pl.ds(n_rows + TILE, STEP)
    base[spare] = jnp.zeros_like(base[spare])
    sides[(n_rows + TILE) // STEP] = jnp.zeros_like(sides[0])
    lax.fori_loop(0, steps, step, 0)

    done = steps * per_step
    rounds(
        (2 * steps, 2 * steps + 1),
        done + ahead,
        TILE,
        lambda: turn_rows(done - per_step, per_step),
    )
    to_out(done - per_step, per_step, sems.at[steps - 1]).start()
    at = 2 * steps + 2
    lows = range(0, STEP, PART)
    side_parts = conv_sides((at,))
    parts = [conv_parts(at, low) for low in lows]
    turn_rows(done, per_step)
    to_out(done, per_step, sems.at[steps]).start()
    (ends,) = ends_of(side_parts)
    mids = [shifted(part, ends, low) for low, part in zip(lows, parts)]
    mixed = [mix(mid) for mid in mids]
    for low, cells in zip(lows, mixed):
        put_mixed(at, low, cells)
    done += per_step
    turn_rows(done, n_rows - done)
    last = to_out(done, n_rows - done, sems.at[steps + 1])
    last.start()
    for at in range(steps + 1):
        to_out(at * per_step, per_step, sems.at[at]).wait()
    last.wait()


def on_device(trunk, row_weight, column_weight, pair_map_weight, dilated_weight, mixing_weight):
    n_row, n_chip = lax.axis_size("row"), lax.axis_size("chip")
    shard, depth = trunk.shape
    n_rows, n_cols = shard * n_chip * 2, shard * n_row
    channels = pair_map_weight.shape[1]
    width = row_weight.shape[1]
    small = jnp.concatenate([dilated_weight.reshape(-1, channels), mixing_weight], axis=0)
    small = jnp.pad(small, ((0, 0), (0, width - channels)))
    weights = jnp.concatenate([row_weight, column_weight, pair_map_weight.T, small], axis=0)

    half = depth // 2
    to = lax.broadcasted_iota(jnp.int32, (n_row * n_chip * 2, shard, half), 0)
    copies = jnp.where(to % 2 == 0, trunk[None, :, :half], trunk[None, :, half:])
    mine = lax.all_to_all(copies, ("row", "chip", "core"), 0, 0).reshape(-1, half)
    other = lax.ppermute(mine, "core", [(0, 1), (1, 0)])
    span = -(-WINDOWS * channels // n_cols) * n_cols
    groups = -(-n_rows // GROUP)
    padded = groups * GROUP + TILE
    return pl.pallas_call(
        functools.partial(kernel, n_row, n_chip),
        out_shape=jax.ShapeDtypeStruct((channels, n_rows, n_cols), jnp.bfloat16),
        out_specs=pl.BlockSpec(memory_space=pl.ANY),
        scratch_shapes=[
            pltpu.VMEM((TAPS * TAPS * channels, span), jnp.bfloat16),
            pltpu.VMEM((TAPS * channels, span), jnp.bfloat16),
            pltpu.VMEM((n_rows + TILE, width), jnp.float32),
            pltpu.VMEM((n_cols + TILE, width), jnp.bfloat16),
            pltpu.VMEM((padded, channels, n_cols), jnp.bfloat16),
            pltpu.VMEM((padded // STEP, channels, n_cols), jnp.bfloat16),
            pltpu.VMEM((groups * GROUP * (channels + STEP), n_cols), jnp.float32),
            pltpu.VMEM((channels, n_rows, n_cols), jnp.bfloat16),
            pltpu.SemaphoreType.DMA((n_rows // (2 * GROUP) + 1,)),
        ],
        compiler_params=pltpu.CompilerParams(vmem_limit_bytes=52 * 2**20),
        name="pair_block",
    )(mine, other, weights)


def solution(mesh):
    n_row, n_col = mesh.devices.shape
    chips = Mesh(mesh.devices.reshape(n_row, n_col // 2, 2), ("row", "chip", "core"))
    return jax.shard_map(
        on_device,
        mesh=chips,
        in_specs=(P(("row", "chip", "core"), None), P(), P(), P(), P(), P()),
        out_specs=P(None, "row", ("chip", "core")),
        check_vma=False,
    )
```

```python
import functools

import jax
import jax.numpy as jnp
from jax import lax
from jax.experimental import pallas as pl
from jax.experimental.pallas import tpu as pltpu
from jax.sharding import Mesh
from jax.sharding import PartitionSpec as P

STEP = 8
TILE = 2 * STEP
TAPS = 3
PART = 4
WINDOWS = TAPS + 2
GROUP = TAPS * STEP
OUTSIDE = -1e30


def kernel(
    n_row,
    n_chip,
    mine,
    other,
    weights,
    out,
    conv_weight,
    mix_weight,
    row_proj,
    col_proj,
    base,
    sides,
    result,
    staged,
    sems,
):
    depth = 2 * mine.shape[1]
    row_weight = weights.at[pl.ds(0, depth)]
    col_weight = weights.at[pl.ds(depth, depth)]
    pair_weight = weights.at[pl.ds(2 * depth, out.shape[0])]
    f32, bf16 = jnp.float32, jnp.bfloat16
    row, chip, core = (lax.axis_index(name) for name in ("row", "chip", "core"))
    channels, n_rows, n_cols = out.shape

    span = conv_weight.shape[1]

    def block(at):
        cells = weights[pl.ds(2 * depth + (1 + at) * channels, channels), :span]
        return cells.astype(f32)

    taps = [[block(a * TAPS + b) for b in range(TAPS)] for a in range(TAPS)]
    mixing = block(TAPS * TAPS)
    for m in range(TAPS):
        for b in range(TAPS):
            moved = [pltpu.roll(taps[a][b], (m + a) * channels, 1) for a in range(TAPS)]
            rows = pl.ds((b * TAPS + m) * channels, channels)
            conv_weight[rows, :] = (moved[0] + moved[1] + moved[2]).astype(bf16)
        moved = pltpu.roll(mixing, m * channels, 1) if m else mixing
        mix_weight[pl.ds(m * channels, channels), :] = moved.astype(bf16)

    tiles = n_cols // TILE + 1
    zero = jnp.zeros((), bf16)

    def projected(start, size, weight):
        ends = (jnp.maximum(start - TILE, 0), jnp.minimum(start + size, mine.shape[0] - TILE))
        spans = [pl.ds(pl.multiple_of(start, TILE), size)]
        spans += [pl.ds(pl.multiple_of(end, TILE), TILE) for end in ends]
        halves = [jnp.concatenate([half[rows] for rows in spans], axis=0) for half in (mine, other)]
        cells = jnp.concatenate(
            [jnp.where(core == k, halves[0], halves[1]) for k in range(2)], axis=1
        )
        cells = jnp.dot(cells, weight[...], preferred_element_type=f32).astype(bf16).astype(f32)
        return cells[:size], cells[size + STEP : size + TILE], cells[size + TILE : size + TILE + STEP]

    width = row_proj.shape[1]

    cells, left, right = projected((chip * 2 + core) * n_cols, n_cols, col_weight)
    col_proj[:n_cols, :] = cells.astype(bf16)
    left = jnp.where((chip == 0) & (core == 0), OUTSIDE, left)
    right = jnp.where((chip == n_chip - 1) & (core == 1), OUTSIDE, right)
    col_proj[n_cols:, :] = jnp.concatenate([right, left], axis=0).astype(bf16)

    cells, left, right = projected(row * n_rows, n_rows, row_weight)
    row_proj[:STEP, :] = jnp.where(row == 0, OUTSIDE, left)
    row_proj[STEP : STEP + n_rows, :] = cells
    row_proj[STEP + n_rows : TILE + n_rows, :] = jnp.where(row == n_row - 1, OUTSIDE, right)

    lane = lax.broadcasted_iota(jnp.int32, (1, n_cols), 1)
    transposed = (((1,), (1,)), ((), ()))

    half = width // 2

    def pair_cells(acts, part):
        act = jnp.concatenate(acts, axis=0)
        weight = pair_weight[:, part * half : (part + 1) * half]
        return lax.dot_general(weight, act, transposed, preferred_element_type=f32)

    def side_cells(outer):
        return (pair_cells(outer[0], 0) + pair_cells(outer[1], 1)).astype(bf16)

    def pair_acts(rows, part, outer):
        inner = []
        channels_in = slice(part * half, (part + 1) * half)
        for k in range(PART):
            spread = jnp.broadcast_to(rows[k : k + 1, channels_in], (TILE, half)).astype(bf16)
            cells = col_proj[:, channels_in].reshape(tiles, TILE, half) + spread[None]
            act = jnp.maximum(cells, zero)
            inner.append(act[:-1].reshape(n_cols, half))
            outer[part].append(act[-1])
        return inner

    def pair_rows(rows, outer):
        parts, acts = [], None
        for low in range(0, rows.shape[0], PART):
            for part in range(2):
                ahead_acts = pair_acts(rows[low : low + PART], part, outer)
                if acts is not None:
                    parts.append(pair_cells(acts, 1 - part))
                acts = ahead_acts
        if acts is not None:
            parts.append(pair_cells(acts, 1))
        return [(parts[k] + parts[k + 1]).astype(bf16) for k in range(0, len(parts), 2)]

    def put_rows(start, hidden):
        for n, cells in enumerate(hidden):
            for k in range(PART):
                base[start + n * PART + k] = cells[:, k * n_cols : (k + 1) * n_cols]

    def put_sides(start, cells):
        for k in range(cells.shape[1] // n_cols):
            sides[start // STEP + k] = cells[:, k * n_cols : (k + 1) * n_cols]

    reach = TAPS * channels
    pitch = channels + STEP
    fill = [jnp.zeros((span - WINDOWS * channels, n_cols), bf16)]

    def conv_cells(blocks):
        cells = [jnp.concatenate(windows + fill, axis=0) for windows in blocks]
        cells = jnp.maximum(jnp.concatenate(cells, axis=1), zero)
        return jnp.dot(conv_weight[...], cells, preferred_element_type=f32)

    def conv_ends(groups):
        parts = conv_cells([[sides[at * TAPS + m] for m in range(WINDOWS)] for at in groups])
        ends = []
        for n in range(len(groups)):
            part = parts[:, n * n_cols : (n + 1) * n_cols]
            ends.append(jnp.where(lane % TILE >= STEP, part[:reach], part[2 * reach :]))
        return ends

    def conv_parts(at, low):
        places = [at * GROUP + p for p in range(low, low + PART)]
        return conv_cells([[base[p + STEP * m] for m in range(WINDOWS)] for p in places])

    def shifted(parts, ends, low):
        mids = []
        for k in range(PART):
            here = parts[:, k * n_cols : (k + 1) * n_cols]
            end = pltpu.roll(ends, (n_cols - STEP - (low + k) * TILE) % n_cols, 1)
            left = jnp.where(lane < STEP, end, pltpu.roll(here[:reach], STEP, 1))
            right = pltpu.roll(here[2 * reach :], n_cols - STEP, 1)
            right = jnp.where(lane >= n_cols - STEP, end, right)
            total = here[reach : 2 * reach] + left + right
            mids.append(jnp.maximum(total, 0.0).astype(bf16))
        return jnp.concatenate(mids, axis=1)

    def mixed_rows(at, low, mid):
        mixed = jnp.dot(mix_weight[:, :reach], mid, preferred_element_type=f32)
        for k in range(PART):
            for m in range(TAPS):
                row_at = at * GROUP + low + k + STEP * m
                here = mixed[m * channels : (m + 1) * channels, k * n_cols : (k + 1) * n_cols]
                here = here + base[row_at + STEP].astype(f32)
                result[pl.ds(pl.multiple_of(row_at * pitch, STEP), channels), :] = here

    def turn_rows(start, count):
        start = pl.multiple_of(start, TILE)
        for o in range(channels):
            cells = result[pl.ds(start * pitch + o, count, stride=pitch), :]
            staged[o, pl.ds(start, count), :] = cells.astype(bf16)

    def to_out(start, count, sem):
        rows = pl.ds(pl.multiple_of(start, TILE), count)
        return pltpu.make_async_copy(staged.at[:, rows], out.at[:, rows], sem)

    per_step = 2 * GROUP
    steps = n_rows // per_step - 1
    ahead = per_step + TILE
    outer = ([], [])
    put_rows(0, pair_rows(row_proj[:ahead, :], outer))
    put_sides(0, side_cells(outer))

    def rounds(groups, start, count, turn):
        ends = conv_ends(groups)
        places = [(n, low) for n in range(len(groups)) for low in range(0, STEP, PART)]
        share = -(-count // (PART * len(places))) * PART
        hidden, outer, mid = [], ([], []), None
        rows = row_proj[pl.ds(pl.multiple_of(start, STEP), count), :]
        for n, (group, low) in enumerate(places):
            parts = conv_parts(groups[group], low)
            if n == 0:
                turn()
            hidden += pair_rows(rows[n * share : (n + 1) * share], outer)
            if n:
                mixed_rows(groups[places[n - 1][0]], places[n - 1][1], mid)
            mid = shifted(parts, ends[group], low)
        outer = side_cells(outer)
        mixed_rows(groups[-1], places[-1][1], mid)
        put_rows(start, hidden)
        put_sides(start, outer)

    def step(at, _):
        before = jnp.maximum(at - 1, 0)
        rounds(
            (2 * at, 2 * at + 1),
            at * per_step + ahead,
            per_step,
            lambda: turn_rows(before * per_step, per_step),
        )

        @pl.when(at > 0)
        def _send():
            to_out(before * per_step, per_step, sems.at[before]).start()

        return _

    spare = pl.ds(n_rows + TILE, STEP)
    base[spare] = jnp.zeros_like(base[spare])
    sides[(n_rows + TILE) // STEP] = jnp.zeros_like(sides[0])
    lax.fori_loop(0, steps, step, 0)

    done = steps * per_step
    rounds(
        (2 * steps, 2 * steps + 1),
        done + ahead,
        TILE,
        lambda: turn_rows(done - per_step, per_step),
    )
    to_out(done - per_step, per_step, sems.at[steps - 1]).start()
    at = 2 * steps + 2
    (ends,) = conv_ends((at,))
    lows = range(0, STEP, PART)
    parts = [conv_parts(at, low) for low in lows]
    turn_rows(done, per_step)
    to_out(done, per_step, sems.at[steps]).start()
    for low, part in zip(lows, parts):
        mixed_rows(at, low, shifted(part, ends, low))
    done += per_step
    turn_rows(done, n_rows - done)
    last = to_out(done, n_rows - done, sems.at[steps + 1])
    last.start()
    for at in range(steps + 1):
        to_out(at * per_step, per_step, sems.at[at]).wait()
    last.wait()


def on_device(trunk, row_weight, column_weight, pair_map_weight, dilated_weight, mixing_weight):
    n_row, n_chip = lax.axis_size("row"), lax.axis_size("chip")
    shard, depth = trunk.shape
    n_rows, n_cols = shard * n_chip * 2, shard * n_row
    channels = pair_map_weight.shape[1]
    width = row_weight.shape[1]
    small = jnp.concatenate([dilated_weight.reshape(-1, channels), mixing_weight], axis=0)
    small = jnp.pad(small, ((0, 0), (0, width - channels)))
    weights = jnp.concatenate([row_weight, column_weight, pair_map_weight.T, small], axis=0)

    half = depth // 2
    to = lax.broadcasted_iota(jnp.int32, (n_row * n_chip * 2, shard, half), 0)
    copies = jnp.where(to % 2 == 0, trunk[None, :, :half], trunk[None, :, half:])
    mine = lax.all_to_all(copies, ("row", "chip", "core"), 0, 0).reshape(-1, half)
    other = lax.ppermute(mine, "core", [(0, 1), (1, 0)])
    span = -(-WINDOWS * channels // n_cols) * n_cols
    groups = -(-n_rows // GROUP)
    padded = groups * GROUP + TILE
    return pl.pallas_call(
        functools.partial(kernel, n_row, n_chip),
        out_shape=jax.ShapeDtypeStruct((channels, n_rows, n_cols), jnp.bfloat16),
        out_specs=pl.BlockSpec(memory_space=pl.ANY),
        scratch_shapes=[
            pltpu.VMEM((TAPS * TAPS * channels, span), jnp.bfloat16),
            pltpu.VMEM((TAPS * channels, span), jnp.bfloat16),
            pltpu.VMEM((n_rows + TILE, width), jnp.float32),
            pltpu.VMEM((n_cols + TILE, width), jnp.bfloat16),
            pltpu.VMEM((padded, channels, n_cols), jnp.bfloat16),
            pltpu.VMEM((padded // STEP, channels, n_cols), jnp.bfloat16),
            pltpu.VMEM((groups * GROUP * (channels + STEP), n_cols), jnp.float32),
            pltpu.VMEM((channels, n_rows, n_cols), jnp.bfloat16),
            pltpu.SemaphoreType.DMA((n_rows // (2 * GROUP) + 1,)),
        ],
        compiler_params=pltpu.CompilerParams(vmem_limit_bytes=52 * 2**20),
        name="pair_block",
    )(mine, other, weights)


def solution(mesh):
    n_row, n_col = mesh.devices.shape
    chips = Mesh(mesh.devices.reshape(n_row, n_col // 2, 2), ("row", "chip", "core"))
    return jax.shard_map(
        on_device,
        mesh=chips,
        in_specs=(P(("row", "chip", "core"), None), P(), P(), P(), P(), P()),
        out_specs=P(None, "row", ("chip", "core")),
        check_vma=False,
    )
```

```python
import functools

import jax
import jax.numpy as jnp
from jax import lax
from jax.experimental import pallas as pl
from jax.experimental.pallas import tpu as pltpu
from jax.sharding import Mesh
from jax.sharding import PartitionSpec as P

STEP = 8
TILE = 2 * STEP
TAPS = 3
PART = 4
WINDOWS = TAPS + 2
GROUP = TAPS * STEP
OUTSIDE = -1e30


def kernel(
    n_row,
    n_chip,
    mine,
    other,
    weights,
    out,
    conv_weight,
    mix_weight,
    row_proj,
    col_proj,
    col_turned,
    base,
    sides,
    result,
    staged,
    sems,
):
    depth = 2 * mine.shape[1]
    row_weight = weights.at[pl.ds(0, depth)]
    col_weight = weights.at[pl.ds(depth, depth)]
    pair_weight = weights.at[pl.ds(2 * depth, out.shape[0])]
    f32, bf16 = jnp.float32, jnp.bfloat16
    row, chip, core = (lax.axis_index(name) for name in ("row", "chip", "core"))
    channels, n_rows, n_cols = out.shape

    span = conv_weight.shape[1]

    def block(at):
        cells = weights[pl.ds(2 * depth + (1 + at) * channels, channels), :span]
        return cells.astype(f32)

    taps = [[block(a * TAPS + b) for b in range(TAPS)] for a in range(TAPS)]
    mixing = block(TAPS * TAPS)
    for m in range(TAPS):
        for b in range(TAPS):
            moved = [pltpu.roll(taps[a][b], (m + a) * channels, 1) for a in range(TAPS)]
            rows = pl.ds((b * TAPS + m) * channels, channels)
            conv_weight[rows, :] = (moved[0] + moved[1] + moved[2]).astype(bf16)
        moved = pltpu.roll(mixing, m * channels, 1) if m else mixing
        mix_weight[pl.ds(m * channels, channels), :] = moved.astype(bf16)

    zero = jnp.zeros((), bf16)

    def projected(start, size, weight):
        ends = (jnp.maximum(start - TILE, 0), jnp.minimum(start + size, mine.shape[0] - TILE))
        spans = [pl.ds(pl.multiple_of(start, TILE), size)]
        spans += [pl.ds(pl.multiple_of(end, TILE), TILE) for end in ends]
        halves = [jnp.concatenate([half[rows] for rows in spans], axis=0) for half in (mine, other)]
        cells = jnp.concatenate(
            [jnp.where(core == k, halves[0], halves[1]) for k in range(2)], axis=1
        )
        cells = jnp.dot(cells, weight[...], preferred_element_type=f32).astype(bf16).astype(f32)
        return cells[:size], cells[size + STEP : size + TILE], cells[size + TILE : size + TILE + STEP]

    width = row_proj.shape[1]

    cells, left, right = projected((chip * 2 + core) * n_cols, n_cols, col_weight)
    col_proj[:n_cols, :] = cells.astype(bf16)
    left = jnp.where((chip == 0) & (core == 0), OUTSIDE, left)
    right = jnp.where((chip == n_chip - 1) & (core == 1), OUTSIDE, right)
    col_proj[n_cols:, :] = jnp.concatenate([right, left], axis=0).astype(bf16)

    cells, left, right = projected(row * n_rows, n_rows, row_weight)
    row_proj[:STEP, :] = jnp.where(row == 0, OUTSIDE, left)
    row_proj[STEP : STEP + n_rows, :] = cells
    row_proj[STEP + n_rows : TILE + n_rows, :] = jnp.where(row == n_row - 1, OUTSIDE, right)

    lane = lax.broadcasted_iota(jnp.int32, (1, n_cols), 1)
    col_turned[:, :n_cols] = jnp.transpose(col_proj[:n_cols, :].astype(f32)).astype(bf16)
    cells = jnp.concatenate([col_proj[n_cols:, :].astype(f32)] * (n_cols // TILE), axis=0)
    col_turned[:, n_cols:] = jnp.transpose(cells).astype(bf16)

    def pair_cells(acts):
        act = jnp.concatenate(acts, axis=1)
        hidden = jnp.dot(pair_weight[...], act, preferred_element_type=f32)
        return hidden.astype(bf16)

    def pair_acts(turned, first, outer):
        inner = []
        for k in range(first, first + PART):
            spread = jnp.broadcast_to(turned[:, k : k + 1], (width, n_cols))
            inner.append(jnp.maximum(col_turned[:, :n_cols] + spread, zero))
            at = k % STEP * TILE
            if at == 0:
                outer.append(spread)
            else:
                outer[-1] = jnp.where(lane >= at, spread, outer[-1])
            if at + TILE == n_cols:
                outer[-1] = jnp.maximum(col_turned[:, n_cols:] + outer[-1], zero)
        return inner

    def pair_rows(turned, first, count, outer):
        hidden, acts = [], None
        for low in range(first, first + count, PART):
            ahead_acts = pair_acts(turned, low, outer)
            if acts is not None:
                hidden.append(pair_cells(acts))
            acts = ahead_acts
        if acts is not None:
            hidden.append(pair_cells(acts))
        return hidden

    def put_rows(start, hidden):
        for n, cells in enumerate(hidden):
            for k in range(PART):
                base[start + n * PART + k] = cells[:, k * n_cols : (k + 1) * n_cols]

    def put_sides(start, cells):
        for k in range(cells.shape[1] // n_cols):
            sides[start // STEP + k] = cells[:, k * n_cols : (k + 1) * n_cols]

    reach = TAPS * channels
    pitch = channels + STEP
    fill = [jnp.zeros((span - WINDOWS * channels, n_cols), bf16)]

    def conv_cells(blocks):
        cells = [jnp.concatenate(windows + fill, axis=0) for windows in blocks]
        cells = jnp.maximum(jnp.concatenate(cells, axis=1), zero)
        return jnp.dot(conv_weight[...], cells, preferred_element_type=f32)

    def conv_ends(groups):
        parts = conv_cells([[sides[at * TAPS + m] for m in range(WINDOWS)] for at in groups])
        ends = []
        for n in range(len(groups)):
            part = parts[:, n * n_cols : (n + 1) * n_cols]
            ends.append(jnp.where(lane % TILE >= STEP, part[:reach], part[2 * reach :]))
        return ends

    def conv_parts(at, low):
        places = [at * GROUP + p for p in range(low, low + PART)]
        return conv_cells([[base[p + STEP * m] for m in range(WINDOWS)] for p in places])

    def shifted(parts, ends, low):
        mids = []
        for k in range(PART):
            here = parts[:, k * n_cols : (k + 1) * n_cols]
            end = pltpu.roll(ends, (n_cols - STEP - (low + k) * TILE) % n_cols, 1)
            left = jnp.where(lane < STEP, end, pltpu.roll(here[:reach], STEP, 1))
            right = pltpu.roll(here[2 * reach :], n_cols - STEP, 1)
            right = jnp.where(lane >= n_cols - STEP, end, right)
            total = here[reach : 2 * reach] + left + right
            mids.append(jnp.maximum(total, 0.0).astype(bf16))
        return jnp.concatenate(mids, axis=1)

    def mixed_rows(at, low, mid):
        mixed = jnp.dot(mix_weight[:, :reach], mid, preferred_element_type=f32)
        for k in range(PART):
            for m in range(TAPS):
                row_at = at * GROUP + low + k + STEP * m
                here = mixed[m * channels : (m + 1) * channels, k * n_cols : (k + 1) * n_cols]
                here = here + base[row_at + STEP].astype(f32)
                result[pl.ds(pl.multiple_of(row_at * pitch, STEP), channels), :] = here

    def turn_rows(start, count):
        start = pl.multiple_of(start, TILE)
        for o in range(channels):
            cells = result[pl.ds(start * pitch + o, count, stride=pitch), :]
            staged[o, pl.ds(start, count), :] = cells.astype(bf16)

    def to_out(start, count, sem):
        rows = pl.ds(pl.multiple_of(start, TILE), count)
        return pltpu.make_async_copy(staged.at[:, rows], out.at[:, rows], sem)

    per_step = 2 * GROUP
    steps = n_rows // per_step - 1
    ahead = per_step + TILE
    outer = []
    turned = jnp.transpose(row_proj[:ahead, :]).astype(bf16)
    put_rows(0, pair_rows(turned, 0, ahead, outer))
    put_sides(0, pair_cells(outer))

    def rounds(groups, start, count, turn):
        ends = conv_ends(groups)
        places = [(n, low) for n in range(len(groups)) for low in range(0, STEP, PART)]
        share = -(-count // (PART * len(places))) * PART
        hidden, outer, mid = [], [], None
        rows = row_proj[pl.ds(pl.multiple_of(start, STEP), count), :]
        turned = jnp.transpose(rows).astype(bf16)
        for n, (group, low) in enumerate(places):
            parts = conv_parts(groups[group], low)
            if n == 0:
                turn()
            taken = min(n * share, count)
            hidden += pair_rows(turned, taken, min(share, count - taken), outer)
            if n:
                mixed_rows(groups[places[n - 1][0]], places[n - 1][1], mid)
            mid = shifted(parts, ends[group], low)
        outer = pair_cells(outer)
        mixed_rows(groups[-1], places[-1][1], mid)
        put_rows(start, hidden)
        put_sides(start, outer)

    def step(at, _):
        before = jnp.maximum(at - 1, 0)
        rounds(
            (2 * at, 2 * at + 1),
            at * per_step + ahead,
            per_step,
            lambda: turn_rows(before * per_step, per_step),
        )

        @pl.when(at > 0)
        def _send():
            to_out(before * per_step, per_step, sems.at[before]).start()

        return _

    spare = pl.ds(n_rows + TILE, STEP)
    base[spare] = jnp.zeros_like(base[spare])
    sides[(n_rows + TILE) // STEP] = jnp.zeros_like(sides[0])
    lax.fori_loop(0, steps, step, 0)

    done = steps * per_step
    rounds(
        (2 * steps, 2 * steps + 1),
        done + ahead,
        TILE,
        lambda: turn_rows(done - per_step, per_step),
    )
    to_out(done - per_step, per_step, sems.at[steps - 1]).start()
    at = 2 * steps + 2
    (ends,) = conv_ends((at,))
    lows = range(0, STEP, PART)
    parts = [conv_parts(at, low) for low in lows]
    turn_rows(done, per_step)
    to_out(done, per_step, sems.at[steps]).start()
    for low, part in zip(lows, parts):
        mixed_rows(at, low, shifted(part, ends, low))
    done += per_step
    turn_rows(done, n_rows - done)
    last = to_out(done, n_rows - done, sems.at[steps + 1])
    last.start()
    for at in range(steps + 1):
        to_out(at * per_step, per_step, sems.at[at]).wait()
    last.wait()


def on_device(trunk, row_weight, column_weight, pair_map_weight, dilated_weight, mixing_weight):
    n_row, n_chip = lax.axis_size("row"), lax.axis_size("chip")
    shard, depth = trunk.shape
    n_rows, n_cols = shard * n_chip * 2, shard * n_row
    channels = pair_map_weight.shape[1]
    width = row_weight.shape[1]
    small = jnp.concatenate([dilated_weight.reshape(-1, channels), mixing_weight], axis=0)
    small = jnp.pad(small, ((0, 0), (0, width - channels)))
    weights = jnp.concatenate([row_weight, column_weight, pair_map_weight.T, small], axis=0)

    half = depth // 2
    to = lax.broadcasted_iota(jnp.int32, (n_row * n_chip * 2, shard, half), 0)
    copies = jnp.where(to % 2 == 0, trunk[None, :, :half], trunk[None, :, half:])
    mine = lax.all_to_all(copies, ("row", "chip", "core"), 0, 0).reshape(-1, half)
    other = lax.ppermute(mine, "core", [(0, 1), (1, 0)])
    span = -(-WINDOWS * channels // n_cols) * n_cols
    groups = -(-n_rows // GROUP)
    padded = groups * GROUP + TILE
    return pl.pallas_call(
        functools.partial(kernel, n_row, n_chip),
        out_shape=jax.ShapeDtypeStruct((channels, n_rows, n_cols), jnp.bfloat16),
        out_specs=pl.BlockSpec(memory_space=pl.ANY),
        scratch_shapes=[
            pltpu.VMEM((TAPS * TAPS * channels, span), jnp.bfloat16),
            pltpu.VMEM((TAPS * channels, span), jnp.bfloat16),
            pltpu.VMEM((n_rows + TILE, width), jnp.float32),
            pltpu.VMEM((n_cols + TILE, width), jnp.bfloat16),
            pltpu.VMEM((width, 2 * n_cols), jnp.bfloat16),
            pltpu.VMEM((padded, channels, n_cols), jnp.bfloat16),
            pltpu.VMEM((padded // STEP, channels, n_cols), jnp.bfloat16),
            pltpu.VMEM((groups * GROUP * (channels + STEP), n_cols), jnp.float32),
            pltpu.VMEM((channels, n_rows, n_cols), jnp.bfloat16),
            pltpu.SemaphoreType.DMA((n_rows // (2 * GROUP) + 1,)),
        ],
        compiler_params=pltpu.CompilerParams(vmem_limit_bytes=52 * 2**20),
        name="pair_block",
    )(mine, other, weights)


def solution(mesh):
    n_row, n_col = mesh.devices.shape
    chips = Mesh(mesh.devices.reshape(n_row, n_col // 2, 2), ("row", "chip", "core"))
    return jax.shard_map(
        on_device,
        mesh=chips,
        in_specs=(P(("row", "chip", "core"), None), P(), P(), P(), P(), P()),
        out_specs=P(None, "row", ("chip", "core")),
        check_vma=False,
    )
```

```python
import functools

import jax
import jax.numpy as jnp
from jax import lax
from jax.experimental import pallas as pl
from jax.experimental.pallas import tpu as pltpu
from jax.sharding import Mesh
from jax.sharding import PartitionSpec as P

STEP = 8
TILE = 2 * STEP
TAPS = 3
PART = 4
WINDOWS = TAPS + 2
GROUP = TAPS * STEP
OUTSIDE = -1e30


def kernel(
    n_row,
    n_chip,
    mine,
    other,
    weights,
    out,
    conv_weight,
    mix_weight,
    row_proj,
    col_proj,
    base,
    sides,
    result,
    staged,
    sems,
):
    depth = 2 * mine.shape[1]
    row_weight = weights.at[pl.ds(0, depth)]
    col_weight = weights.at[pl.ds(depth, depth)]
    pair_weight = weights.at[pl.ds(2 * depth, out.shape[0])]
    f32, bf16 = jnp.float32, jnp.bfloat16
    row, chip, core = (lax.axis_index(name) for name in ("row", "chip", "core"))
    channels, n_rows, n_cols = out.shape

    span = conv_weight.shape[1]
    tiles = n_cols // TILE + 1
    zero = jnp.zeros((), bf16)

    def projected(start, size, weight):
        ends = (jnp.maximum(start - TILE, 0), jnp.minimum(start + size, mine.shape[0] - TILE))
        spans = [pl.ds(pl.multiple_of(start, TILE), size)]
        spans += [pl.ds(pl.multiple_of(end, TILE), TILE) for end in ends]
        halves = [jnp.concatenate([half[rows] for rows in spans], axis=0) for half in (mine, other)]
        cells = jnp.concatenate(
            [jnp.where(core == k, halves[0], halves[1]) for k in range(2)], axis=1
        )
        cells = jnp.dot(cells, weight[...], preferred_element_type=f32).astype(bf16).astype(f32)
        return cells[:size], cells[size + STEP : size + TILE], cells[size + TILE : size + TILE + STEP]

    width = row_proj.shape[1]

    cells, left, right = projected((chip * 2 + core) * n_cols, n_cols, col_weight)
    col_proj[:n_cols, :] = cells.astype(bf16)
    left = jnp.where((chip == 0) & (core == 0), OUTSIDE, left)
    right = jnp.where((chip == n_chip - 1) & (core == 1), OUTSIDE, right)
    col_proj[n_cols:, :] = jnp.concatenate([right, left], axis=0).astype(bf16)

    cells, left, right = projected(row * n_rows, n_rows, row_weight)
    row_proj[:STEP, :] = jnp.where(row == 0, OUTSIDE, left)
    row_proj[STEP : STEP + n_rows, :] = cells
    row_proj[STEP + n_rows : TILE + n_rows, :] = jnp.where(row == n_row - 1, OUTSIDE, right)

    lane = lax.broadcasted_iota(jnp.int32, (1, n_cols), 1)
    transposed = (((1,), (1,)), ((), ()))

    def pair_cells(acts):
        act = jnp.concatenate(acts, axis=0)
        hidden = lax.dot_general(pair_weight[...], act, transposed, preferred_element_type=f32)
        return hidden.astype(bf16)

    def pair_acts(rows, outer):
        inner = []
        for k in range(PART):
            spread = jnp.broadcast_to(rows[k : k + 1], (TILE, width)).astype(bf16)
            cells = col_proj[...].reshape(tiles, TILE, width) + spread[None]
            act = jnp.maximum(cells, zero)
            inner.append(act[:-1].reshape(n_cols, width))
            outer.append(act[-1])
        return inner

    def pair_rows(rows, outer):
        hidden, acts = [], None
        for low in range(0, rows.shape[0], PART):
            ahead_acts = pair_acts(rows[low : low + PART], outer)
            if acts is not None:
                hidden.append(pair_cells(acts))
            acts = ahead_acts
        if acts is not None:
            hidden.append(pair_cells(acts))
        return hidden

    def put_rows(start, hidden):
        for n, cells in enumerate(hidden):
            for k in range(PART):
                base[start + n * PART + k] = cells[:, k * n_cols : (k + 1) * n_cols]

    def put_sides(start, cells):
        for k in range(cells.shape[1] // n_cols):
            sides[start // STEP + k] = cells[:, k * n_cols : (k + 1) * n_cols]

    reach = TAPS * channels
    pitch = channels + STEP
    fill = [jnp.zeros((span - WINDOWS * channels, n_cols), bf16)]

    def conv_cells(blocks):
        cells = [jnp.concatenate(windows + fill, axis=0) for windows in blocks]
        cells = jnp.maximum(jnp.concatenate(cells, axis=1), zero)
        return jnp.dot(conv_weight[...], cells, preferred_element_type=f32)

    def conv_ends(groups):
        parts = conv_cells([[sides[at * TAPS + m] for m in range(WINDOWS)] for at in groups])
        ends = []
        for n in range(len(groups)):
            part = parts[:, n * n_cols : (n + 1) * n_cols]
            ends.append(jnp.where(lane % TILE >= STEP, part[:reach], part[2 * reach :]))
        return ends

    def conv_parts(at, low):
        places = [at * GROUP + p for p in range(low, low + PART)]
        return conv_cells([[base[p + STEP * m] for m in range(WINDOWS)] for p in places])

    def shifted(parts, ends, low):
        mids = []
        for k in range(PART):
            here = parts[:, k * n_cols : (k + 1) * n_cols]
            end = pltpu.roll(ends, (n_cols - STEP - (low + k) * TILE) % n_cols, 1)
            left = jnp.where(lane < STEP, end, pltpu.roll(here[:reach], STEP, 1))
            right = pltpu.roll(here[2 * reach :], n_cols - STEP, 1)
            right = jnp.where(lane >= n_cols - STEP, end, right)
            total = here[reach : 2 * reach] + left + right
            mids.append(jnp.maximum(total, 0.0).astype(bf16))
        return jnp.concatenate(mids, axis=1)

    def mixed_rows(at, low, mid):
        mixed = jnp.dot(mix_weight[:, :reach], mid, preferred_element_type=f32)
        for k in range(PART):
            for m in range(TAPS):
                row_at = at * GROUP + low + k + STEP * m
                here = mixed[m * channels : (m + 1) * channels, k * n_cols : (k + 1) * n_cols]
                here = here + base[row_at + STEP].astype(f32)
                result[pl.ds(pl.multiple_of(row_at * pitch, STEP), channels), :] = here

    def turn_rows(start, count):
        start = pl.multiple_of(start, TILE)
        for o in range(channels):
            cells = result[pl.ds(start * pitch + o, count, stride=pitch), :]
            staged[o, pl.ds(start, count), :] = cells.astype(bf16)

    def to_out(start, count, sem):
        rows = pl.ds(pl.multiple_of(start, TILE), count)
        return pltpu.make_async_copy(staged.at[:, rows], out.at[:, rows], sem)

    per_step = 2 * GROUP
    steps = n_rows // per_step - 1
    ahead = per_step + TILE
    outer = []
    put_rows(0, pair_rows(row_proj[:ahead, :], outer))
    put_sides(0, pair_cells(outer))

    def block(at):
        cells = weights[pl.ds(2 * depth + (1 + at) * channels, channels), :span]
        return cells.astype(f32)

    taps = [[block(a * TAPS + b) for b in range(TAPS)] for a in range(TAPS)]
    mixing = block(TAPS * TAPS)
    for m in range(TAPS):
        for b in range(TAPS):
            moved = [pltpu.roll(taps[a][b], (m + a) * channels, 1) for a in range(TAPS)]
            rows = pl.ds((b * TAPS + m) * channels, channels)
            conv_weight[rows, :] = (moved[0] + moved[1] + moved[2]).astype(bf16)
        moved = pltpu.roll(mixing, m * channels, 1) if m else mixing
        mix_weight[pl.ds(m * channels, channels), :] = moved.astype(bf16)


    def rounds(groups, start, count, turn, share, then=None):
        ends = conv_ends(groups[:2])
        places = [(n, low) for n in range(len(groups)) for low in range(0, STEP, PART)]
        hidden, outer, mid = [], [], None
        rows = row_proj[pl.ds(pl.multiple_of(start, STEP), count), :]

        def put():
            put_rows(start, hidden)
            put_sides(start, pair_cells(outer))

        for n, (group, low) in enumerate(places):
            if group == len(ends):
                ends += conv_ends(groups[group : group + 1])
            parts = conv_parts(groups[group], low)
            if n == 0:
                turn()
            hidden += pair_rows(rows[n * share : (n + 1) * share], outer)
            if n == 0 and then is not None:
                put()
            if n:
                mixed_rows(groups[places[n - 1][0]], places[n - 1][1], mid)
            mid = shifted(parts, ends[group], low)
        if then is not None:
            then()
        mixed_rows(groups[-1], places[-1][1], mid)
        if then is None:
            put()

    def step(at, _):
        before = jnp.maximum(at - 1, 0)
        rounds(
            (2 * at, 2 * at + 1),
            at * per_step + ahead,
            per_step,
            lambda: turn_rows(before * per_step, per_step),
            per_step * PART // (2 * STEP),
        )

        @pl.when(at > 0)
        def _send():
            to_out(before * per_step, per_step, sems.at[before]).start()

        return _

    spare = pl.ds(n_rows + TILE, STEP)
    base[spare] = jnp.zeros_like(base[spare])
    sides[(n_rows + TILE) // STEP] = jnp.zeros_like(sides[0])
    lax.fori_loop(0, steps, step, 0)

    done = steps * per_step

    def send():
        turn_rows(done, per_step)
        to_out(done, per_step, sems.at[steps]).start()

    def turn_before():
        turn_rows(done - per_step, per_step)
        to_out(done - per_step, per_step, sems.at[steps - 1]).start()

    groups = tuple(range(2 * steps, -(-n_rows // GROUP)))
    rounds(groups, done + ahead, TILE, turn_before, TILE, send)
    rest = done + per_step
    turn_rows(rest, n_rows - rest)
    last = to_out(rest, n_rows - rest, sems.at[steps + 1])
    last.start()
    for at in range(steps + 1):
        to_out(at * per_step, per_step, sems.at[at]).wait()
    last.wait()


def on_device(trunk, row_weight, column_weight, pair_map_weight, dilated_weight, mixing_weight):
    n_row, n_chip = lax.axis_size("row"), lax.axis_size("chip")
    shard, depth = trunk.shape
    n_rows, n_cols = shard * n_chip * 2, shard * n_row
    channels = pair_map_weight.shape[1]
    width = row_weight.shape[1]
    small = jnp.concatenate([dilated_weight.reshape(-1, channels), mixing_weight], axis=0)
    small = jnp.pad(small, ((0, 0), (0, width - channels)))
    weights = jnp.concatenate([row_weight, column_weight, pair_map_weight.T, small], axis=0)

    half = depth // 2
    to = lax.broadcasted_iota(jnp.int32, (n_row * n_chip * 2, shard, half), 0)
    copies = jnp.where(to % 2 == 0, trunk[None, :, :half], trunk[None, :, half:])
    mine = lax.all_to_all(copies, ("row", "chip", "core"), 0, 0).reshape(-1, half)
    other = lax.ppermute(mine, "core", [(0, 1), (1, 0)])
    span = -(-WINDOWS * channels // n_cols) * n_cols
    groups = -(-n_rows // GROUP)
    padded = groups * GROUP + TILE
    return pl.pallas_call(
        functools.partial(kernel, n_row, n_chip),
        out_shape=jax.ShapeDtypeStruct((channels, n_rows, n_cols), jnp.bfloat16),
        out_specs=pl.BlockSpec(memory_space=pl.ANY),
        scratch_shapes=[
            pltpu.VMEM((TAPS * TAPS * channels, span), jnp.bfloat16),
            pltpu.VMEM((TAPS * channels, span), jnp.bfloat16),
            pltpu.VMEM((n_rows + TILE, width), jnp.float32),
            pltpu.VMEM((n_cols + TILE, width), jnp.bfloat16),
            pltpu.VMEM((padded, channels, n_cols), jnp.bfloat16),
            pltpu.VMEM((padded // STEP, channels, n_cols), jnp.bfloat16),
            pltpu.VMEM((groups * GROUP * (channels + STEP), n_cols), jnp.float32),
            pltpu.VMEM((channels, n_rows, n_cols), jnp.bfloat16),
            pltpu.SemaphoreType.DMA((n_rows // (2 * GROUP) + 1,)),
        ],
        compiler_params=pltpu.CompilerParams(vmem_limit_bytes=52 * 2**20),
        name="pair_block",
    )(mine, other, weights)


def solution(mesh):
    n_row, n_col = mesh.devices.shape
    chips = Mesh(mesh.devices.reshape(n_row, n_col // 2, 2), ("row", "chip", "core"))
    return jax.shard_map(
        on_device,
        mesh=chips,
        in_specs=(P(("row", "chip", "core"), None), P(), P(), P(), P(), P()),
        out_specs=P(None, "row", ("chip", "core")),
        check_vma=False,
    )
```

```python
import functools

import jax
import jax.numpy as jnp
from jax import lax
from jax.experimental import pallas as pl
from jax.experimental.pallas import tpu as pltpu
from jax.sharding import Mesh
from jax.sharding import PartitionSpec as P

STEP = 8
TILE = 2 * STEP
TAPS = 3
PART = 4
WINDOWS = TAPS + 2
GROUP = TAPS * STEP
OUTSIDE = -1e30


def kernel(
    n_row,
    n_chip,
    mine,
    other,
    weights,
    out,
    conv_weight,
    mix_weight,
    row_proj,
    col_proj,
    base,
    sides,
    result,
    staged,
    sems,
):
    depth = 2 * mine.shape[1]
    row_weight = weights.at[pl.ds(0, depth)]
    col_weight = weights.at[pl.ds(depth, depth)]
    pair_weight = weights.at[pl.ds(2 * depth, out.shape[0])]
    f32, bf16 = jnp.float32, jnp.bfloat16
    row, chip, core = (lax.axis_index(name) for name in ("row", "chip", "core"))
    channels, n_rows, n_cols = out.shape

    span = conv_weight.shape[1]

    def block(at):
        cells = weights[pl.ds(2 * depth + (1 + at) * channels, channels), :span]
        return cells.astype(f32)

    taps = [[block(a * TAPS + b) for b in range(TAPS)] for a in range(TAPS)]
    mixing = block(TAPS * TAPS)
    for m in range(TAPS):
        for b in range(TAPS):
            moved = [pltpu.roll(taps[a][b], (m + a) * channels, 1) for a in range(TAPS)]
            rows = pl.ds((b * TAPS + m) * channels, channels)
            conv_weight[rows, :] = (moved[0] + moved[1] + moved[2]).astype(bf16)
        moved = pltpu.roll(mixing, m * channels, 1) if m else mixing
        mix_weight[pl.ds(m * channels, channels), :] = moved.astype(bf16)

    tiles = n_cols // TILE + 1
    zero = jnp.zeros((), bf16)

    def projected(start, size, weight):
        ends = (jnp.maximum(start - TILE, 0), jnp.minimum(start + size, mine.shape[0] - TILE))
        spans = [pl.ds(pl.multiple_of(start, TILE), size)]
        spans += [pl.ds(pl.multiple_of(end, TILE), TILE) for end in ends]
        halves = [jnp.concatenate([half[rows] for rows in spans], axis=0) for half in (mine, other)]
        cells = jnp.concatenate(
            [jnp.where(core == k, halves[0], halves[1]) for k in range(2)], axis=1
        )
        cells = jnp.dot(cells, weight[...], preferred_element_type=f32).astype(bf16).astype(f32)
        return cells[:size], cells[size + STEP : size + TILE], cells[size + TILE : size + TILE + STEP]

    width = row_proj.shape[1]

    cells, left, right = projected((chip * 2 + core) * n_cols, n_cols, col_weight)
    col_proj[:n_cols, :] = cells.astype(bf16)
    left = jnp.where((chip == 0) & (core == 0), OUTSIDE, left)
    right = jnp.where((chip == n_chip - 1) & (core == 1), OUTSIDE, right)
    col_proj[n_cols:, :] = jnp.concatenate([right, left], axis=0).astype(bf16)

    cells, left, right = projected(row * n_rows, n_rows, row_weight)
    row_proj[:STEP, :] = jnp.where(row == 0, OUTSIDE, left)
    row_proj[STEP : STEP + n_rows, :] = cells
    row_proj[STEP + n_rows : TILE + n_rows, :] = jnp.where(row == n_row - 1, OUTSIDE, right)

    lane = lax.broadcasted_iota(jnp.int32, (1, n_cols), 1)
    transposed = (((1,), (1,)), ((), ()))

    def pair_cells(acts):
        act = jnp.concatenate(acts, axis=0)
        hidden = lax.dot_general(pair_weight[...], act, transposed, preferred_element_type=f32)
        return hidden.astype(bf16)

    def pair_acts(rows, outer):
        inner = []
        for k in range(PART):
            spread = jnp.broadcast_to(rows[k : k + 1], (TILE, width)).astype(bf16)
            cells = col_proj[...].reshape(tiles, TILE, width) + spread[None]
            act = jnp.maximum(cells, zero)
            inner.append(act[:-1].reshape(n_cols, width))
            outer.append(act[-1])
        return inner

    def pair_rows(rows, outer):
        hidden, acts = [], None
        for low in range(0, rows.shape[0], PART):
            ahead_acts = pair_acts(rows[low : low + PART], outer)
            if acts is not None:
                hidden.append(pair_cells(acts))
            acts = ahead_acts
        if acts is not None:
            hidden.append(pair_cells(acts))
        return hidden

    def put_rows(start, hidden):
        for n, cells in enumerate(hidden):
            for k in range(PART):
                base[start + n * PART + k] = cells[:, k * n_cols : (k + 1) * n_cols]

    def put_sides(start, cells):
        for k in range(cells.shape[1] // n_cols):
            sides[start // STEP + k] = cells[:, k * n_cols : (k + 1) * n_cols]

    reach = TAPS * channels
    pitch = channels + STEP
    fill = [jnp.zeros((span - WINDOWS * channels, n_cols), bf16)]

    def conv_cells(blocks):
        cells = [jnp.concatenate(windows + fill, axis=0) for windows in blocks]
        cells = jnp.maximum(jnp.concatenate(cells, axis=1), zero)
        return jnp.dot(conv_weight[...], cells, preferred_element_type=f32)

    def conv_ends(groups):
        parts = conv_cells([[sides[at * TAPS + m] for m in range(WINDOWS)] for at in groups])
        ends = []
        for n in range(len(groups)):
            part = parts[:, n * n_cols : (n + 1) * n_cols]
            ends.append(jnp.where(lane % TILE >= STEP, part[:reach], part[2 * reach :]))
        return ends

    def conv_parts(at, low):
        places = [at * GROUP + p for p in range(low, low + PART)]
        return conv_cells([[base[p + STEP * m] for m in range(WINDOWS)] for p in places])

    def shifted(parts, ends, low):
        mids = []
        for k in range(PART):
            here = parts[:, k * n_cols : (k + 1) * n_cols]
            end = pltpu.roll(ends, (n_cols - STEP - (low + k) * TILE) % n_cols, 1)
            left = jnp.where(lane < STEP, end, pltpu.roll(here[:reach], STEP, 1))
            right = pltpu.roll(here[2 * reach :], n_cols - STEP, 1)
            right = jnp.where(lane >= n_cols - STEP, end, right)
            total = here[reach : 2 * reach] + left + right
            mids.append(jnp.maximum(total, 0.0).astype(bf16))
        return jnp.concatenate(mids, axis=1)

    def mixed_rows(at, low, mid):
        mixed = jnp.dot(mix_weight[:, :reach], mid, preferred_element_type=f32)
        for k in range(PART):
            for m in range(TAPS):
                row_at = at * GROUP + low + k + STEP * m
                here = mixed[m * channels : (m + 1) * channels, k * n_cols : (k + 1) * n_cols]
                here = here + base[row_at + STEP].astype(f32)
                result[pl.ds(pl.multiple_of(row_at * pitch, STEP), channels), :] = here

    def turn_rows(start, count):
        start = pl.multiple_of(start, TILE)
        for o in range(channels):
            cells = result[pl.ds(start * pitch + o, count, stride=pitch), :]
            staged[o, pl.ds(start, count), :] = cells.astype(bf16)

    def to_out(start, count, sem):
        rows = pl.ds(pl.multiple_of(start, TILE), count)
        return pltpu.make_async_copy(staged.at[:, rows], out.at[:, rows], sem)

    per_step = 2 * GROUP
    steps = n_rows // per_step - 1
    ahead = per_step + TILE
    outer = []
    put_rows(0, pair_rows(row_proj[:ahead, :], outer))
    put_sides(0, pair_cells(outer))

    def rounds(groups, start, count, turn):
        ends = conv_ends(groups)
        places = [(n, low) for n in range(len(groups)) for low in range(0, STEP, PART)]
        share = -(-count // (PART * len(places))) * PART
        hidden, outer, mid = [], [], None
        rows = row_proj[pl.ds(pl.multiple_of(start, STEP), count), :]
        for n, (group, low) in enumerate(places):
            parts = conv_parts(groups[group], low)
            if n == 0:
                turn()
            taken = rows[n * share : (n + 1) * share]
            hidden += pair_rows(taken[:PART], outer)
            if n:
                mixed_rows(groups[places[n - 1][0]], places[n - 1][1], mid)
            hidden += pair_rows(taken[PART:], outer)
            mid = shifted(parts, ends[group], low)
        outer = pair_cells(outer)
        mixed_rows(groups[-1], places[-1][1], mid)
        put_rows(start, hidden)
        put_sides(start, outer)

    def step(at, _):
        before = jnp.maximum(at - 1, 0)
        rounds(
            (2 * at, 2 * at + 1),
            at * per_step + ahead,
            per_step,
            lambda: turn_rows(before * per_step, per_step),
        )

        @pl.when(at > 0)
        def _send():
            to_out(before * per_step, per_step, sems.at[before]).start()

        return _

    spare = pl.ds(n_rows + TILE, STEP)
    base[spare] = jnp.zeros_like(base[spare])
    sides[(n_rows + TILE) // STEP] = jnp.zeros_like(sides[0])
    lax.fori_loop(0, steps, step, 0)

    done = steps * per_step
    rounds(
        (2 * steps, 2 * steps + 1),
        done + ahead,
        TILE,
        lambda: turn_rows(done - per_step, per_step),
    )
    to_out(done - per_step, per_step, sems.at[steps - 1]).start()
    at = 2 * steps + 2
    (ends,) = conv_ends((at,))
    lows = range(0, STEP, PART)
    parts = [conv_parts(at, low) for low in lows]
    turn_rows(done, per_step)
    to_out(done, per_step, sems.at[steps]).start()
    for low, part in zip(lows, parts):
        mixed_rows(at, low, shifted(part, ends, low))
    done += per_step
    turn_rows(done, n_rows - done)
    last = to_out(done, n_rows - done, sems.at[steps + 1])
    last.start()
    for at in range(steps + 1):
        to_out(at * per_step, per_step, sems.at[at]).wait()
    last.wait()


def on_device(trunk, row_weight, column_weight, pair_map_weight, dilated_weight, mixing_weight):
    n_row, n_chip = lax.axis_size("row"), lax.axis_size("chip")
    shard, depth = trunk.shape
    n_rows, n_cols = shard * n_chip * 2, shard * n_row
    channels = pair_map_weight.shape[1]
    width = row_weight.shape[1]
    small = jnp.concatenate([dilated_weight.reshape(-1, channels), mixing_weight], axis=0)
    small = jnp.pad(small, ((0, 0), (0, width - channels)))
    weights = jnp.concatenate([row_weight, column_weight, pair_map_weight.T, small], axis=0)

    half = depth // 2
    to = lax.broadcasted_iota(jnp.int32, (n_row * n_chip * 2, shard, half), 0)
    copies = jnp.where(to % 2 == 0, trunk[None, :, :half], trunk[None, :, half:])
    mine = lax.all_to_all(copies, ("row", "chip", "core"), 0, 0).reshape(-1, half)
    other = lax.ppermute(mine, "core", [(0, 1), (1, 0)])
    span = -(-WINDOWS * channels // n_cols) * n_cols
    groups = -(-n_rows // GROUP)
    padded = groups * GROUP + TILE
    return pl.pallas_call(
        functools.partial(kernel, n_row, n_chip),
        out_shape=jax.ShapeDtypeStruct((channels, n_rows, n_cols), jnp.bfloat16),
        out_specs=pl.BlockSpec(memory_space=pl.ANY),
        scratch_shapes=[
            pltpu.VMEM((TAPS * TAPS * channels, span), jnp.bfloat16),
            pltpu.VMEM((TAPS * channels, span), jnp.bfloat16),
            pltpu.VMEM((n_rows + TILE, width), jnp.float32),
            pltpu.VMEM((n_cols + TILE, width), jnp.bfloat16),
            pltpu.VMEM((padded, channels, n_cols), jnp.bfloat16),
            pltpu.VMEM((padded // STEP, channels, n_cols), jnp.bfloat16),
            pltpu.VMEM((groups * GROUP * (channels + STEP), n_cols), jnp.float32),
            pltpu.VMEM((channels, n_rows, n_cols), jnp.bfloat16),
            pltpu.SemaphoreType.DMA((n_rows // (2 * GROUP) + 1,)),
        ],
        compiler_params=pltpu.CompilerParams(vmem_limit_bytes=52 * 2**20),
        name="pair_block",
    )(mine, other, weights)


def solution(mesh):
    n_row, n_col = mesh.devices.shape
    chips = Mesh(mesh.devices.reshape(n_row, n_col // 2, 2), ("row", "chip", "core"))
    return jax.shard_map(
        on_device,
        mesh=chips,
        in_specs=(P(("row", "chip", "core"), None), P(), P(), P(), P(), P()),
        out_specs=P(None, "row", ("chip", "core")),
        check_vma=False,
    )
```

```python
import functools

import jax
import jax.numpy as jnp
from jax import lax
from jax.experimental import pallas as pl
from jax.experimental.pallas import tpu as pltpu
from jax.sharding import Mesh
from jax.sharding import PartitionSpec as P

STEP = 8
TILE = 2 * STEP
TAPS = 3
PART = 4
WINDOWS = TAPS + 2
GROUP = TAPS * STEP
OUTSIDE = -1e30


def kernel(
    n_row,
    n_chip,
    mine,
    other,
    weights,
    out,
    conv_weight,
    mix_weight,
    row_proj,
    col_proj,
    base,
    sides,
    result,
    staged,
    sems,
):
    depth = 2 * mine.shape[1]
    row_weight = weights.at[pl.ds(0, depth)]
    col_weight = weights.at[pl.ds(depth, depth)]
    pair_weight = weights.at[pl.ds(2 * depth, out.shape[0])]
    f32, bf16 = jnp.float32, jnp.bfloat16
    row, chip, core = (lax.axis_index(name) for name in ("row", "chip", "core"))
    channels, n_rows, n_cols = out.shape

    span = conv_weight.shape[1]

    def block(at):
        cells = weights[pl.ds(2 * depth + (1 + at) * channels, channels), :span]
        return cells.astype(f32)

    taps = [[block(a * TAPS + b) for b in range(TAPS)] for a in range(TAPS)]
    mixing = block(TAPS * TAPS)
    for m in range(TAPS):
        for b in range(TAPS):
            moved = [pltpu.roll(taps[a][b], (m + a) * channels, 1) for a in range(TAPS)]
            rows = pl.ds((b * TAPS + m) * channels, channels)
            conv_weight[rows, :] = (moved[0] + moved[1] + moved[2]).astype(bf16)
        moved = pltpu.roll(mixing, m * channels, 1) if m else mixing
        mix_weight[pl.ds(m * channels, channels), :] = moved.astype(bf16)

    tiles = n_cols // TILE + 1
    zero = jnp.zeros((), bf16)

    def projected(start, size, weight):
        ends = (jnp.maximum(start - TILE, 0), jnp.minimum(start + size, mine.shape[0] - TILE))
        spans = [pl.ds(pl.multiple_of(start, TILE), size)]
        spans += [pl.ds(pl.multiple_of(end, TILE), TILE) for end in ends]
        halves = [jnp.concatenate([half[rows] for rows in spans], axis=0) for half in (mine, other)]
        cells = jnp.concatenate(
            [jnp.where(core == k, halves[0], halves[1]) for k in range(2)], axis=1
        )
        cells = jnp.dot(cells, weight[...], preferred_element_type=f32).astype(bf16).astype(f32)
        return cells[:size], cells[size + STEP : size + TILE], cells[size + TILE : size + TILE + STEP]

    width = row_proj.shape[1]

    cells, left, right = projected((chip * 2 + core) * n_cols, n_cols, col_weight)
    col_proj[:n_cols, :] = cells.astype(bf16)
    left = jnp.where((chip == 0) & (core == 0), OUTSIDE, left)
    right = jnp.where((chip == n_chip - 1) & (core == 1), OUTSIDE, right)
    col_proj[n_cols:, :] = jnp.concatenate([right, left], axis=0).astype(bf16)

    cells, left, right = projected(row * n_rows, n_rows, row_weight)
    row_proj[:STEP, :] = jnp.where(row == 0, OUTSIDE, left)
    row_proj[STEP : STEP + n_rows, :] = cells
    row_proj[STEP + n_rows : TILE + n_rows, :] = jnp.where(row == n_row - 1, OUTSIDE, right)

    lane = lax.broadcasted_iota(jnp.int32, (1, n_cols), 1)
    transposed = (((1,), (1,)), ((), ()))

    def pair_cells(acts):
        act = jnp.concatenate(acts, axis=0)
        hidden = lax.dot_general(pair_weight[...], act, transposed, preferred_element_type=f32)
        return hidden.astype(bf16)

    def pair_acts(rows, outer):
        inner = []
        for k in range(PART):
            spread = jnp.broadcast_to(rows[k : k + 1], (TILE, width)).astype(bf16)
            cells = col_proj[...].reshape(tiles, TILE, width) + spread[None]
            act = jnp.maximum(cells, zero)
            inner.append(act[:-1].reshape(n_cols, width))
            outer.append(act[-1])
        return inner

    def pair_rows(rows, outer):
        hidden, acts = [], None
        for low in range(0, rows.shape[0], PART):
            ahead_acts = pair_acts(rows[low : low + PART], outer)
            if acts is not None:
                hidden.append(pair_cells(acts))
            acts = ahead_acts
        if acts is not None:
            hidden.append(pair_cells(acts))
        return hidden

    def put_rows(start, hidden):
        for n, cells in enumerate(hidden):
            for k in range(PART):
                base[start + n * PART + k] = cells[:, k * n_cols : (k + 1) * n_cols]

    def put_sides(start, cells):
        for k in range(cells.shape[1] // n_cols):
            sides[start // STEP + k] = cells[:, k * n_cols : (k + 1) * n_cols]

    reach = TAPS * channels
    pitch = channels + STEP
    fill = [jnp.zeros((span - WINDOWS * channels, n_cols), bf16)]

    def conv_cells(blocks):
        cells = [jnp.concatenate(windows + fill, axis=0) for windows in blocks]
        cells = jnp.maximum(jnp.concatenate(cells, axis=1), zero)
        return jnp.dot(conv_weight[...], cells, preferred_element_type=f32)

    def conv_ends(groups):
        parts = conv_cells([[sides[at * TAPS + m] for m in range(WINDOWS)] for at in groups])
        ends = []
        for n in range(len(groups)):
            part = parts[:, n * n_cols : (n + 1) * n_cols]
            ends.append(jnp.where(lane % TILE >= STEP, part[:reach], part[2 * reach :]))
        return ends

    def conv_parts(at, low):
        places = [at * GROUP + p for p in range(low, low + PART)]
        return conv_cells([[base[p + STEP * m] for m in range(WINDOWS)] for p in places])

    def shifted(parts, ends, low):
        mids = []
        for k in range(PART):
            here = parts[:, k * n_cols : (k + 1) * n_cols]
            end = pltpu.roll(ends, (n_cols - STEP - (low + k) * TILE) % n_cols, 1)
            left = jnp.where(lane < STEP, end, pltpu.roll(here[:reach], STEP, 1))
            right = pltpu.roll(here[2 * reach :], n_cols - STEP, 1)
            right = jnp.where(lane >= n_cols - STEP, end, right)
            total = here[reach : 2 * reach] + left + right
            mids.append(jnp.maximum(total, 0.0).astype(bf16))
        return jnp.concatenate(mids, axis=1)

    def mixed_rows(at, low, mid):
        mixed = jnp.dot(mix_weight[:, :reach], mid, preferred_element_type=f32)
        for k in range(PART):
            for m in range(TAPS):
                row_at = at * GROUP + low + k + STEP * m
                here = mixed[m * channels : (m + 1) * channels, k * n_cols : (k + 1) * n_cols]
                here = here + base[row_at + STEP].astype(f32)
                result[pl.ds(pl.multiple_of(row_at * pitch, STEP), channels), :] = here

    def turn_rows(start, count):
        start = pl.multiple_of(start, TILE)
        for o in range(channels):
            cells = result[pl.ds(start * pitch + o, count, stride=pitch), :]
            staged[o, pl.ds(start, count), :] = cells.astype(bf16)

    def to_out(start, count, sem):
        rows = pl.ds(pl.multiple_of(start, TILE), count)
        return pltpu.make_async_copy(staged.at[:, rows], out.at[:, rows], sem)

    per_step = 2 * GROUP
    steps = n_rows // per_step - 1
    ahead = per_step + TILE
    outer = []
    put_rows(0, pair_rows(row_proj[:ahead, :], outer))
    put_sides(0, pair_cells(outer))

    def rounds(groups, start, count, turn):
        ends = conv_ends(groups)
        places = [(n, low) for n in range(len(groups)) for low in range(0, STEP, PART)]
        share = -(-count // (PART * len(places))) * PART
        hidden, outer, mid = [], [], None
        rows = row_proj[pl.ds(pl.multiple_of(start, STEP), count), :]
        for n, (group, low) in enumerate(places):
            if n == 0:
                parts = conv_parts(groups[group], low)
                turn()
            hidden += pair_rows(rows[n * share : (n + 1) * share], outer)
            if n:
                mixed_rows(groups[places[n - 1][0]], places[n - 1][1], mid)
            coming = None
            if n + 1 < len(places):
                coming = conv_parts(groups[places[n + 1][0]], places[n + 1][1])
            mid = shifted(parts, ends[group], low)
            parts = coming
        outer = pair_cells(outer)
        mixed_rows(groups[-1], places[-1][1], mid)
        put_rows(start, hidden)
        put_sides(start, outer)

    def step(at, _):
        before = jnp.maximum(at - 1, 0)
        rounds(
            (2 * at, 2 * at + 1),
            at * per_step + ahead,
            per_step,
            lambda: turn_rows(before * per_step, per_step),
        )

        @pl.when(at > 0)
        def _send():
            to_out(before * per_step, per_step, sems.at[before]).start()

        return _

    spare = pl.ds(n_rows + TILE, STEP)
    base[spare] = jnp.zeros_like(base[spare])
    sides[(n_rows + TILE) // STEP] = jnp.zeros_like(sides[0])
    lax.fori_loop(0, steps, step, 0)

    done = steps * per_step
    rounds(
        (2 * steps, 2 * steps + 1),
        done + ahead,
        TILE,
        lambda: turn_rows(done - per_step, per_step),
    )
    to_out(done - per_step, per_step, sems.at[steps - 1]).start()
    at = 2 * steps + 2
    (ends,) = conv_ends((at,))
    lows = range(0, STEP, PART)
    parts = [conv_parts(at, low) for low in lows]
    turn_rows(done, per_step)
    to_out(done, per_step, sems.at[steps]).start()
    for low, part in zip(lows, parts):
        mixed_rows(at, low, shifted(part, ends, low))
    done += per_step
    turn_rows(done, n_rows - done)
    last = to_out(done, n_rows - done, sems.at[steps + 1])
    last.start()
    for at in range(steps + 1):
        to_out(at * per_step, per_step, sems.at[at]).wait()
    last.wait()


def on_device(trunk, row_weight, column_weight, pair_map_weight, dilated_weight, mixing_weight):
    n_row, n_chip = lax.axis_size("row"), lax.axis_size("chip")
    shard, depth = trunk.shape
    n_rows, n_cols = shard * n_chip * 2, shard * n_row
    channels = pair_map_weight.shape[1]
    width = row_weight.shape[1]
    small = jnp.concatenate([dilated_weight.reshape(-1, channels), mixing_weight], axis=0)
    small = jnp.pad(small, ((0, 0), (0, width - channels)))
    weights = jnp.concatenate([row_weight, column_weight, pair_map_weight.T, small], axis=0)

    half = depth // 2
    to = lax.broadcasted_iota(jnp.int32, (n_row * n_chip * 2, shard, half), 0)
    copies = jnp.where(to % 2 == 0, trunk[None, :, :half], trunk[None, :, half:])
    mine = lax.all_to_all(copies, ("row", "chip", "core"), 0, 0).reshape(-1, half)
    other = lax.ppermute(mine, "core", [(0, 1), (1, 0)])
    span = -(-WINDOWS * channels // n_cols) * n_cols
    groups = -(-n_rows // GROUP)
    padded = groups * GROUP + TILE
    return pl.pallas_call(
        functools.partial(kernel, n_row, n_chip),
        out_shape=jax.ShapeDtypeStruct((channels, n_rows, n_cols), jnp.bfloat16),
        out_specs=pl.BlockSpec(memory_space=pl.ANY),
        scratch_shapes=[
            pltpu.VMEM((TAPS * TAPS * channels, span), jnp.bfloat16),
            pltpu.VMEM((TAPS * channels, span), jnp.bfloat16),
            pltpu.VMEM((n_rows + TILE, width), jnp.float32),
            pltpu.VMEM((n_cols + TILE, width), jnp.bfloat16),
            pltpu.VMEM((padded, channels, n_cols), jnp.bfloat16),
            pltpu.VMEM((padded // STEP, channels, n_cols), jnp.bfloat16),
            pltpu.VMEM((groups * GROUP * (channels + STEP), n_cols), jnp.float32),
            pltpu.VMEM((channels, n_rows, n_cols), jnp.bfloat16),
            pltpu.SemaphoreType.DMA((n_rows // (2 * GROUP) + 1,)),
        ],
        compiler_params=pltpu.CompilerParams(vmem_limit_bytes=52 * 2**20),
        name="pair_block",
    )(mine, other, weights)


def solution(mesh):
    n_row, n_col = mesh.devices.shape
    chips = Mesh(mesh.devices.reshape(n_row, n_col // 2, 2), ("row", "chip", "core"))
    return jax.shard_map(
        on_device,
        mesh=chips,
        in_specs=(P(("row", "chip", "core"), None), P(), P(), P(), P(), P()),
        out_specs=P(None, "row", ("chip", "core")),
        check_vma=False,
    )
```

```python
import functools

import jax
import jax.numpy as jnp
from jax import lax
from jax.experimental import pallas as pl
from jax.experimental.pallas import tpu as pltpu
from jax.sharding import Mesh
from jax.sharding import PartitionSpec as P

STEP = 8
TILE = 2 * STEP
TAPS = 3
PART = 4
WINDOWS = TAPS + 2
GROUP = TAPS * STEP
OUTSIDE = -1e30


def kernel(
    n_row,
    n_chip,
    mine,
    other,
    weights,
    out,
    conv_weight,
    mix_weight,
    row_proj,
    col_proj,
    base,
    sides,
    result,
    staged,
    sems,
):
    depth = 2 * mine.shape[1]
    row_weight = weights.at[pl.ds(0, depth)]
    col_weight = weights.at[pl.ds(depth, depth)]
    pair_weight = weights.at[pl.ds(2 * depth, out.shape[0])]
    f32, bf16 = jnp.float32, jnp.bfloat16
    row, chip, core = (lax.axis_index(name) for name in ("row", "chip", "core"))
    channels, n_rows, n_cols = out.shape

    span = conv_weight.shape[1]

    def block(at):
        cells = weights[pl.ds(2 * depth + (1 + at) * channels, channels), :span]
        return cells.astype(f32)

    taps = [[block(a * TAPS + b) for b in range(TAPS)] for a in range(TAPS)]
    mixing = block(TAPS * TAPS)
    for m in range(TAPS):
        for b in range(TAPS):
            moved = [pltpu.roll(taps[a][b], (m + a) * channels, 1) for a in range(TAPS)]
            rows = pl.ds((b * TAPS + m) * channels, channels)
            conv_weight[rows, :] = (moved[0] + moved[1] + moved[2]).astype(bf16)
        moved = pltpu.roll(mixing, m * channels, 1) if m else mixing
        mix_weight[pl.ds(m * channels, channels), :] = moved.astype(bf16)

    tiles = n_cols // TILE + 1
    zero = jnp.zeros((), bf16)

    def projected(start, size, weight):
        ends = (jnp.maximum(start - TILE, 0), jnp.minimum(start + size, mine.shape[0] - TILE))
        spans = [pl.ds(pl.multiple_of(start, TILE), size)]
        spans += [pl.ds(pl.multiple_of(end, TILE), TILE) for end in ends]
        halves = [jnp.concatenate([half[rows] for rows in spans], axis=0) for half in (mine, other)]
        cells = jnp.concatenate(
            [jnp.where(core == k, halves[0], halves[1]) for k in range(2)], axis=1
        )
        cells = jnp.dot(cells, weight[...], preferred_element_type=f32).astype(bf16).astype(f32)
        return cells[:size], cells[size + STEP : size + TILE], cells[size + TILE : size + TILE + STEP]

    width = row_proj.shape[1]

    cells, left, right = projected((chip * 2 + core) * n_cols, n_cols, col_weight)
    col_proj[:n_cols, :] = cells.astype(bf16)
    left = jnp.where((chip == 0) & (core == 0), OUTSIDE, left)
    right = jnp.where((chip == n_chip - 1) & (core == 1), OUTSIDE, right)
    col_proj[n_cols:, :] = jnp.concatenate([right, left], axis=0).astype(bf16)

    cells, left, right = projected(row * n_rows, n_rows, row_weight)
    row_proj[:STEP, :] = jnp.where(row == 0, OUTSIDE, left)
    row_proj[STEP : STEP + n_rows, :] = cells
    row_proj[STEP + n_rows : TILE + n_rows, :] = jnp.where(row == n_row - 1, OUTSIDE, right)

    lane = lax.broadcasted_iota(jnp.int32, (1, n_cols), 1)
    transposed = (((1,), (1,)), ((), ()))

    def pair_cells(acts):
        act = jnp.concatenate(acts, axis=0)
        hidden = lax.dot_general(pair_weight[...], act, transposed, preferred_element_type=f32)
        return hidden.astype(bf16)

    def pair_acts(rows, outer):
        inner = []
        for k in range(PART):
            spread = jnp.broadcast_to(rows[k : k + 1], (TILE, width)).astype(bf16)
            cells = col_proj[...].reshape(tiles, TILE, width) + spread[None]
            act = jnp.maximum(cells, zero)
            inner.append(act[:-1].reshape(n_cols, width))
            outer.append(act[-1])
        return inner

    def pair_rows(rows, outer):
        hidden, acts = [], None
        for low in range(0, rows.shape[0], PART):
            ahead_acts = pair_acts(rows[low : low + PART], outer)
            if acts is not None:
                hidden.append(pair_cells(acts))
            acts = ahead_acts
        if acts is not None:
            hidden.append(pair_cells(acts))
        return hidden

    def put_rows(start, hidden):
        for n, cells in enumerate(hidden):
            for k in range(PART):
                base[start + n * PART + k] = cells[:, k * n_cols : (k + 1) * n_cols]

    def put_sides(start, cells):
        for k in range(cells.shape[1] // n_cols):
            sides[start // STEP + k] = cells[:, k * n_cols : (k + 1) * n_cols]

    reach = TAPS * channels
    pitch = channels + STEP
    fill = [jnp.zeros((span - WINDOWS * channels, n_cols), bf16)]

    def conv_cells(blocks):
        cells = [jnp.concatenate(windows + fill, axis=0) for windows in blocks]
        cells = jnp.maximum(jnp.concatenate(cells, axis=1), zero)
        return jnp.dot(conv_weight[...], cells, preferred_element_type=f32)

    def conv_ends(groups):
        parts = conv_cells([[sides[at * TAPS + m] for m in range(WINDOWS)] for at in groups])
        ends = []
        for n in range(len(groups)):
            part = parts[:, n * n_cols : (n + 1) * n_cols]
            ends.append(jnp.where(lane % TILE >= STEP, part[:reach], part[2 * reach :]))
        return ends

    def conv_parts(at, low):
        places = [at * GROUP + p for p in range(low, low + PART)]
        return conv_cells([[base[p + STEP * m] for m in range(WINDOWS)] for p in places])

    def shifted(parts, ends, low):
        mids = []
        for k in range(PART):
            here = parts[:, k * n_cols : (k + 1) * n_cols]
            end = pltpu.roll(ends, (n_cols - STEP - (low + k) * TILE) % n_cols, 1)
            left = jnp.where(lane < STEP, end, pltpu.roll(here[:reach], STEP, 1))
            right = pltpu.roll(here[2 * reach :], n_cols - STEP, 1)
            right = jnp.where(lane >= n_cols - STEP, end, right)
            total = here[reach : 2 * reach] + left + right
            mids.append(jnp.maximum(total, 0.0).astype(bf16))
        return jnp.concatenate(mids, axis=1)

    def mixed_rows(at, low, mid):
        mixed = jnp.dot(mix_weight[:, :reach], mid, preferred_element_type=f32)
        for k in range(PART):
            for m in range(TAPS):
                row_at = at * GROUP + low + k + STEP * m
                here = mixed[m * channels : (m + 1) * channels, k * n_cols : (k + 1) * n_cols]
                here = here + base[row_at + STEP].astype(f32)
                result[pl.ds(pl.multiple_of(row_at * pitch, STEP), channels), :] = here

    def turn_rows(start, count):
        start = pl.multiple_of(start, TILE)
        for o in range(channels):
            cells = result[pl.ds(start * pitch + o, count, stride=pitch), :]
            staged[o, pl.ds(start, count), :] = cells.astype(bf16)

    def to_out(start, count, sem):
        rows = pl.ds(pl.multiple_of(start, TILE), count)
        return pltpu.make_async_copy(staged.at[:, rows], out.at[:, rows], sem)

    per_step = 2 * GROUP
    steps = n_rows // per_step - 1
    ahead = per_step + TILE
    outer = []
    put_rows(0, pair_rows(row_proj[:ahead, :], outer))
    put_sides(0, pair_cells(outer))

    def rounds(groups, start, count, turn):
        places = [(n, low) for n in range(len(groups)) for low in range(0, STEP, PART)]
        share = -(-count // (PART * len(places))) * PART
        hidden, outer, mid = [], [], None
        rows = row_proj[pl.ds(pl.multiple_of(start, STEP), count), :]
        for n, (group, low) in enumerate(places):
            parts = conv_parts(groups[group], low)
            if n == 0:
                ends = conv_ends(groups)
                turn()
            hidden += pair_rows(rows[n * share : (n + 1) * share], outer)
            if n:
                mixed_rows(groups[places[n - 1][0]], places[n - 1][1], mid)
            mid = shifted(parts, ends[group], low)
        outer = pair_cells(outer)
        mixed_rows(groups[-1], places[-1][1], mid)
        put_rows(start, hidden)
        put_sides(start, outer)

    def step(at, _):
        before = jnp.maximum(at - 1, 0)
        rounds(
            (2 * at, 2 * at + 1),
            at * per_step + ahead,
            per_step,
            lambda: turn_rows(before * per_step, per_step),
        )

        @pl.when(at > 0)
        def _send():
            to_out(before * per_step, per_step, sems.at[before]).start()

        return _

    spare = pl.ds(n_rows + TILE, STEP)
    base[spare] = jnp.zeros_like(base[spare])
    sides[(n_rows + TILE) // STEP] = jnp.zeros_like(sides[0])
    lax.fori_loop(0, steps, step, 0)

    done = steps * per_step
    rounds(
        (2 * steps, 2 * steps + 1),
        done + ahead,
        TILE,
        lambda: turn_rows(done - per_step, per_step),
    )
    to_out(done - per_step, per_step, sems.at[steps - 1]).start()
    at = 2 * steps + 2
    (ends,) = conv_ends((at,))
    lows = range(0, STEP, PART)
    parts = [conv_parts(at, low) for low in lows]
    turn_rows(done, per_step)
    to_out(done, per_step, sems.at[steps]).start()
    for low, part in zip(lows, parts):
        mixed_rows(at, low, shifted(part, ends, low))
    done += per_step
    turn_rows(done, n_rows - done)
    last = to_out(done, n_rows - done, sems.at[steps + 1])
    last.start()
    for at in range(steps + 1):
        to_out(at * per_step, per_step, sems.at[at]).wait()
    last.wait()


def on_device(trunk, row_weight, column_weight, pair_map_weight, dilated_weight, mixing_weight):
    n_row, n_chip = lax.axis_size("row"), lax.axis_size("chip")
    shard, depth = trunk.shape
    n_rows, n_cols = shard * n_chip * 2, shard * n_row
    channels = pair_map_weight.shape[1]
    width = row_weight.shape[1]
    small = jnp.concatenate([dilated_weight.reshape(-1, channels), mixing_weight], axis=0)
    small = jnp.pad(small, ((0, 0), (0, width - channels)))
    weights = jnp.concatenate([row_weight, column_weight, pair_map_weight.T, small], axis=0)

    half = depth // 2
    to = lax.broadcasted_iota(jnp.int32, (n_row * n_chip * 2, shard, half), 0)
    copies = jnp.where(to % 2 == 0, trunk[None, :, :half], trunk[None, :, half:])
    mine = lax.all_to_all(copies, ("row", "chip", "core"), 0, 0).reshape(-1, half)
    other = lax.ppermute(mine, "core", [(0, 1), (1, 0)])
    span = -(-WINDOWS * channels // n_cols) * n_cols
    groups = -(-n_rows // GROUP)
    padded = groups * GROUP + TILE
    return pl.pallas_call(
        functools.partial(kernel, n_row, n_chip),
        out_shape=jax.ShapeDtypeStruct((channels, n_rows, n_cols), jnp.bfloat16),
        out_specs=pl.BlockSpec(memory_space=pl.ANY),
        scratch_shapes=[
            pltpu.VMEM((TAPS * TAPS * channels, span), jnp.bfloat16),
            pltpu.VMEM((TAPS * channels, span), jnp.bfloat16),
            pltpu.VMEM((n_rows + TILE, width), jnp.float32),
            pltpu.VMEM((n_cols + TILE, width), jnp.bfloat16),
            pltpu.VMEM((padded, channels, n_cols), jnp.bfloat16),
            pltpu.VMEM((padded // STEP, channels, n_cols), jnp.bfloat16),
            pltpu.VMEM((groups * GROUP * (channels + STEP), n_cols), jnp.float32),
            pltpu.VMEM((channels, n_rows, n_cols), jnp.bfloat16),
            pltpu.SemaphoreType.DMA((n_rows // (2 * GROUP) + 1,)),
        ],
        compiler_params=pltpu.CompilerParams(vmem_limit_bytes=52 * 2**20),
        name="pair_block",
    )(mine, other, weights)


def solution(mesh):
    n_row, n_col = mesh.devices.shape
    chips = Mesh(mesh.devices.reshape(n_row, n_col // 2, 2), ("row", "chip", "core"))
    return jax.shard_map(
        on_device,
        mesh=chips,
        in_specs=(P(("row", "chip", "core"), None), P(), P(), P(), P(), P()),
        out_specs=P(None, "row", ("chip", "core")),
        check_vma=False,
    )
```
